256 devices in a mesh: ctx: 32 (over y_hi, z, core), grp: 2 (over y_lo), tp: 4 (over x).
Axes of the slice: x: 4, y: 4 (y_hi: 2, y_lo: 2; y = y_hi * 2 + y_lo), z: 8, core: 2. Of those that a mesh axis runs over, the one named last changes fastest.
Arguments:
- q_stretch: bfloat16 [2048, 8192], P('ctx', ('grp', 'tp')), may hold values from -200 to 200
- stretch_key_value: bfloat16 [2048, 2, 1024], P('ctx', None, ('grp', 'tp')), may hold values from -6 to 6
- context_key_value: bfloat16 [40960, 2, 1024], P('ctx', None, ('grp', 'tp')), may hold values from -6 to 6
- dec_q: bfloat16 [128, 2, 8192], P('ctx', None, ('grp', 'tp')), may hold values from -200 to 200
- dec_new: bfloat16 [128, 2, 2, 1024], P('ctx', None, None, ('grp', 'tp')), may hold values from -6 to 6
- pool_key_value: bfloat16 [1024, 128, 2, 1024], P('ctx', None, None, ('grp', 'tp')), may hold values from -6 to 6
- block_table: int32 [128, 8], replicated, may hold values from 0 to 1023, as said below
- cache_len: int32 [128], P('ctx'), may hold values from 1 to 1024, as said below
- w_out: bfloat16 [8192, 8192], P(('grp', 'tp'), 'ctx'), may hold values from -0.0625 to 0.0625
Outputs:
- pre_out: bfloat16 [2048, 8192], P('ctx', ('grp', 'tp'))
- dec_out: bfloat16 [128, 2, 8192], P(('grp', 'tp'), None, 'ctx')
The draws below stay inside these ranges and needn't reach their ends.
Inputs may be any that keep to these rules, and one draw needn't show every extreme that they name: `block_table`: every pool block is named exactly once. The pool blocks of one index of ctx are an aligned run of 32; the decode rows of one index of ctx (an aligned run of 4 rows) name exactly 1 block of each such run. `cache_len`: some row has the full 1024 positions, and some other row has one.
All inputs are finite; a program needn't handle non-finite values.
Results may differ from the reference program's by a relative error of at most 0.035.
Values may be sent and summed in bfloat16 or wider, within the bound.
No kernel may reach another device: no remote copies, remote signals or barrier semaphores. Data moves between devices by JAX's collectives and lax.ppermute only.
A program may use at most 128 MiB of HBM per device.

```python
import math
import jax
import jax.numpy as jnp
from jax import lax

D = 8192
QUERY_HEADS = 64
VALUE_HEADS = 8
HEAD_SIZE = 128
BLOCK_POSITIONS = 128
ROWS_DEV = 4
NBLK = 8
STRETCH_TOKENS = 2048
CONTEXT_LENGTH = 40960
DECODE_ROWS = 128
CACHE_POSITIONS = 1024
POOL_BLOCKS = 1024
CAP = 1


def prefix_draw(key):
    key_primary, key_secondary = jax.random.split(key, 2)
    sampled_values = jax.random.normal(key_primary, (CONTEXT_LENGTH, 2, VALUE_HEADS * HEAD_SIZE), jnp.float32)
    anchor = jax.random.randint(key_secondary, (8,), 0, CONTEXT_LENGTH - 1)
    sampled_values = sampled_values.at[anchor + 1, 0].set(sampled_values[anchor + 1, 0])
    return jnp.clip(sampled_values, -6.0, 6.0)


def fresh_draw(key):
    key_primary = jax.random.fold_in(key, 0)
    sampled_values = jax.random.normal(key_primary, (DECODE_ROWS, 2, 2, VALUE_HEADS * HEAD_SIZE), jnp.float32)
    sampled_values = sampled_values.at[:, 1, 0].set(sampled_values[:, 1, 0])
    return jnp.clip(sampled_values, -6.0, 6.0)


def draw_context_key_value(key, part):
    sampled_values = prefix_draw(key)
    return sampled_values.astype(jnp.bfloat16)


def draw_q_stretch(key, part):
    key = jax.random.fold_in(key, 7)
    key_primary = jax.random.fold_in(key, 0)
    queries = 3.5 * jax.random.normal(key_primary, (STRETCH_TOKENS, QUERY_HEADS * HEAD_SIZE), jnp.float32)
    return jnp.clip(queries, -200.0, 200.0).astype(jnp.bfloat16)


def draw_dec_new(key, part):
    sampled_values = fresh_draw(key)
    return sampled_values.astype(jnp.bfloat16)


def draw_dec_q(key, part):
    key = jax.random.fold_in(key, 11)
    key_primary = jax.random.fold_in(key, 0)
    queries = 3.5 * jax.random.normal(key_primary, (DECODE_ROWS, 2, QUERY_HEADS * HEAD_SIZE), jnp.float32)
    return jnp.clip(queries, -200.0, 200.0).astype(jnp.bfloat16)


def draw_block_table(key, part):
    key = jax.random.fold_in(key, 5)
    key_primary, key_secondary = jax.random.split(key, 2)
    cycle_count = DECODE_ROWS // ROWS_DEV
    entries = ROWS_DEV * NBLK
    dest_order = jax.vmap(lambda single: jax.random.permutation(single, entries))(jax.random.split(key_primary, cycle_count))
    source = dest_order // CAP
    within = dest_order % CAP
    slot_order = jax.vmap(lambda single: jax.random.permutation(single, entries))(jax.random.split(key_secondary, cycle_count))
    owner_index = jnp.arange(cycle_count, dtype=jnp.int32)[:, None]
    position = slot_order[source, owner_index * CAP + within]
    table = source * entries + position
    return table.reshape(DECODE_ROWS, NBLK).astype(jnp.int32)


def draw_cache_len(key, part):
    key = jax.random.fold_in(key, 9)
    key_primary, key_secondary, key_tertiary, key_fourth = jax.random.split(key, 4)
    cycle_count = DECODE_ROWS // ROWS_DEV
    ceiling = jax.random.randint(key_primary, (cycle_count,), CACHE_POSITIONS // 4, CACHE_POSITIONS + 1)
    ceiling_rows = jnp.repeat(ceiling, ROWS_DEV)
    shortfall = jax.random.randint(key_secondary, (DECODE_ROWS,), 0, ceiling_rows // 2 + 1)
    lengths = ceiling_rows - shortfall
    longest = jax.random.randint(key_tertiary, (), 0, DECODE_ROWS)
    shortest = (longest + 1 + jax.random.randint(key_fourth, (), 0, DECODE_ROWS - 1)) % DECODE_ROWS
    lengths = lengths.at[longest].set(CACHE_POSITIONS)
    lengths = lengths.at[shortest].set(1)
    return jnp.maximum(lengths, 1).astype(jnp.int32)


def block_scale(key, extent, cuts, smallest, top_value):
    gain, own = 1.0, jax.random.fold_in(key, 6)
    for dim, shards_of in cuts:
        steps = jnp.exp(jax.random.uniform(jax.random.fold_in(own, dim), (shards_of,), jnp.float32, smallest / len(cuts), top_value / len(cuts)))
        gain = gain * jnp.repeat(steps, extent[dim] // shards_of).reshape([-1 if axis == dim else 1 for axis in range(len(extent))])
    return gain


def bell_draw(key, extent, deviation, reach, pieces=(), held_as=jnp.bfloat16):
    result = jax.random.normal(key, extent, jnp.float32) * deviation
    if len(pieces) > 0:
        result = block_scale(key, extent, pieces, -0.22, 0.18) * result
    return jnp.clip(result, min=-reach, max=reach).astype(held_as)


def setup_inputs(seed: int = 0) -> dict:
    arg_keys = jax.random.split(jax.random.key(seed), 10)
    return {
        "q_stretch": draw_q_stretch(jax.random.fold_in(arg_keys[9], 71), 0),
        "stretch_key_value": bell_draw(arg_keys[1], (STRETCH_TOKENS, 2, VALUE_HEADS * HEAD_SIZE), 1.0, 6.0, ((0, 32), (2, 8))),
        "context_key_value": draw_context_key_value(jax.random.fold_in(arg_keys[9], 71), 0),
        "dec_q": draw_dec_q(jax.random.fold_in(arg_keys[9], 71), 0),
        "dec_new": draw_dec_new(jax.random.fold_in(arg_keys[9], 71), 0),
        "pool_key_value": bell_draw(arg_keys[5], (POOL_BLOCKS, BLOCK_POSITIONS, 2, VALUE_HEADS * HEAD_SIZE), 1.0, 6.0, ((0, 32), (3, 8))),
        "block_table": draw_block_table(jax.random.fold_in(arg_keys[9], 71), 0),
        "cache_len": draw_cache_len(jax.random.fold_in(arg_keys[9], 71), 0),
        "w_out": bell_draw(arg_keys[8], (QUERY_HEADS * HEAD_SIZE, D), (QUERY_HEADS * HEAD_SIZE) ** -0.5, 0.0625, ((0, 8), (1, 32))),
    }


def attend_head(query_row_list, key_row_list, value_row_list, allowed):
    scores = jnp.dot(query_row_list, key_row_list.T, preferred_element_type=jnp.float32) / math.sqrt(HEAD_SIZE)
    scores = jnp.where(allowed, scores, -jnp.inf)
    top_score = lax.optimization_barrier(jnp.max(scores, axis=-1, keepdims=True))
    exponent = jnp.exp(scores - top_score)
    denominator = lax.optimization_barrier(jnp.sum(exponent, axis=-1, keepdims=True))
    summed = jnp.dot(exponent.astype(jnp.bfloat16), value_row_list, preferred_element_type=jnp.float32)
    return (summed / denominator).astype(jnp.bfloat16)

def prefill(q_stretch, stretch_key_value, context_key_value):
    head_groups = QUERY_HEADS // VALUE_HEADS
    key_combined = jnp.concatenate([context_key_value[:, 0], stretch_key_value[:, 0]], axis=0).reshape(CONTEXT_LENGTH + STRETCH_TOKENS, VALUE_HEADS, HEAD_SIZE)
    value_combined = jnp.concatenate([context_key_value[:, 1], stretch_key_value[:, 1]], axis=0).reshape(CONTEXT_LENGTH + STRETCH_TOKENS, VALUE_HEADS, HEAD_SIZE)
    queries = q_stretch.reshape(STRETCH_TOKENS, QUERY_HEADS, HEAD_SIZE).transpose(1, 0, 2)
    positions = jnp.arange(CONTEXT_LENGTH + STRETCH_TOKENS, dtype=jnp.int32)
    row_index = jnp.arange(STRETCH_TOKENS, dtype=jnp.int32)
    allowed = (positions[None, :] < CONTEXT_LENGTH) | (positions[None, :] - CONTEXT_LENGTH <= row_index[:, None])

    def one_head(head_index):
        query_row_list = lax.dynamic_index_in_dim(queries, head_index, 0, keepdims=False)
        kv_head = head_index // head_groups
        key_row_list = lax.dynamic_index_in_dim(key_combined, kv_head, 1, keepdims=False)
        value_row_list = lax.dynamic_index_in_dim(value_combined, kv_head, 1, keepdims=False)
        return attend_head(query_row_list, key_row_list, value_row_list, allowed)
    results = lax.map(one_head, jnp.arange(QUERY_HEADS, dtype=jnp.int32))
    return results.transpose(1, 0, 2).reshape(STRETCH_TOKENS, QUERY_HEADS * HEAD_SIZE)

def decode(dec_q, dec_new, pool_key_value, block_table, cache_len):
    head_groups = QUERY_HEADS // VALUE_HEADS

    def decode_row(inputs):
        query_row_list, newest_rows, table_row, length = inputs
        block_list = jnp.take(pool_key_value, table_row, axis=0)
        cache_row_list = block_list.reshape(CACHE_POSITIONS, 2, VALUE_HEADS * HEAD_SIZE)
        key_row_list = jnp.concatenate([cache_row_list[:, 0], newest_rows[:, 0]], axis=0).reshape(CACHE_POSITIONS + 2, VALUE_HEADS, HEAD_SIZE)
        value_row_list = jnp.concatenate([cache_row_list[:, 1], newest_rows[:, 1]], axis=0).reshape(CACHE_POSITIONS + 2, VALUE_HEADS, HEAD_SIZE)
        query_head_list = query_row_list.reshape(2, VALUE_HEADS, head_groups, HEAD_SIZE).astype(jnp.float32)
        scores = jnp.einsum('tngd,knd->tngk', query_head_list, key_row_list.astype(jnp.float32)) / math.sqrt(HEAD_SIZE)
        positions = jnp.arange(CACHE_POSITIONS + 2, dtype=jnp.int32)
        step_index = jnp.arange(2, dtype=jnp.int32)
        allowed = jnp.where(positions[None, :] < CACHE_POSITIONS, positions[None, :] < length, positions[None, :] - CACHE_POSITIONS <= step_index[:, None])
        scores = jnp.where(allowed[:, None, None, :], scores, -jnp.inf)
        top_score = lax.optimization_barrier(jnp.max(scores, axis=-1, keepdims=True))
        exponent = jnp.exp(scores - top_score)
        denominator = lax.optimization_barrier(jnp.sum(exponent, axis=-1, keepdims=True))
        rounded = lax.optimization_barrier(exponent.astype(jnp.bfloat16))
        summed = jnp.einsum('tngk,knd->tngd', rounded.astype(jnp.float32), value_row_list.astype(jnp.float32))
        return (summed / denominator).astype(jnp.bfloat16).reshape(2, QUERY_HEADS * HEAD_SIZE)
    return lax.map(decode_row, (dec_q, dec_new, block_table, cache_len))

def reference(q_stretch, stretch_key_value, context_key_value, dec_q, dec_new, pool_key_value, block_table, cache_len, w_out):
    pre_out = prefill(q_stretch, stretch_key_value, context_key_value)
    dec_attn = decode(dec_q, dec_new, pool_key_value, block_table, cache_len)
    projected = jnp.dot(dec_attn.reshape(DECODE_ROWS * 2, QUERY_HEADS * HEAD_SIZE), w_out, preferred_element_type=jnp.float32)
    dec_out = projected.astype(jnp.bfloat16).reshape(DECODE_ROWS, 2, D)
    return (pre_out, dec_out)
```

```python
import functools
import math

import jax
import jax.numpy as jnp
from jax import lax
from jax.experimental import pallas as pl
from jax.experimental.pallas import tpu as pltpu
from jax.sharding import PartitionSpec as P

HEAD_SIZE = 128
CORES = 2
Z_CHIPS = 8
CTX = ("y", "z", "core")
SCALE = math.log2(math.e) / math.sqrt(HEAD_SIZE)
LOWEST = -1e30
F32 = jnp.float32
BF16 = jnp.bfloat16
TILE = 256
VMEM = pl.BlockSpec(memory_space=pltpu.VMEM)
SMEM = pl.BlockSpec(memory_space=pltpu.SMEM)


def params(mib):
    return pltpu.CompilerParams(vmem_limit_bytes=mib * 1024 * 1024)


def dot_nt(a, b):
    return lax.dot_general(a, b, (((1,), (1,)), ((), ())), preferred_element_type=F32)


def dot_nn(a, b):
    return lax.dot_general(a, b, (((1,), (0,)), ((), ())), preferred_element_type=F32)


def split_body(context_ref, stretch_ref, out_ref):
    def split(rows, at):
        count = rows.shape[0]
        half = count // 2
        i = lax.broadcasted_iota(jnp.int32, (count, count), 0)
        j = lax.broadcasted_iota(jnp.int32, (count, count), 1)
        source = jnp.where(i < half, 2 * i, 2 * (i - half) + 1)
        pick = jnp.where(j == source, 1.0, 0.0).astype(BF16)
        parted = dot_nn(pick, rows).astype(BF16)
        out_ref[0, at : at + half, :] = parted[:half]
        out_ref[1, at : at + half, :] = parted[half:]

    total = context_ref.shape[0]
    for start in range(0, total, 256):
        split(context_ref[start : start + 256, :], start // 2)
    split(stretch_ref[...], total // 2)


def split_keys_values(context, stretch):
    rows = (context.shape[0] + stretch.shape[0]) // 2
    return pl.pallas_call(
        split_body,
        out_shape=jax.ShapeDtypeStruct((2, rows, HEAD_SIZE), BF16),
        in_specs=[VMEM, VMEM],
        out_specs=VMEM,
        compiler_params=params(16),
        name="split_keys_values",
    )(context, stretch)


def attend_body(first_head, deltas_ref, q_ref, kv_ref, out_ref, s_ref, p_ref, v_ref, top_ref):
    tiles, stretch = q_ref.shape[:2]
    sets = kv_ref.shape[0]
    keys = kv_ref.shape[2] - stretch
    heads_tile = TILE // stretch
    chunk_size = 256

    v_ref[:, HEAD_SIZE:] = jnp.ones((v_ref.shape[0], HEAD_SIZE), BF16)
    for n in range(sets):
        v_ref[n * keys : (n + 1) * keys, :HEAD_SIZE] = kv_ref[n, 1, :keys, :]
        v_ref[sets * keys + n * stretch : sets * keys + (n + 1) * stretch, :HEAD_SIZE] = kv_ref[n, 1, keys:, :]

    chunks = []
    for n in range(sets):
        for start in range(0, keys, chunk_size):
            chunks.append((n, start, n * keys + start, chunk_size))
    chunks.append((None, 0, sets * keys, sets * stretch))

    def queries(t):
        heads = range(first_head, first_head + heads_tile)
        return jnp.concatenate([q_ref[t, :, h * HEAD_SIZE : (h + 1) * HEAD_SIZE] for h in heads], axis=0)

    def score(t, slot, q, top, chunk):
        n, start, at, size = chunk
        if n is None:
            k = jnp.concatenate([kv_ref[m, 0, keys:, :] for m in range(sets)], axis=0)
        else:
            k = kv_ref[n, 0, start : start + size, :]
        s = dot_nt(q, k)
        if n is None:
            row = lax.rem(lax.broadcasted_iota(jnp.int32, (TILE, size), 0), stretch)
            col = lax.broadcasted_iota(jnp.int32, (TILE, size), 1)
            bound = deltas_ref[t * sets + sets - 1] + (sets - 1) * stretch - col
            for m in reversed(range(sets - 1)):
                bound = jnp.where(col < (m + 1) * stretch, deltas_ref[t * sets + m] + m * stretch - col, bound)
            s = jnp.where(row + bound >= 0, s, LOWEST)
        s_ref[slot, :, at : at + size] = s
        for c in range(0, size, HEAD_SIZE):
            part = s[:, c : c + HEAD_SIZE]
            top = part if top is None else jnp.maximum(top, part)
        return top

    def settle(slot, top):
        top_ref[slot] = jnp.broadcast_to(jnp.max(top, axis=1, keepdims=True), (TILE, HEAD_SIZE)) * SCALE

    def weigh(slot, top, chunk):
        at, size = chunk[2], chunk[3]
        for c in range(at, at + size, HEAD_SIZE):
            p_ref[slot, :, c : c + HEAD_SIZE] = jnp.exp2(s_ref[slot, :, c : c + HEAD_SIZE] * SCALE - top).astype(BF16)

    def finish(t, slot, top):
        total = dot_nn(p_ref[slot], v_ref[...])
        weight = total[:, HEAD_SIZE:]
        out_ref[t, :TILE, :] = (total[:, :HEAD_SIZE] / weight).astype(BF16)
        level = top + jnp.log2(weight)
        i = lax.broadcasted_iota(jnp.int32, (HEAD_SIZE, HEAD_SIZE), 0)
        j = lax.broadcasted_iota(jnp.int32, (HEAD_SIZE, HEAD_SIZE), 1)
        rows = []
        for g in range(TILE // HEAD_SIZE):
            part = jnp.where(i == j, level[g * HEAD_SIZE : (g + 1) * HEAD_SIZE], 0.0)
            rows.append(jnp.sum(part, axis=0, keepdims=True))
        k = lax.broadcasted_iota(jnp.int32, (8, HEAD_SIZE), 0)
        level = jnp.where(k == 0, rows[0], jnp.where(k == 1, rows[1], 0.0))
        high = level.astype(BF16).astype(F32)
        rest = level - high
        middle = rest.astype(BF16).astype(F32)
        pieces = [high, middle, rest - middle, jnp.zeros_like(level)]
        out_ref[t, TILE:, :] = jnp.concatenate(pieces, axis=0).astype(BF16)

    def step(t, slot, following):
        top = top_ref[slot]
        coming = None
        if following is not None:
            q = queries(following)
        for chunk in chunks:
            weigh(slot, top, chunk)
            if following is not None:
                coming = score(following, 1 - slot, q, coming, chunk)
        if following is not None:
            settle(1 - slot, coming)
        finish(t, slot, top)

    top = None
    q = queries(0)
    for chunk in chunks:
        top = score(0, 0, q, top, chunk)
    settle(0, top)

    def pair(i, carry):
        step(2 * i, 0, 2 * i + 1)
        step(2 * i + 1, 1, 2 * i + 2)
        return carry

    lax.fori_loop(0, tiles // 2 - 1, pair, 0)
    step(tiles - 2, 0, tiles - 1)
    step(tiles - 1, 1, None)


def attend(first_head, deltas, queries, kv):
    tiles, stretch, _ = queries.shape
    keys = kv.shape[0] * kv.shape[2]
    return pl.pallas_call(
        functools.partial(attend_body, first_head),
        out_shape=jax.ShapeDtypeStruct((tiles, TILE + 32, HEAD_SIZE), BF16),
        in_specs=[SMEM, VMEM, VMEM],
        out_specs=VMEM,
        scratch_shapes=[
            pltpu.VMEM((2, TILE, keys), F32),
            pltpu.VMEM((2, TILE, keys), BF16),
            pltpu.VMEM((keys, 2 * HEAD_SIZE), BF16),
            pltpu.VMEM((2, TILE, HEAD_SIZE), F32),
        ],
        compiler_params=params(40),
        cost_estimate=pl.CostEstimate(
            flops=8 * tiles * TILE * keys * HEAD_SIZE,
            bytes_accessed=4 * keys * HEAD_SIZE,
            transcendentals=tiles * TILE * keys,
        ),
        name="attend",
    )(deltas, queries, kv)


def merge_body(*refs):
    out_ref = refs[-1]
    stretch = out_ref.shape[0]
    i = lax.broadcasted_iota(jnp.int32, (HEAD_SIZE, HEAD_SIZE), 0)
    j = lax.broadcasted_iota(jnp.int32, (HEAD_SIZE, HEAD_SIZE), 1)
    head = 0
    for ref in refs[:-1]:
        count = ref.shape[0]
        levels = []
        for n in range(count):
            stat = ref[n, TILE:, :].astype(F32)
            levels.append(stat[0:8] + stat[8:16] + stat[16:24])
        top = functools.reduce(jnp.maximum, levels)
        weights = [jnp.exp2(level - top) for level in levels]
        total = functools.reduce(jnp.add, weights)
        weights = [weight / total for weight in weights]
        for g in range(TILE // HEAD_SIZE):
            mixed = None
            for n in range(count):
                column = jnp.sum(jnp.where(i == j, weights[n][g : g + 1, :], 0.0), axis=1, keepdims=True)
                term = column * ref[n, g * HEAD_SIZE : (g + 1) * HEAD_SIZE, :].astype(F32)
                mixed = term if mixed is None else mixed + term
            mixed = mixed.astype(BF16)
            for h in range(HEAD_SIZE // stretch):
                out_ref[:, head * HEAD_SIZE : (head + 1) * HEAD_SIZE] = mixed[h * stretch : (h + 1) * stretch]
                head += 1


def merge(parts, stretch):
    width = len(parts) * TILE // stretch * HEAD_SIZE
    return pl.pallas_call(
        merge_body,
        out_shape=jax.ShapeDtypeStruct((stretch, width), BF16),
        in_specs=[VMEM] * len(parts),
        out_specs=VMEM,
        compiler_params=params(16),
        name="merge_parts",
    )(*parts)


def look_body(place_ref, ask_ref, pool_ref, out_ref, s_ref, p_ref):
    owners = ask_ref.shape[0]
    half = ask_ref.shape[1] // 2
    span = pool_ref.shape[1]
    for d in range(owners):
        s_ref[d * half : (d + 1) * half, :] = dot_nt(ask_ref[d, :half, :], pool_ref[place_ref[d]])
    col = lax.broadcasted_iota(jnp.int32, (half, span), 1)
    lane = lax.broadcasted_iota(jnp.int32, (half, HEAD_SIZE), 1)
    even = (col & 1) == 0
    for d in range(owners):
        limit = ask_ref[d, half:, :].astype(F32) * 2.0
        limit = jnp.concatenate([limit] * (span // HEAD_SIZE), axis=1)
        allowed = even & (col.astype(F32) < limit)
        s = jnp.where(allowed, s_ref[d * half : (d + 1) * half, :], LOWEST)
        top = jnp.max(s, axis=1, keepdims=True)
        p = jnp.where(allowed, jnp.exp2((s - top) * SCALE), 0.0)
        total = jnp.sum(p, axis=1, keepdims=True)
        p_ref[d * half : (d + 1) * half, :] = pltpu.roll(p, 1, 1).astype(BF16)
        seen = total > 0.0
        level = jnp.where(seen, top * SCALE + jnp.log2(jnp.where(seen, total, 1.0)), LOWEST)
        level = jnp.broadcast_to(level, (half, HEAD_SIZE))
        high = level.astype(BF16).astype(F32)
        rest = level - high
        middle = rest.astype(BF16).astype(F32)
        low = rest - middle
        stat = jnp.where(lane == 0, high, jnp.where(lane == 1, middle, jnp.where(lane == 2, low, 0.0)))
        out_ref[d, half:, :] = stat.astype(BF16)
        s_ref[d * half : (d + 1) * half, :HEAD_SIZE] = jnp.broadcast_to(
            jnp.where(seen, 1.0 / jnp.where(seen, total, 1.0), 0.0), (half, HEAD_SIZE)
        )
    for d in range(owners):
        o = dot_nn(p_ref[d * half : (d + 1) * half, :], pool_ref[place_ref[d]])
        out_ref[d, :half, :] = (o * s_ref[d * half : (d + 1) * half, :HEAD_SIZE]).astype(BF16)


def look(place, ask, pool):
    owners, rows, width = ask.shape
    span = pool.shape[1]
    return pl.pallas_call(
        look_body,
        out_shape=jax.ShapeDtypeStruct(ask.shape, BF16),
        in_specs=[SMEM, VMEM, VMEM],
        out_specs=VMEM,
        scratch_shapes=[
            pltpu.VMEM((owners * rows // 2, span), F32),
            pltpu.VMEM((owners * rows // 2, span), BF16),
        ],
        compiler_params=params(24),
        cost_estimate=pl.CostEstimate(
            flops=16 * owners * rows * span * width, bytes_accessed=2 * owners * span * width, transcendentals=0
        ),
        name="look_in_blocks",
    )(place, ask, pool)


def gather_body(row_ref, answer_ref, q_ref, new_ref, out_ref, level_ref, top_ref, sum_ref, acc_ref, flat_ref):
    holders = answer_ref.shape[0]
    rows, lists = q_ref.shape[0], q_ref.shape[1]
    heads = lists // 2
    lane = lax.broadcasted_iota(jnp.int32, (lists, HEAD_SIZE), 1)
    later = lax.broadcasted_iota(jnp.int32, (lists, HEAD_SIZE), 0) >= heads
    own = []
    for r in range(rows):
        q = q_ref[r].astype(F32)
        new = new_ref[r].astype(F32)
        scores = []
        for t in range(2):
            s = jnp.sum(q * new[2 * t : 2 * t + 1, :], axis=1, keepdims=True) * SCALE
            scores.append(jnp.broadcast_to(s, (lists, HEAD_SIZE)))
        scores[1] = jnp.where(later, scores[1], LOWEST)
        top_ref[r] = jnp.maximum(scores[0], scores[1])
        own.append((scores, new))
    for d in range(holders):
        stat = answer_ref[d, lists:, :].astype(F32)
        level = jnp.sum(jnp.where(lane < 3, stat, 0.0), axis=1, keepdims=True)
        level_ref[d] = jnp.broadcast_to(level, (lists, HEAD_SIZE))
    for d in range(holders):
        r = row_ref[d]
        top_ref[r] = jnp.maximum(top_ref[r], level_ref[d])
    for r in range(rows):
        scores, new = own[r]
        first = jnp.exp2(scores[0] - top_ref[r])
        second = jnp.exp2(scores[1] - top_ref[r])
        sum_ref[r] = first + second
        acc_ref[r] = first * new[1:2, :] + second * new[3:4, :]
    for d in range(holders):
        r = row_ref[d]
        weight = jnp.exp2(level_ref[d] - top_ref[r])
        sum_ref[r] = sum_ref[r] + weight
        acc_ref[r] = acc_ref[r] + weight * answer_ref[d, :lists, :].astype(F32)
    for r in range(rows):
        o = acc_ref[r] / sum_ref[r]
        for t in range(2):
            for h in range(heads):
                flat_ref[2 * r + t : 2 * r + t + 1, h * HEAD_SIZE : (h + 1) * HEAD_SIZE] = o[
                    t * heads + h : t * heads + h + 1, :
                ]
    out_ref[...] = flat_ref[...].astype(BF16)


def gather_answers(row_of, answer, q, new):
    rows, lists, width = q.shape
    holders = answer.shape[0]
    heads = lists // 2
    state = pltpu.VMEM((rows, lists, width), F32)
    return pl.pallas_call(
        gather_body,
        out_shape=jax.ShapeDtypeStruct((2 * rows, heads * width), BF16),
        in_specs=[SMEM, VMEM, VMEM, VMEM],
        out_specs=VMEM,
        scratch_shapes=[
            pltpu.VMEM((holders, lists, width), F32),
            state,
            state,
            state,
            pltpu.VMEM((2 * rows, heads * width), F32),
        ],
        compiler_params=params(16),
        name="gather_answers",
    )(row_of, answer, q, new)


def shards(
    q_stretch,
    stretch_key_value,
    context_key_value,
    dec_q,
    dec_new,
    pool_key_value,
    block_table,
    cache_len,
    w_out,
):
    me = lax.axis_index(CTX)
    cycle = lax.axis_size(CTX)
    stretch = q_stretch.shape[0]

    q_all = lax.all_gather(q_stretch, "z", axis=0)
    kv = split_keys_values(
        context_key_value.reshape(-1, HEAD_SIZE), stretch_key_value.reshape(-1, HEAD_SIZE)
    )
    kv_all = lax.all_gather(kv, ("y", "core"), axis=0)

    rows_dev, nblk = dec_q.shape[0], block_table.shape[1]
    entries = rows_dev * nblk
    pool_dev, block_size = pool_key_value.shape[:2]
    heads = dec_q.shape[2] // HEAD_SIZE
    table = block_table.reshape(cycle, entries)
    source, slot = table // pool_dev, table % pool_dev
    place = jnp.sum(jnp.where(source == me, slot, 0), axis=1)
    mine = lax.dynamic_index_in_dim(source, me, 0, keepdims=False)
    entry_ids = jnp.arange(entries, dtype=jnp.int32)
    holder_ids = jnp.arange(cycle, dtype=jnp.int32)
    entry_of = jnp.sum(jnp.where(mine[None, :] == holder_ids[:, None], entry_ids[None, :], 0), axis=1)
    row_of = entry_of // nblk
    block_of = entry_of % nblk
    own_rows = jnp.arange(rows_dev, dtype=jnp.int32)
    length_of = jnp.sum(jnp.where(row_of[:, None] == own_rows[None, :], cache_len[None, :], 0), axis=1)
    count_of = jnp.clip(length_of - block_of * block_size, 0, block_size).astype(BF16)
    lists = 2 * heads
    q_rows = dec_q.reshape(rows_dev, lists, HEAD_SIZE)
    asked = q_rows[0][None]
    for r in range(1, rows_dev):
        asked = jnp.where((row_of == r)[:, None, None], q_rows[r][None], asked)
    asked = jnp.broadcast_to(asked, (cycle, lists, HEAD_SIZE))
    counts = jnp.broadcast_to(count_of[:, None, None], (cycle, lists, HEAD_SIZE))
    ask = jnp.concatenate([asked, counts], axis=1)
    ask = lax.all_to_all(ask, CTX, split_axis=0, concat_axis=0, tiled=True)

    look_out = look(place, ask, pool_key_value.reshape(pool_dev, 2 * block_size, HEAD_SIZE))
    answer = lax.all_to_all(look_out, CTX, split_axis=0, concat_axis=0, tiled=True)
    attn = gather_answers(row_of, answer, q_rows, dec_new.reshape(rows_dev, 4, HEAD_SIZE))
    everyone = lax.all_gather(attn, CTX, axis=0, tiled=True)

    y, z, core = (lax.axis_index(name) for name in CTX)
    asker = (y * Z_CHIPS + jnp.arange(Z_CHIPS, dtype=jnp.int32)) * CORES + core
    shard = jnp.arange(2 * CORES, dtype=jnp.int32)
    shard = ((shard // CORES) * Z_CHIPS + z) * CORES + shard % CORES
    deltas = ((asker[:, None] - shard[None, :]) * stretch).reshape(-1)
    parts = []
    heads_tile = TILE // stretch
    deltas, _ = lax.optimization_barrier((deltas, attn))
    for first_head in range(0, heads, heads_tile):
        part = attend(first_head, deltas, q_all, kv_all)
        deltas, part = lax.optimization_barrier((deltas, part))
        parts.append(lax.all_to_all(part, "z", split_axis=0, concat_axis=0, tiled=True))

    partial_out = jnp.dot(
        everyone, w_out, preferred_element_type=F32
    ).astype(BF16)
    shares = lax.axis_size(("grp", "tp"))
    pieces = lax.all_to_all(
        partial_out.reshape(shares, -1, partial_out.shape[1]), ("grp", "tp"), split_axis=0, concat_axis=0, tiled=True
    )
    dec_out = jnp.sum(pieces.astype(F32), axis=0).astype(BF16)
    pre_out = merge(parts, stretch)
    return (pre_out, dec_out.reshape(-1, 2, dec_out.shape[1]))


def solution(mesh):
    shape = mesh.devices.shape
    fine = jax.sharding.Mesh(mesh.devices.reshape(-1, Z_CHIPS, CORES, *shape[1:]), (*CTX, *mesh.axis_names[1:]))
    placed = (
        P(CTX, ("grp", "tp")),
        P(CTX, None, ("grp", "tp")),
        P(CTX, None, ("grp", "tp")),
        P(CTX, None, ("grp", "tp")),
        P(CTX, None, None, ("grp", "tp")),
        P(CTX, None, None, ("grp", "tp")),
        P(),
        P(CTX),
        P(("grp", "tp"), CTX),
    )
    return jax.shard_map(
        shards,
        mesh=fine,
        in_specs=placed,
        out_specs=(P(CTX, ("grp", "tp")), P(("grp", "tp"), None, CTX)),
        check_vma=False,
    )
```

```python
import functools
import math

import jax
import jax.numpy as jnp
from jax import lax
from jax.experimental import pallas as pl
from jax.experimental.pallas import tpu as pltpu
from jax.sharding import PartitionSpec as P

HEAD_SIZE = 128
CORES = 2
Z_CHIPS = 8
CONTEXT_DEV = 1280
CTX = ("y", "z", "core")
SCALE = math.log2(math.e) / math.sqrt(HEAD_SIZE)
LOWEST = -1e30
F32 = jnp.float32
BF16 = jnp.bfloat16
TILE = 256
VMEM = pl.BlockSpec(memory_space=pltpu.VMEM)
SMEM = pl.BlockSpec(memory_space=pltpu.SMEM)


def params(mib):
    return pltpu.CompilerParams(vmem_limit_bytes=mib * 1024 * 1024)


def dot_nt(a, b):
    return lax.dot_general(a, b, (((1,), (1,)), ((), ())), preferred_element_type=F32)


def dot_nn(a, b):
    return lax.dot_general(a, b, (((1,), (0,)), ((), ())), preferred_element_type=F32)


def prepare_body(
    me_ref, table_ref, length_ref, q_ref, context_ref, stretch_ref, ask_ref, row_ref, rows_ref, kv_ref, list_ref
):
    rows_dev = length_ref.shape[0]
    nblk = table_ref.shape[0]
    lists = ask_ref.shape[1] // 2
    heads = lists // 2
    pool_dev = ask_ref.shape[0]
    block = context_ref.shape[0] // 20
    q = q_ref[...].astype(F32)
    for r in range(rows_dev):
        for t in range(2):
            for h in range(heads):
                at = t * heads + h
                list_ref[r, at : at + 1, :] = q[2 * r + t : 2 * r + t + 1, h * HEAD_SIZE : (h + 1) * HEAD_SIZE]
    for r in range(rows_dev):
        asked = list_ref[r].astype(BF16)
        rows_ref[r] = asked
        for n in range(nblk):
            holder = table_ref[n, me_ref[0] * rows_dev + r] // pool_dev
            left = jnp.clip(length_ref[r] - n * block, 0, block).astype(F32)
            ask_ref[holder, :lists, :] = asked
            ask_ref[holder, lists:, :] = jnp.full((lists, HEAD_SIZE), left, F32).astype(BF16)
            row_ref[holder] = r

    def split(rows, at):
        count = rows.shape[0]
        half = count // 2
        i = lax.broadcasted_iota(jnp.int32, (count, count), 0)
        j = lax.broadcasted_iota(jnp.int32, (count, count), 1)
        source = jnp.where(i < half, 2 * i, 2 * (i - half) + 1)
        pick = jnp.where(j == source, 1.0, 0.0).astype(BF16)
        parted = dot_nn(pick, rows).astype(BF16)
        kv_ref[0, at : at + half, :] = parted[:half]
        kv_ref[1, at : at + half, :] = parted[half:]

    total = context_ref.shape[0]
    for start in range(0, total, 256):
        split(context_ref[start : start + 256, :], start // 2)
    split(stretch_ref[...], total // 2)


def prepare(me, table, length, q, context, stretch, holders):
    rows = (context.shape[0] + stretch.shape[0]) // 2
    rows_dev = length.shape[0]
    lists = 2 * q.shape[1] // HEAD_SIZE
    return pl.pallas_call(
        prepare_body,
        out_shape=[
            jax.ShapeDtypeStruct((holders, 2 * lists, HEAD_SIZE), BF16),
            jax.ShapeDtypeStruct((holders,), jnp.int32),
            jax.ShapeDtypeStruct((rows_dev, lists, HEAD_SIZE), BF16),
            jax.ShapeDtypeStruct((2, rows, HEAD_SIZE), BF16),
        ],
        in_specs=[SMEM, SMEM, SMEM, VMEM, VMEM, VMEM],
        out_specs=[VMEM, SMEM, VMEM, VMEM],
        scratch_shapes=[pltpu.VMEM((rows_dev, lists, HEAD_SIZE), F32)],
        compiler_params=params(16),
        name="prepare",
    )(me, table, length, q, context, stretch)


def stack_body(*refs):
    kv_refs, k_ref, v_ref = refs[:-2], refs[-2], refs[-1]
    sets = len(kv_refs)
    stretch = k_ref.shape[0] // sets - CONTEXT_DEV
    v_ref[:, HEAD_SIZE:] = jnp.ones((v_ref.shape[0], HEAD_SIZE), BF16)
    for n, ref in enumerate(kv_refs):
        first, last = n * CONTEXT_DEV, sets * CONTEXT_DEV + n * stretch
        k_ref[first : first + CONTEXT_DEV, :] = ref[0, :CONTEXT_DEV, :]
        v_ref[first : first + CONTEXT_DEV, :HEAD_SIZE] = ref[1, :CONTEXT_DEV, :]
        k_ref[last : last + stretch, :] = ref[0, CONTEXT_DEV:, :]
        v_ref[last : last + stretch, :HEAD_SIZE] = ref[1, CONTEXT_DEV:, :]


def stack(sets):
    keys = len(sets) * sets[0].shape[1]
    return pl.pallas_call(
        stack_body,
        out_shape=[
            jax.ShapeDtypeStruct((keys, HEAD_SIZE), BF16),
            jax.ShapeDtypeStruct((keys, 2 * HEAD_SIZE), BF16),
        ],
        in_specs=[VMEM] * len(sets),
        out_specs=[VMEM, VMEM],
        compiler_params=params(16),
        name="stack",
    )(*sets)


def diagonal():
    i = lax.broadcasted_iota(jnp.int32, (HEAD_SIZE, HEAD_SIZE), 0)
    j = lax.broadcasted_iota(jnp.int32, (HEAD_SIZE, HEAD_SIZE), 1)
    return i == j


def read_part(ref, first, stretch):
    width = TILE // stretch * HEAD_SIZE
    outputs = jnp.concatenate(
        [ref[:stretch, first + c : first + c + HEAD_SIZE] for c in range(0, width, HEAD_SIZE)], axis=0
    ).astype(F32)
    stat = ref[stretch : stretch + 16, first : first + TILE].astype(F32)
    level = stat[0:1] + stat[1:2] + stat[2:3]
    columns = []
    for g in range(0, TILE, HEAD_SIZE):
        column = jnp.sum(jnp.where(diagonal(), level[:, g : g + HEAD_SIZE], 0.0), axis=1, keepdims=True)
        columns.append(jnp.broadcast_to(column, (HEAD_SIZE, HEAD_SIZE)))
    return outputs, jnp.concatenate(columns, axis=0)


def join(outputs, levels):
    top = functools.reduce(jnp.maximum, levels)
    weights = [jnp.exp2(level - top) for level in levels]
    total = functools.reduce(jnp.add, weights)
    mixed = functools.reduce(jnp.add, [weight * output for weight, output in zip(weights, outputs)])
    return mixed / total, top + jnp.log2(total)


def write_outputs(ref, first, outputs, stretch):
    outputs = outputs.astype(BF16)
    for h in range(TILE // stretch):
        ref[:stretch, first + h * HEAD_SIZE : first + (h + 1) * HEAD_SIZE] = outputs[h * stretch : (h + 1) * stretch]


def write_level(ref, first, level, stretch):
    rows = []
    for g in range(0, TILE, HEAD_SIZE):
        rows.append(jnp.sum(jnp.where(diagonal(), level[g : g + HEAD_SIZE], 0.0), axis=0, keepdims=True))
    level = jnp.concatenate(rows, axis=1)
    high = level.astype(BF16).astype(F32)
    rest = level - high
    middle = rest.astype(BF16).astype(F32)
    row = lax.broadcasted_iota(jnp.int32, (16, TILE), 0)
    stat = jnp.where(row == 0, high, jnp.where(row == 1, middle, jnp.where(row == 2, rest - middle, 0.0)))
    ref[stretch : stretch + 16, first : first + TILE] = stat.astype(BF16)
    ref[stretch : stretch + 16, first + TILE : first + TILE // stretch * HEAD_SIZE] = jnp.zeros(
        (16, TILE // stretch * HEAD_SIZE - TILE), BF16
    )


def attend_body(which, groups, arrived, riders, delta_ref, q_ref, k_ref, v_ref, *refs):
    refs = list(refs)
    part_ref = refs.pop(0) if arrived else None
    rider_ref = refs.pop(0) if riders == "own" else part_ref
    out_ref, s_ref, p_ref = refs
    stretch = q_ref.shape[0]
    sets = delta_ref.shape[1]
    keys = k_ref.shape[0]
    heads_tile = TILE // stretch
    chunks = [(at, 256) for at in range(0, keys, 256)]

    if riders == "own":
        out_ref[stretch + 16 :, :] = rider_ref[...]
    elif riders == "arrived":
        out_ref[stretch + 16 :, :] = rider_ref[stretch + 16 :, :]

    def queries(group):
        heads = range(group * heads_tile, (group + 1) * heads_tile)
        return jnp.concatenate([q_ref[:, h * HEAD_SIZE : (h + 1) * HEAD_SIZE] for h in heads], axis=0)

    def score(slot, q, top, chunk):
        at, size = chunk
        s = dot_nt(q, k_ref[at : at + size, :])
        if at + size > sets * CONTEXT_DEV:
            row = lax.rem(lax.broadcasted_iota(jnp.int32, (TILE, size), 0), stretch)
            col = lax.broadcasted_iota(jnp.int32, (TILE, size), 1)
            bound = delta_ref[which, sets - 1] + (sets - 1) * stretch - col
            for m in reversed(range(sets - 1)):
                bound = jnp.where(col < (m + 1) * stretch, delta_ref[which, m] + m * stretch - col, bound)
            s = jnp.where(row + bound >= 0, s, LOWEST)
        s_ref[slot, :, at : at + size] = s
        for c in range(0, size, HEAD_SIZE):
            part = s[:, c : c + HEAD_SIZE]
            top = part if top is None else jnp.maximum(top, part)
        return top

    def settle(top):
        return jnp.broadcast_to(jnp.max(top, axis=1, keepdims=True), (TILE, HEAD_SIZE)) * SCALE

    def weigh(slot, top, chunk):
        at, size = chunk
        for c in range(at, at + size, HEAD_SIZE):
            p_ref[slot, :, c : c + HEAD_SIZE] = jnp.exp2(s_ref[slot, :, c : c + HEAD_SIZE] * SCALE - top).astype(BF16)

    def finish(n, slot, top):
        first = n * heads_tile * HEAD_SIZE
        total = dot_nn(p_ref[slot], v_ref[...])
        weight = total[:, HEAD_SIZE:]
        output, level = total[:, :HEAD_SIZE] / weight, top + jnp.log2(weight)
        if arrived:
            other, other_level = read_part(part_ref, first, stretch)
            output, level = join([output, other], [level, other_level])
        write_outputs(out_ref, first, output, stretch)
        write_level(out_ref, first, level, stretch)

    top = None
    q = queries(groups[0])
    for chunk in chunks:
        top = score(0, q, top, chunk)
    top = settle(top)
    for n in range(len(groups)):
        coming = None
        more = n + 1 < len(groups)
        if more:
            q = queries(groups[n + 1])
        for chunk in chunks:
            weigh(n % 2, top, chunk)
            if more:
                coming = score((n + 1) % 2, q, coming, chunk)
        finish(n, n % 2, top)
        if more:
            top = settle(coming)


def attend(which, groups, deltas, queries, keys, values, part=None, rider=None):
    stretch = queries.shape[0]
    width = len(groups) * TILE // stretch * HEAD_SIZE
    count = keys.shape[0]
    operands = [deltas, queries, keys, values]
    rows = stretch + 16
    riders = None
    if part is not None:
        operands.append(part)
        if rider == "arrived":
            riders = rider
            rows = part.shape[0]
    if riders is None and rider is not None:
        riders = "own"
        operands.append(rider)
        rows += rider.shape[0]
    return pl.pallas_call(
        functools.partial(attend_body, which, groups, part is not None, riders),
        out_shape=jax.ShapeDtypeStruct((rows, width), BF16),
        in_specs=[SMEM] + [VMEM] * (len(operands) - 1),
        out_specs=VMEM,
        scratch_shapes=[pltpu.VMEM((2, TILE, count), F32), pltpu.VMEM((2, TILE, count), BF16)],
        compiler_params=params(32),
        cost_estimate=pl.CostEstimate(
            flops=8 * len(groups) * TILE * count * HEAD_SIZE,
            bytes_accessed=4 * count * HEAD_SIZE,
            transcendentals=len(groups) * TILE * count,
        ),
        name="attend",
    )(*operands)


def merge_body(own_count, *refs):
    own_refs, part_refs, out_ref = refs[:own_count], refs[own_count:-1], refs[-1]
    stretch = out_ref.shape[0]
    for n, ref in enumerate(own_refs):
        first = n * TILE // stretch * HEAD_SIZE
        read = [read_part(ref, 0, stretch)] + [read_part(part, first, stretch) for part in part_refs]
        output, _ = join([x for x, _ in read], [x for _, x in read])
        write_outputs(out_ref, first, output, stretch)


def merge(own, parts, stretch):
    width = sum(x.shape[1] for x in own)
    return pl.pallas_call(
        functools.partial(merge_body, len(own)),
        out_shape=jax.ShapeDtypeStruct((stretch, width), BF16),
        in_specs=[VMEM] * (len(own) + len(parts)),
        out_specs=VMEM,
        compiler_params=params(16),
        name="merge",
    )(*own, *parts)


def look_body(place_ref, ask_ref, pool_ref, out_ref, s_ref, p_ref):
    owners = ask_ref.shape[0]
    half = ask_ref.shape[1] // 2
    span = pool_ref.shape[1]
    for d in range(owners):
        s_ref[d * half : (d + 1) * half, :] = dot_nt(ask_ref[d, :half, :], pool_ref[place_ref[d]])
    col = lax.broadcasted_iota(jnp.int32, (half, span), 1)
    lane = lax.broadcasted_iota(jnp.int32, (half, HEAD_SIZE), 1)
    even = (col & 1) == 0
    for d in range(owners):
        limit = ask_ref[d, half:, :].astype(F32) * 2.0
        limit = jnp.concatenate([limit] * (span // HEAD_SIZE), axis=1)
        allowed = even & (col.astype(F32) < limit)
        s = jnp.where(allowed, s_ref[d * half : (d + 1) * half, :], LOWEST)
        top = jnp.max(s, axis=1, keepdims=True)
        p = jnp.where(allowed, jnp.exp2((s - top) * SCALE), 0.0)
        total = jnp.sum(p, axis=1, keepdims=True)
        p_ref[d * half : (d + 1) * half, :] = pltpu.roll(p, 1, 1).astype(BF16)
        seen = total > 0.0
        level = jnp.where(seen, top * SCALE + jnp.log2(jnp.where(seen, total, 1.0)), LOWEST)
        level = jnp.broadcast_to(level, (half, HEAD_SIZE))
        high = level.astype(BF16).astype(F32)
        rest = level - high
        middle = rest.astype(BF16).astype(F32)
        low = rest - middle
        stat = jnp.where(lane == 0, high, jnp.where(lane == 1, middle, jnp.where(lane == 2, low, 0.0)))
        out_ref[d, half:, :] = stat.astype(BF16)
        s_ref[d * half : (d + 1) * half, :HEAD_SIZE] = jnp.broadcast_to(
            jnp.where(seen, 1.0 / jnp.where(seen, total, 1.0), 0.0), (half, HEAD_SIZE)
        )
    for d in range(owners):
        o = dot_nn(p_ref[d * half : (d + 1) * half, :], pool_ref[place_ref[d]])
        out_ref[d, :half, :] = (o * s_ref[d * half : (d + 1) * half, :HEAD_SIZE]).astype(BF16)


def look(place, ask, pool):
    owners, rows, width = ask.shape
    span = pool.shape[1]
    return pl.pallas_call(
        look_body,
        out_shape=jax.ShapeDtypeStruct(ask.shape, BF16),
        in_specs=[SMEM, VMEM, VMEM],
        out_specs=VMEM,
        scratch_shapes=[
            pltpu.VMEM((owners * rows // 2, span), F32),
            pltpu.VMEM((owners * rows // 2, span), BF16),
        ],
        compiler_params=params(24),
        cost_estimate=pl.CostEstimate(
            flops=16 * owners * rows * span * width, bytes_accessed=2 * owners * span * width, transcendentals=0
        ),
        name="look_in_blocks",
    )(place, ask, pool)


def gather_body(row_ref, answer_ref, q_ref, new_ref, out_ref, level_ref, top_ref, sum_ref, acc_ref, flat_ref):
    holders = answer_ref.shape[0]
    rows, lists = q_ref.shape[0], q_ref.shape[1]
    heads = lists // 2
    lane = lax.broadcasted_iota(jnp.int32, (lists, HEAD_SIZE), 1)
    later = lax.broadcasted_iota(jnp.int32, (lists, HEAD_SIZE), 0) >= heads
    own = []
    for r in range(rows):
        q = q_ref[r].astype(F32)
        new = new_ref[r].astype(F32)
        scores = []
        for t in range(2):
            s = jnp.sum(q * new[2 * t : 2 * t + 1, :], axis=1, keepdims=True) * SCALE
            scores.append(jnp.broadcast_to(s, (lists, HEAD_SIZE)))
        scores[1] = jnp.where(later, scores[1], LOWEST)
        top_ref[r] = jnp.maximum(scores[0], scores[1])
        own.append((scores, new))
    for d in range(holders):
        stat = answer_ref[d, lists:, :].astype(F32)
        level = jnp.sum(jnp.where(lane < 3, stat, 0.0), axis=1, keepdims=True)
        level_ref[d] = jnp.broadcast_to(level, (lists, HEAD_SIZE))
    for d in range(holders):
        r = row_ref[d]
        top_ref[r] = jnp.maximum(top_ref[r], level_ref[d])
    for r in range(rows):
        scores, new = own[r]
        first = jnp.exp2(scores[0] - top_ref[r])
        second = jnp.exp2(scores[1] - top_ref[r])
        sum_ref[r] = first + second
        acc_ref[r] = first * new[1:2, :] + second * new[3:4, :]
    for d in range(holders):
        r = row_ref[d]
        weight = jnp.exp2(level_ref[d] - top_ref[r])
        sum_ref[r] = sum_ref[r] + weight
        acc_ref[r] = acc_ref[r] + weight * answer_ref[d, :lists, :].astype(F32)
    for r in range(rows):
        o = acc_ref[r] / sum_ref[r]
        for t in range(2):
            for h in range(heads):
                flat_ref[2 * r + t : 2 * r + t + 1, h * HEAD_SIZE : (h + 1) * HEAD_SIZE] = o[
                    t * heads + h : t * heads + h + 1, :
                ]
    out_ref[...] = flat_ref[...].astype(BF16)


def gather_answers(row_of, answer, q, new):
    rows, lists, width = q.shape
    holders = answer.shape[0]
    heads = lists // 2
    state = pltpu.VMEM((rows, lists, width), F32)
    return pl.pallas_call(
        gather_body,
        out_shape=jax.ShapeDtypeStruct((2 * rows, heads * width), BF16),
        in_specs=[SMEM, VMEM, VMEM, VMEM],
        out_specs=VMEM,
        scratch_shapes=[
            pltpu.VMEM((holders, lists, width), F32),
            state,
            state,
            state,
            pltpu.VMEM((2 * rows, heads * width), F32),
        ],
        compiler_params=params(16),
        name="gather_answers",
    )(row_of, answer, q, new)


def project_body(place_ref, own_ref, w_ref, *refs):
    ref_list, out_ref, total_ref, rows_ref = refs[:-3], refs[-3], refs[-2], refs[-1]
    rows = own_ref.shape[0]
    rows_ref[:rows, :] = own_ref[...]
    for n, ref in enumerate(ref_list):
        rows_ref[(n + 1) * rows : (n + 2) * rows, :] = ref[ref.shape[0] - rows :, :]
    total = dot_nn(rows_ref[...], w_ref[...])
    for n in range(rows_ref.shape[0] // 8):
        at = pl.multiple_of(place_ref[n], 8)
        total_ref[pl.ds(at, 8), :] = total[8 * n : 8 * n + 8]
    out_ref[...] = total_ref[...].astype(BF16)


def project(place, own, w, parts):
    rows = own.shape[0] * (len(parts) + 1)
    return pl.pallas_call(
        project_body,
        out_shape=jax.ShapeDtypeStruct((rows, w.shape[1]), BF16),
        in_specs=[SMEM] + [VMEM] * (len(parts) + 2),
        out_specs=VMEM,
        scratch_shapes=[pltpu.VMEM((rows, w.shape[1]), F32), pltpu.VMEM((rows, own.shape[1]), BF16)],
        compiler_params=params(16),
        name="project",
    )(place, own, w, *parts)


def shards(
    q_stretch,
    stretch_key_value,
    context_key_value,
    dec_q,
    dec_new,
    pool_key_value,
    block_table,
    cache_len,
    w_out,
):
    me = lax.axis_index(CTX)
    z = lax.axis_index("z")
    cycle = lax.axis_size(CTX)
    stretch = q_stretch.shape[0]
    rows_dev, nblk = dec_q.shape[0], block_table.shape[1]
    pool_dev, block_size = pool_key_value.shape[:2]

    def after(x, *others):
        return lax.optimization_barrier((x, *others))[0]

    def swap(x, name):
        return lax.ppermute(x, name, [(0, 1), (1, 0)])

    def turn(x, step):
        return lax.ppermute(x, "z", [(n, (n + step) % Z_CHIPS) for n in range(Z_CHIPS)])

    ask, row_of, q_rows, kv = prepare(
        me.reshape(1).astype(jnp.int32),
        block_table.T,
        cache_len,
        dec_q.reshape(2 * rows_dev, -1),
        context_key_value.reshape(-1, HEAD_SIZE),
        stretch_key_value.reshape(-1, HEAD_SIZE),
        cycle,
    )
    kv_core, kv_y = swap(kv, "core"), swap(kv, "y")
    right, left = [q_stretch], [q_stretch]
    right.append(turn(q_stretch, 1))
    left.append(turn(q_stretch, -1))
    ask = lax.all_to_all(ask, CTX, split_axis=0, concat_axis=0, tiled=True)
    table = block_table.reshape(cycle, rows_dev * nblk)
    place = jnp.sum(jnp.where(table // pool_dev == me, table % pool_dev, 0), axis=1)
    right.append(turn(after(right[1], ask), 1))
    left.append(turn(after(left[1], ask), -1))
    look_out = look(place, ask, pool_key_value.reshape(pool_dev, 2 * block_size, HEAD_SIZE))
    kv_yc = swap(after(kv_y, look_out), "core")
    answer = lax.all_to_all(look_out, CTX, split_axis=0, concat_axis=0, tiled=True)
    attn = gather_answers(row_of, answer, q_rows, dec_new.reshape(rows_dev, 4, HEAD_SIZE))
    right.append(turn(after(right[2], attn), 1))
    left.append(turn(after(left[2], attn), -1))
    attn_core = swap(attn, "core")

    shifts = jnp.arange(Z_CHIPS, dtype=jnp.int32)
    corners = jnp.arange(2 * CORES, dtype=jnp.int32)
    corners = me ^ (corners // CORES * CORES * Z_CHIPS + corners % CORES)
    askers = me + ((z - shifts + Z_CHIPS) % Z_CHIPS - z) * CORES
    deltas = (askers[:, None] - corners[None, :]) * stretch
    keys, values = stack([kv, kv_core, kv_y, kv_yc])

    groups = (0, 1)
    own = [attend(0, (0,), after(deltas, attn), q_stretch, keys, values)]
    right.append(turn(after(right[3], own[0]), 1))
    pair = jnp.concatenate([attn, attn_core], axis=0)
    pair_y = swap(after(pair, own[0]), "y")
    own.append(attend(0, (1,), after(deltas, own[0]), q_stretch, keys, values))
    attn = jnp.concatenate([pair, pair_y], axis=0)
    riders = attn.shape[0]

    def go(shift, previous, part=None, rider="arrived"):
        queries = right[shift] if shift > 0 else left[-shift]
        return attend(shift % Z_CHIPS, groups, after(deltas, previous), queries, keys, values, part, rider)

    out = go(4, own[1], None, attn)
    from_right = [turn(out, -1)]
    out = go(-3, out, None, attn)
    from_left = [turn(out, 1)]
    out = go(3, out, from_right[0])
    from_right.append(turn(out, -1))
    out = go(-2, out, from_left[0])
    from_left.append(turn(out, 1))
    out = go(2, out, from_right[1])
    from_right.append(turn(out, -1))
    out = go(-1, out, from_left[1])
    from_left.append(turn(out, 1))
    rest = from_right[2][stretch + 16 :]
    farthest = turn(rest, -1)
    out = go(1, (out, rest), from_right[2], None)
    last = turn(out, -1)

    relative = jnp.where(shifts > Z_CHIPS // 2, Z_CHIPS // 2 - shifts, shifts)
    there = ((z + relative + Z_CHIPS) % Z_CHIPS - z) * CORES
    holders = ((there[:, None] + corners[None, :]) * (2 * rows_dev)).reshape(-1)
    partial_out = project(holders, after(attn, out), w_out, [*from_right, farthest, *from_left])
    shares = lax.axis_size(("grp", "tp"))
    pieces = lax.all_to_all(
        partial_out.reshape(shares, -1, partial_out.shape[1]), ("grp", "tp"), split_axis=0, concat_axis=0, tiled=True
    )
    pre_out = merge(own, [last, from_left[2]], stretch)
    dec_out = jnp.sum(pieces.astype(F32), axis=0).astype(BF16)
    return (pre_out, dec_out.reshape(-1, 2, dec_out.shape[1]))


def solution(mesh):
    shape = mesh.devices.shape
    fine = jax.sharding.Mesh(mesh.devices.reshape(-1, Z_CHIPS, CORES, *shape[1:]), (*CTX, *mesh.axis_names[1:]))
    placed = (
        P(CTX, ("grp", "tp")),
        P(CTX, None, ("grp", "tp")),
        P(CTX, None, ("grp", "tp")),
        P(CTX, None, ("grp", "tp")),
        P(CTX, None, None, ("grp", "tp")),
        P(CTX, None, None, ("grp", "tp")),
        P(),
        P(CTX),
        P(("grp", "tp"), CTX),
    )
    return jax.shard_map(
        shards,
        mesh=fine,
        in_specs=placed,
        out_specs=(P(CTX, ("grp", "tp")), P(("grp", "tp"), None, CTX)),
        check_vma=False,
    )
```

```python
import functools
import math

import jax
import jax.numpy as jnp
from jax import lax
from jax.experimental import pallas as pl
from jax.experimental.pallas import tpu as pltpu
from jax.sharding import PartitionSpec as P

HEAD_SIZE = 128
CORES = 2
Z_CHIPS = 8
CONTEXT_DEV = 1280
BLOCK = 128
CTX = ("y", "z", "core")
SCALE = math.log2(math.e) / math.sqrt(HEAD_SIZE)
LOWEST = -1e30
F32 = jnp.float32
BF16 = jnp.bfloat16
VMEM = pl.BlockSpec(memory_space=pltpu.VMEM)
SMEM = pl.BlockSpec(memory_space=pltpu.SMEM)


def params(mib):
    return pltpu.CompilerParams(vmem_limit_bytes=mib * 1024 * 1024)


def dot_nt(a, b):
    return lax.dot_general(a, b, (((1,), (1,)), ((), ())), preferred_element_type=F32)


def dot_nn(a, b):
    return lax.dot_general(a, b, (((1,), (0,)), ((), ())), preferred_element_type=F32)


def split_body(context_hbm, stretch_hbm, kv_ref, context_ref, stretch_ref, sem):
    copies = []
    total = context_ref.shape[0]
    step = total // 5
    for n in range(5):
        rows = pl.ds(n * step, step)
        copies.append(pltpu.make_async_copy(context_hbm.at[rows], context_ref.at[rows], sem.at[n]))
    copies.append(pltpu.make_async_copy(stretch_hbm, stretch_ref, sem.at[5]))
    for copy in copies:
        copy.start()

    def split(rows, at):
        count = rows.shape[0]
        half = count // 2
        i = lax.broadcasted_iota(jnp.int32, (count, count), 0)
        j = lax.broadcasted_iota(jnp.int32, (count, count), 1)
        source = jnp.where(i < half, 2 * i, 2 * (i - half) + 1)
        pick = jnp.where(j == source, 1.0, 0.0).astype(BF16)
        parted = dot_nn(pick, rows).astype(BF16)
        kv_ref[0, at : at + half, :] = parted[:half]
        kv_ref[1, at : at + half, :] = parted[half:]

    for n in range(5):
        copies[n].wait()
        for start in range(n * step, (n + 1) * step, 256):
            split(context_ref[start : start + 256, :], start // 2)
    copies[5].wait()
    split(stretch_ref[...], total // 2)


def split_keys_values(context, stretch):
    rows = (context.shape[0] + stretch.shape[0]) // 2
    hbm = pl.BlockSpec(memory_space=pltpu.HBM)
    return pl.pallas_call(
        split_body,
        out_shape=jax.ShapeDtypeStruct((2, rows, HEAD_SIZE), BF16),
        in_specs=[hbm, hbm],
        out_specs=VMEM,
        scratch_shapes=[
            pltpu.VMEM(context.shape, BF16),
            pltpu.VMEM(stretch.shape, BF16),
            pltpu.SemaphoreType.DMA((6,)),
        ],
        compiler_params=params(16),
        name="split_keys_values",
    )(*(pltpu.with_memory_space_constraint(x, pltpu.HBM) for x in (context, stretch)))


def question_body(me_ref, table_ref, length_ref, q_ref, ask_ref, row_ref, rows_ref, list_ref):
    rows_dev = length_ref.shape[0]
    nblk = table_ref.shape[0]
    lists = ask_ref.shape[1] // 2
    heads = lists // 2
    pool_dev = ask_ref.shape[0]
    for r in range(rows_dev):
        q = q_ref[r].astype(F32)
        for t in range(2):
            for h in range(heads):
                at = t * heads + h
                list_ref[r, at : at + 1, :] = q[t : t + 1, h * HEAD_SIZE : (h + 1) * HEAD_SIZE]
    for r in range(rows_dev):
        asked = list_ref[r].astype(BF16)
        rows_ref[r] = asked
        for n in range(nblk):
            holder = table_ref[n, me_ref[0] * rows_dev + r] // pool_dev
            left = jnp.clip(length_ref[r] - n * BLOCK, 0, BLOCK).astype(F32)
            ask_ref[holder, :lists, :] = asked
            ask_ref[holder, lists:, :] = jnp.full((lists, HEAD_SIZE), left, F32).astype(BF16)
            row_ref[holder] = r


def question(me, table, length, q, holders):
    rows_dev = length.shape[0]
    lists = 2 * q.shape[2] // HEAD_SIZE
    return pl.pallas_call(
        question_body,
        out_shape=[
            jax.ShapeDtypeStruct((holders, 2 * lists, HEAD_SIZE), BF16),
            jax.ShapeDtypeStruct((holders,), jnp.int32),
            jax.ShapeDtypeStruct((rows_dev, lists, HEAD_SIZE), BF16),
        ],
        in_specs=[SMEM, SMEM, SMEM, VMEM],
        out_specs=[VMEM, SMEM, VMEM],
        scratch_shapes=[pltpu.VMEM((rows_dev, lists, HEAD_SIZE), F32)],
        compiler_params=params(16),
        name="question",
    )(me, table, length, q)


def stack_body(*refs):
    kv_refs, k_ref, v_ref = refs[:-2], refs[-2], refs[-1]
    sets = len(kv_refs)
    stretch = v_ref.shape[0] // sets - CONTEXT_DEV
    one = jnp.where(diagonal(), 1.0, 0.0).astype(BF16)
    v_ref[:, HEAD_SIZE:] = jnp.ones((v_ref.shape[0], HEAD_SIZE), BF16)
    for n, ref in enumerate(kv_refs):
        first, last = n * CONTEXT_DEV, sets * CONTEXT_DEV + n * stretch
        for at in range(0, CONTEXT_DEV, 256):
            k_ref[:, first + at : first + at + 256] = dot_nt(one, ref[0, at : at + 256, :]).astype(BF16)
        v_ref[first : first + CONTEXT_DEV, :HEAD_SIZE] = ref[1, :CONTEXT_DEV, :]
        v_ref[last : last + stretch, :HEAD_SIZE] = ref[1, CONTEXT_DEV:, :]
    k = jnp.concatenate([ref[0, CONTEXT_DEV:, :] for ref in kv_refs], axis=0)
    k_ref[:, sets * CONTEXT_DEV :] = dot_nt(one, k).astype(BF16)


def stack(sets):
    keys = len(sets) * sets[0].shape[1]
    return pl.pallas_call(
        stack_body,
        out_shape=[
            jax.ShapeDtypeStruct((HEAD_SIZE, keys), BF16),
            jax.ShapeDtypeStruct((keys, 2 * HEAD_SIZE), BF16),
        ],
        in_specs=[VMEM] * len(sets),
        out_specs=[VMEM, VMEM],
        compiler_params=params(16),
        name="stack",
    )(*sets)


def diagonal():
    i = lax.broadcasted_iota(jnp.int32, (HEAD_SIZE, HEAD_SIZE), 0)
    j = lax.broadcasted_iota(jnp.int32, (HEAD_SIZE, HEAD_SIZE), 1)
    return i == j


def read_part(ref, stretch):
    width = ref.shape[1]
    rows = width // HEAD_SIZE * stretch
    outputs = jnp.concatenate([ref[:stretch, c : c + HEAD_SIZE] for c in range(0, width, HEAD_SIZE)], axis=0)
    stat = ref[stretch : stretch + 16, :rows].astype(F32)
    level = stat[0:1] + stat[1:2] + stat[2:3]
    columns = []
    for g in range(0, rows, HEAD_SIZE):
        column = jnp.sum(jnp.where(diagonal(), level[:, g : g + HEAD_SIZE], 0.0), axis=1, keepdims=True)
        columns.append(jnp.broadcast_to(column, (HEAD_SIZE, HEAD_SIZE)))
    return outputs.astype(F32), jnp.concatenate(columns, axis=0)


def join(outputs, levels):
    top = functools.reduce(jnp.maximum, levels)
    weights = [jnp.exp2(level - top) for level in levels]
    total = functools.reduce(jnp.add, weights)
    mixed = functools.reduce(jnp.add, [weight * output for weight, output in zip(weights, outputs)])
    return mixed / total, top + jnp.log2(total)


def write_outputs(ref, outputs, stretch):
    outputs = outputs.astype(BF16)
    for h in range(outputs.shape[0] // stretch):
        ref[:stretch, h * HEAD_SIZE : (h + 1) * HEAD_SIZE] = outputs[h * stretch : (h + 1) * stretch]


def write_level(ref, level, stretch):
    rows = level.shape[0]
    lines = []
    for g in range(0, rows, HEAD_SIZE):
        lines.append(jnp.sum(jnp.where(diagonal(), level[g : g + HEAD_SIZE], 0.0), axis=0, keepdims=True))
    level = jnp.concatenate(lines, axis=1)
    high = level.astype(BF16).astype(F32)
    rest = level - high
    middle = rest.astype(BF16).astype(F32)
    row = lax.broadcasted_iota(jnp.int32, (16, rows), 0)
    stat = jnp.where(row == 0, high, jnp.where(row == 1, middle, jnp.where(row == 2, rest - middle, 0.0)))
    ref[stretch : stretch + 16, :rows] = stat.astype(BF16)
    ref[stretch : stretch + 16, rows:] = jnp.zeros((16, ref.shape[1] - rows), BF16)


def attend_body(which, arrived, delta_ref, q_ref, k_ref, v_ref, *refs):
    refs = list(refs)
    part_ref = refs.pop(0) if arrived else None
    out_ref, p_ref, total_ref, top_ref = refs
    stretch, width = q_ref.shape
    sets = delta_ref.shape[1]
    keys = v_ref.shape[0]
    rows = width // HEAD_SIZE * stretch
    chunk = 256
    span = CONTEXT_DEV
    q = jnp.concatenate([q_ref[:, c : c + HEAD_SIZE] for c in range(0, width, HEAD_SIZE)], axis=0)

    def score(k, masked):
        s = dot_nn(q, k)
        if masked:
            row = lax.rem(lax.broadcasted_iota(jnp.int32, s.shape, 0), stretch)
            col = lax.broadcasted_iota(jnp.int32, s.shape, 1)
            bound = delta_ref[which, sets - 1] + (sets - 1) * stretch - col
            for m in reversed(range(sets - 1)):
                bound = jnp.where(col < (m + 1) * stretch, delta_ref[which, m] + m * stretch - col, bound)
            s = jnp.where(row + bound >= 0, s, LOWEST)
        return s

    def highest(s):
        parts = [s[:, c : c + HEAD_SIZE] for c in range(0, s.shape[1], HEAD_SIZE)]
        return functools.reduce(jnp.maximum, parts)

    def spread(top):
        return jnp.broadcast_to(jnp.max(top, axis=1, keepdims=True), (rows, HEAD_SIZE)) * SCALE

    def weigh(s, top):
        parts = [s[:, c : c + HEAD_SIZE] for c in range(0, s.shape[1], HEAD_SIZE)]
        return jnp.concatenate([jnp.exp2(part * SCALE - top) for part in parts], axis=1).astype(BF16)

    top = spread(highest(score(k_ref[:, :chunk], False)))
    total = None
    begun = 0
    for at in range(0, keys, chunk):
        p_ref[:, at : at + chunk] = weigh(score(k_ref[:, at : at + chunk], at >= sets * CONTEXT_DEV), top)
        done = at + chunk
        if done - begun >= span and keys - done >= chunk * 2 or done == keys:
            part = dot_nn(p_ref[:, begun:done], v_ref[begun:done, :])
            total = part if total is None else total + part
            begun = done
    total_ref[...] = total
    top_ref[...] = top

    @pl.when(jnp.logical_not(jnp.max(total[:, HEAD_SIZE:]) < 1e37))
    def again():
        last = score(k_ref[:, keys - chunk :], True)

        def climb(n, top):
            k = k_ref[:, pl.ds(pl.multiple_of(n * chunk, chunk), chunk)]
            return jnp.maximum(top, highest(score(k, False)))

        count = (keys - chunk) // chunk
        top_ref[...] = spread(lax.fori_loop(0, count, climb, highest(last)))
        total_ref[...] = dot_nn(weigh(last, top_ref[...]), v_ref[keys - chunk :, :])

        def add(n, carry):
            at = pl.ds(pl.multiple_of(n * chunk, chunk), chunk)
            total_ref[...] += dot_nn(weigh(score(k_ref[:, at], False), top_ref[...]), v_ref[at, :])
            return carry

        lax.fori_loop(0, count, add, 0)

    weight = total_ref[:, HEAD_SIZE:]
    output, level = total_ref[:, :HEAD_SIZE] / weight, top_ref[...] + jnp.log2(weight)
    if arrived:
        other, other_level = read_part(part_ref, stretch)
        output, level = join([output, other], [level, other_level])
    write_outputs(out_ref, output, stretch)
    write_level(out_ref, level, stretch)


def attend(which, deltas, queries, keys, values, part=None):
    stretch, width = queries.shape
    rows = width // HEAD_SIZE * stretch
    count = values.shape[0]
    operands = [deltas, queries, keys, values] + ([] if part is None else [part])
    return pl.pallas_call(
        functools.partial(attend_body, which, part is not None),
        out_shape=jax.ShapeDtypeStruct((stretch + 16, width), BF16),
        in_specs=[SMEM] + [VMEM] * (len(operands) - 1),
        out_specs=VMEM,
        scratch_shapes=[
            pltpu.VMEM((rows, count), BF16),
            pltpu.VMEM((rows, 2 * HEAD_SIZE), F32),
            pltpu.VMEM((rows, HEAD_SIZE), F32),
        ],
        compiler_params=params(32),
        cost_estimate=pl.CostEstimate(
            flops=8 * rows * count * HEAD_SIZE,
            bytes_accessed=4 * count * HEAD_SIZE,
            transcendentals=rows * count,
        ),
        name="attend",
    )(*operands)


def merge_body(*refs):
    part_refs, out_ref = refs[:-1], refs[-1]
    stretch = out_ref.shape[0]
    read = [read_part(ref, stretch) for ref in part_refs]
    output, _ = join([x for x, _ in read], [x for _, x in read])
    write_outputs(out_ref, output, stretch)


def merge(parts, stretch):
    return pl.pallas_call(
        merge_body,
        out_shape=jax.ShapeDtypeStruct((stretch, parts[0].shape[1]), BF16),
        in_specs=[VMEM] * len(parts),
        out_specs=VMEM,
        compiler_params=params(16),
        name="merge",
    )(*parts)


def look_body(place_ref, ask_ref, pool_ref, out_ref, s_ref, p_ref):
    owners = ask_ref.shape[0]
    half = ask_ref.shape[1] // 2
    span = pool_ref.shape[1]
    for d in range(owners):
        s_ref[d * half : (d + 1) * half, :] = dot_nt(ask_ref[d, :half, :], pool_ref[place_ref[d]])
    col = lax.broadcasted_iota(jnp.int32, (half, span), 1)
    lane = lax.broadcasted_iota(jnp.int32, (half, HEAD_SIZE), 1)
    even = (col & 1) == 0
    for d in range(owners):
        limit = ask_ref[d, half:, :].astype(F32) * 2.0
        limit = jnp.concatenate([limit] * (span // HEAD_SIZE), axis=1)
        allowed = even & (col.astype(F32) < limit)
        s = jnp.where(allowed, s_ref[d * half : (d + 1) * half, :], LOWEST)
        top = jnp.max(s, axis=1, keepdims=True)
        p = jnp.where(allowed, jnp.exp2((s - top) * SCALE), 0.0)
        total = jnp.sum(p, axis=1, keepdims=True)
        p_ref[d * half : (d + 1) * half, :] = pltpu.roll(p, 1, 1).astype(BF16)
        seen = total > 0.0
        level = jnp.where(seen, top * SCALE + jnp.log2(jnp.where(seen, total, 1.0)), LOWEST)
        level = jnp.broadcast_to(level, (half, HEAD_SIZE))
        high = level.astype(BF16).astype(F32)
        rest = level - high
        middle = rest.astype(BF16).astype(F32)
        low = rest - middle
        stat = jnp.where(lane == 0, high, jnp.where(lane == 1, middle, jnp.where(lane == 2, low, 0.0)))
        out_ref[d, half:, :] = stat.astype(BF16)
        s_ref[d * half : (d + 1) * half, :HEAD_SIZE] = jnp.broadcast_to(
            jnp.where(seen, 1.0 / jnp.where(seen, total, 1.0), 0.0), (half, HEAD_SIZE)
        )
    for d in range(owners):
        o = dot_nn(p_ref[d * half : (d + 1) * half, :], pool_ref[place_ref[d]])
        out_ref[d, :half, :] = (o * s_ref[d * half : (d + 1) * half, :HEAD_SIZE]).astype(BF16)


def look(place, ask, pool):
    owners, rows, width = ask.shape
    span = pool.shape[1]
    return pl.pallas_call(
        look_body,
        out_shape=jax.ShapeDtypeStruct(ask.shape, BF16),
        in_specs=[SMEM, VMEM, VMEM],
        out_specs=VMEM,
        scratch_shapes=[
            pltpu.VMEM((owners * rows // 2, span), F32),
            pltpu.VMEM((owners * rows // 2, span), BF16),
        ],
        compiler_params=params(24),
        cost_estimate=pl.CostEstimate(
            flops=16 * owners * rows * span * width, bytes_accessed=2 * owners * span * width, transcendentals=0
        ),
        name="look_in_blocks",
    )(place, ask, pool)


def gather_body(row_ref, answer_ref, q_ref, new_ref, out_ref, level_ref, top_ref, sum_ref, acc_ref, flat_ref):
    holders = answer_ref.shape[0]
    rows, lists = q_ref.shape[0], q_ref.shape[1]
    heads = lists // 2
    lane = lax.broadcasted_iota(jnp.int32, (lists, HEAD_SIZE), 1)
    later = lax.broadcasted_iota(jnp.int32, (lists, HEAD_SIZE), 0) >= heads
    own = []
    for r in range(rows):
        q = q_ref[r].astype(F32)
        new = new_ref[r].astype(F32)
        scores = []
        for t in range(2):
            s = jnp.sum(q * new[2 * t : 2 * t + 1, :], axis=1, keepdims=True) * SCALE
            scores.append(jnp.broadcast_to(s, (lists, HEAD_SIZE)))
        scores[1] = jnp.where(later, scores[1], LOWEST)
        top_ref[r] = jnp.maximum(scores[0], scores[1])
        own.append((scores, new))
    for d in range(holders):
        stat = answer_ref[d, lists:, :].astype(F32)
        level = jnp.sum(jnp.where(lane < 3, stat, 0.0), axis=1, keepdims=True)
        level_ref[d] = jnp.broadcast_to(level, (lists, HEAD_SIZE))
    for d in range(holders):
        r = row_ref[d]
        top_ref[r] = jnp.maximum(top_ref[r], level_ref[d])
    for r in range(rows):
        scores, new = own[r]
        first = jnp.exp2(scores[0] - top_ref[r])
        second = jnp.exp2(scores[1] - top_ref[r])
        sum_ref[r] = first + second
        acc_ref[r] = first * new[1:2, :] + second * new[3:4, :]
    for d in range(holders):
        r = row_ref[d]
        weight = jnp.exp2(level_ref[d] - top_ref[r])
        sum_ref[r] = sum_ref[r] + weight
        acc_ref[r] = acc_ref[r] + weight * answer_ref[d, :lists, :].astype(F32)
    for r in range(rows):
        o = acc_ref[r] / sum_ref[r]
        for t in range(2):
            for h in range(heads):
                flat_ref[2 * r + t : 2 * r + t + 1, h * HEAD_SIZE : (h + 1) * HEAD_SIZE] = o[
                    t * heads + h : t * heads + h + 1, :
                ]
    out_ref[...] = flat_ref[...].astype(BF16)


def gather_answers(row_of, answer, q, new):
    rows, lists, width = q.shape
    holders = answer.shape[0]
    heads = lists // 2
    state = pltpu.VMEM((rows, lists, width), F32)
    return pl.pallas_call(
        gather_body,
        out_shape=jax.ShapeDtypeStruct((2 * rows, heads * width), BF16),
        in_specs=[SMEM, VMEM, VMEM, VMEM],
        out_specs=VMEM,
        scratch_shapes=[
            pltpu.VMEM((holders, lists, width), F32),
            state,
            state,
            state,
            pltpu.VMEM((2 * rows, heads * width), F32),
        ],
        compiler_params=params(16),
        name="gather_answers",
    )(row_of, answer, q, new)


def shards(
    q_stretch,
    stretch_key_value,
    context_key_value,
    dec_q,
    dec_new,
    pool_key_value,
    block_table,
    cache_len,
    w_out,
):
    me = lax.axis_index(CTX)
    z = lax.axis_index("z")
    cycle = lax.axis_size(CTX)
    stretch = q_stretch.shape[0]
    rows_dev, nblk = dec_q.shape[0], block_table.shape[1]
    pool_dev, block_size = pool_key_value.shape[:2]

    def after(x, *others):
        return lax.optimization_barrier((x, *others))[0]

    def swap(x, name):
        return lax.ppermute(x, name, [(0, 1), (1, 0)])

    def turn(x, step):
        return lax.ppermute(x, "z", [(n, (n + step) % Z_CHIPS) for n in range(Z_CHIPS)])

    kv = split_keys_values(
        context_key_value.reshape(-1, HEAD_SIZE), stretch_key_value.reshape(-1, HEAD_SIZE)
    )
    kv_core, kv_y = swap(kv, "core"), swap(kv, "y")
    right, left = [q_stretch, turn(q_stretch, 1)], [q_stretch, turn(q_stretch, -1)]

    first = after(me.reshape(1).astype(jnp.int32), kv, right[1], left[1])
    ask, row_of, q_rows = question(first, block_table.T, cache_len, dec_q, cycle)
    ask = lax.all_to_all(ask, CTX, split_axis=0, concat_axis=0, tiled=True)
    table = block_table.reshape(cycle, rows_dev * nblk)
    place = jnp.sum(jnp.where(table // pool_dev == me, table % pool_dev, 0), axis=1)
    for n in (1, 2):
        right.append(turn(right[n], 1))
        left.append(turn(left[n], -1))
    ask = after(ask, right[3], left[3])
    look_out = look(place, ask, pool_key_value.reshape(pool_dev, 2 * block_size, HEAD_SIZE))
    answer = lax.all_to_all(look_out, CTX, split_axis=0, concat_axis=0, tiled=True)
    right.append(turn(after(right[3], look_out), 1))
    kv_yc = swap(after(kv_y, look_out), "core")
    keys, values = stack([kv, kv_core, kv_y, kv_yc])

    shifts = jnp.arange(Z_CHIPS, dtype=jnp.int32)
    corners = jnp.arange(2 * CORES, dtype=jnp.int32)
    corners = me ^ (corners // CORES * CORES * Z_CHIPS + corners % CORES)
    askers = me + ((z - shifts + Z_CHIPS) % Z_CHIPS - z) * CORES
    deltas = (askers[:, None] - corners[None, :]) * stretch

    def go(shift, previous, part=None):
        queries = right[shift] if shift >= 0 else left[-shift]
        return attend(shift % Z_CHIPS, after(deltas, previous), queries, keys, values, part)

    out = go(-3, values)
    from_left = turn(out, 1)
    out = go(4, out)
    from_right = turn(out, -1)

    attn = gather_answers(row_of, after(answer, out), q_rows, dec_new.reshape(rows_dev, 4, HEAD_SIZE))
    everyone = lax.all_to_all(
        jnp.broadcast_to(attn[None], (cycle, *attn.shape)), CTX, split_axis=0, concat_axis=0, tiled=True
    )
    out = go(-2, attn, from_left)
    from_left = turn(out, 1)
    out = go(3, out, from_right)
    from_right = turn(out, -1)
    out = go(-1, out, from_left)
    from_left = turn(out, 1)
    out = go(2, out, from_right)
    from_right = turn(out, -1)
    partial_out = jnp.dot(
        after(everyone, out).reshape(-1, attn.shape[1]), w_out, preferred_element_type=F32
    ).astype(BF16)
    shares = lax.axis_size(("grp", "tp"))
    pieces = lax.all_to_all(
        partial_out.reshape(shares, -1, partial_out.shape[1]), ("grp", "tp"), split_axis=0, concat_axis=0, tiled=True
    )
    out = go(1, partial_out, from_right)
    from_right = turn(out, -1)
    own = go(0, out)
    pre_out = merge([own, from_right, from_left], stretch)
    dec_out = jnp.sum(pieces.astype(F32), axis=0).astype(BF16)
    return (pre_out, dec_out.reshape(-1, 2, dec_out.shape[1]))


def solution(mesh):
    shape = mesh.devices.shape
    fine = jax.sharding.Mesh(mesh.devices.reshape(-1, Z_CHIPS, CORES, *shape[1:]), (*CTX, *mesh.axis_names[1:]))
    placed = (
        P(CTX, ("grp", "tp")),
        P(CTX, None, ("grp", "tp")),
        P(CTX, None, ("grp", "tp")),
        P(CTX, None, ("grp", "tp")),
        P(CTX, None, None, ("grp", "tp")),
        P(CTX, None, None, ("grp", "tp")),
        P(),
        P(CTX),
        P(("grp", "tp"), CTX),
    )
    return jax.shard_map(
        shards,
        mesh=fine,
        in_specs=placed,
        out_specs=(P(CTX, ("grp", "tp")), P(("grp", "tp"), None, CTX)),
        check_vma=False,
    )
```

```python
import functools
import math

import jax
import jax.numpy as jnp
from jax import lax
from jax.experimental import pallas as pl
from jax.experimental.pallas import tpu as pltpu
from jax.sharding import PartitionSpec as P

HEAD_SIZE = 128
CORES = 2
Z_CHIPS = 8
CONTEXT_DEV = 1280
BLOCK = 128
CTX = ("y", "z", "core")
SCALE = math.log2(math.e) / math.sqrt(HEAD_SIZE)
LOWEST = -1e30
F32 = jnp.float32
BF16 = jnp.bfloat16
VMEM = pl.BlockSpec(memory_space=pltpu.VMEM)
SMEM = pl.BlockSpec(memory_space=pltpu.SMEM)
HBM = pl.BlockSpec(memory_space=pltpu.HBM)


def params(mib):
    return pltpu.CompilerParams(vmem_limit_bytes=mib * 1024 * 1024)


def in_hbm(x):
    return pltpu.with_memory_space_constraint(x, pltpu.HBM)


def dot_nt(a, b):
    return lax.dot_general(a, b, (((1,), (1,)), ((), ())), preferred_element_type=F32)


def dot_nn(a, b):
    return lax.dot_general(a, b, (((1,), (0,)), ((), ())), preferred_element_type=F32)


def split_body(context_hbm, stretch_hbm, kv_ref, context_ref, stretch_ref, sem):
    copies = []
    total = context_ref.shape[0]
    step = total // 5
    for n in range(5):
        rows = pl.ds(n * step, step)
        copies.append(pltpu.make_async_copy(context_hbm.at[rows], context_ref.at[rows], sem.at[n]))
    copies.append(pltpu.make_async_copy(stretch_hbm, stretch_ref, sem.at[5]))
    for copy in copies:
        copy.start()

    def split(rows, at):
        count = rows.shape[0]
        half = count // 2
        i = lax.broadcasted_iota(jnp.int32, (count, count), 0)
        j = lax.broadcasted_iota(jnp.int32, (count, count), 1)
        source = jnp.where(i < half, 2 * i, 2 * (i - half) + 1)
        pick = jnp.where(j == source, 1.0, 0.0).astype(BF16)
        parted = dot_nn(pick, rows).astype(BF16)
        kv_ref[0, at : at + half, :] = parted[:half]
        kv_ref[1, at : at + half, :] = parted[half:]

    for n in range(5):
        copies[n].wait()
        for start in range(n * step, (n + 1) * step, 256):
            split(context_ref[start : start + 256, :], start // 2)
    copies[5].wait()
    split(stretch_ref[...], total // 2)


def split_keys_values(context, stretch):
    rows = (context.shape[0] + stretch.shape[0]) // 2
    return pl.pallas_call(
        split_body,
        out_shape=jax.ShapeDtypeStruct((2, rows, HEAD_SIZE), BF16),
        in_specs=[HBM, HBM],
        out_specs=VMEM,
        scratch_shapes=[
            pltpu.VMEM(context.shape, BF16),
            pltpu.VMEM(stretch.shape, BF16),
            pltpu.SemaphoreType.DMA((6,)),
        ],
        compiler_params=params(16),
        name="split_keys_values",
    )(in_hbm(context), in_hbm(stretch))


def question_body(
    me_ref, table_hbm, length_ref, q_hbm, ask_ref, row_ref, rows_ref, list_ref, table_ref, q_ref, sem
):
    copies = [
        pltpu.make_async_copy(q_hbm, q_ref, sem.at[0]),
        pltpu.make_async_copy(table_hbm, table_ref, sem.at[1]),
    ]
    for copy in copies:
        copy.start()
    rows_dev = length_ref.shape[0]
    nblk = table_ref.shape[0]
    lists = ask_ref.shape[1] // 2
    heads = lists // 2
    pool_dev = ask_ref.shape[0]
    copies[0].wait()
    for r in range(rows_dev):
        q = q_ref[r].astype(F32)
        for t in range(2):
            for h in range(heads):
                at = t * heads + h
                list_ref[r, at : at + 1, :] = q[t : t + 1, h * HEAD_SIZE : (h + 1) * HEAD_SIZE]
    copies[1].wait()
    for r in range(rows_dev):
        asked = list_ref[r].astype(BF16)
        rows_ref[r] = asked
        for n in range(nblk):
            holder = table_ref[n, me_ref[0] * rows_dev + r] // pool_dev
            left = jnp.clip(length_ref[r] - n * BLOCK, 0, BLOCK).astype(F32)
            ask_ref[holder, :lists, :] = asked
            ask_ref[holder, lists:, :] = jnp.full((lists, HEAD_SIZE), left, F32).astype(BF16)
            row_ref[holder] = r


def question(me, table, length, q, holders):
    rows_dev = length.shape[0]
    lists = 2 * q.shape[2] // HEAD_SIZE
    return pl.pallas_call(
        question_body,
        out_shape=[
            jax.ShapeDtypeStruct((holders, 2 * lists, HEAD_SIZE), BF16),
            jax.ShapeDtypeStruct((holders,), jnp.int32),
            jax.ShapeDtypeStruct((rows_dev, lists, HEAD_SIZE), BF16),
        ],
        in_specs=[SMEM, HBM, SMEM, HBM],
        out_specs=[VMEM, SMEM, VMEM],
        scratch_shapes=[
            pltpu.VMEM((rows_dev, lists, HEAD_SIZE), F32),
            pltpu.SMEM(table.shape, jnp.int32),
            pltpu.VMEM(q.shape, BF16),
            pltpu.SemaphoreType.DMA((2,)),
        ],
        compiler_params=params(16),
        name="question",
    )(me, in_hbm(table), length, in_hbm(q))


def stack_body(*refs):
    kv_refs, k_ref, v_ref = refs[:-2], refs[-2], refs[-1]
    sets = len(kv_refs)
    stretch = v_ref.shape[0] // sets - CONTEXT_DEV
    one = jnp.where(diagonal(), 1.0, 0.0).astype(BF16)
    for n, ref in enumerate(kv_refs):
        first, last = n * CONTEXT_DEV, sets * CONTEXT_DEV + n * stretch
        for at in range(0, CONTEXT_DEV, 256):
            k_ref[:, first + at : first + at + 256] = dot_nt(one, ref[0, at : at + 256, :]).astype(BF16)
        v_ref[first : first + CONTEXT_DEV, :] = ref[1, :CONTEXT_DEV, :]
        v_ref[last : last + stretch, :] = ref[1, CONTEXT_DEV:, :]
    k = jnp.concatenate([ref[0, CONTEXT_DEV:, :] for ref in kv_refs], axis=0)
    k_ref[:, sets * CONTEXT_DEV :] = dot_nt(one, k).astype(BF16)


def stack(sets):
    keys = len(sets) * sets[0].shape[1]
    return pl.pallas_call(
        stack_body,
        out_shape=[
            jax.ShapeDtypeStruct((HEAD_SIZE, keys), BF16),
            jax.ShapeDtypeStruct((keys, HEAD_SIZE), BF16),
        ],
        in_specs=[VMEM] * len(sets),
        out_specs=[VMEM, VMEM],
        compiler_params=params(16),
        name="stack",
    )(*sets)


def diagonal():
    i = lax.broadcasted_iota(jnp.int32, (HEAD_SIZE, HEAD_SIZE), 0)
    j = lax.broadcasted_iota(jnp.int32, (HEAD_SIZE, HEAD_SIZE), 1)
    return i == j


def read_part(ref, stretch):
    width = ref.shape[1]
    rows = width // HEAD_SIZE * stretch
    outputs = jnp.concatenate([ref[:stretch, c : c + HEAD_SIZE] for c in range(0, width, HEAD_SIZE)], axis=0)
    stat = ref[stretch : stretch + 16, :rows].astype(F32)
    level = stat[0:1] + stat[1:2] + stat[2:3]
    columns = []
    for g in range(0, rows, HEAD_SIZE):
        column = jnp.sum(jnp.where(diagonal(), level[:, g : g + HEAD_SIZE], 0.0), axis=1, keepdims=True)
        columns.append(jnp.broadcast_to(column, (HEAD_SIZE, HEAD_SIZE)))
    return outputs.astype(F32), jnp.concatenate(columns, axis=0)


def join(outputs, levels):
    top = functools.reduce(jnp.maximum, levels)
    weights = [jnp.exp2(level - top) for level in levels]
    total = functools.reduce(jnp.add, weights)
    mixed = functools.reduce(jnp.add, [weight * output for weight, output in zip(weights, outputs)])
    return mixed / total, top + jnp.log2(total)


def write_outputs(ref, outputs, stretch):
    outputs = outputs.astype(BF16)
    for h in range(outputs.shape[0] // stretch):
        ref[:stretch, h * HEAD_SIZE : (h + 1) * HEAD_SIZE] = outputs[h * stretch : (h + 1) * stretch]


def write_level(ref, level, stretch):
    rows = level.shape[0]
    lines = []
    for g in range(0, rows, HEAD_SIZE):
        lines.append(jnp.sum(jnp.where(diagonal(), level[g : g + HEAD_SIZE], 0.0), axis=0, keepdims=True))
    level = jnp.concatenate(lines, axis=1)
    high = level.astype(BF16).astype(F32)
    rest = level - high
    middle = rest.astype(BF16).astype(F32)
    row = lax.broadcasted_iota(jnp.int32, (16, rows), 0)
    stat = jnp.where(row == 0, high, jnp.where(row == 1, middle, jnp.where(row == 2, rest - middle, 0.0)))
    ref[stretch : stretch + 16, :rows] = stat.astype(BF16)
    ref[stretch : stretch + 16, rows:] = jnp.zeros((16, ref.shape[1] - rows), BF16)


def attend_body(which, arrived, delta_ref, q_ref, k_ref, v_ref, *refs):
    refs = list(refs)
    part_ref = refs.pop(0) if arrived else None
    out_ref, p_ref, total_ref, sum_ref, top_ref = refs
    stretch, width = q_ref.shape
    sets = delta_ref.shape[1]
    keys = v_ref.shape[0]
    rows = width // HEAD_SIZE * stretch
    chunk = 256
    span = CONTEXT_DEV
    q = jnp.concatenate([q_ref[:, c : c + HEAD_SIZE] for c in range(0, width, HEAD_SIZE)], axis=0)

    def score(k, masked):
        s = dot_nn(q, k)
        if masked:
            row = lax.rem(lax.broadcasted_iota(jnp.int32, s.shape, 0), stretch)
            col = lax.broadcasted_iota(jnp.int32, s.shape, 1)
            bound = delta_ref[which, sets - 1] + (sets - 1) * stretch - col
            for m in reversed(range(sets - 1)):
                bound = jnp.where(col < (m + 1) * stretch, delta_ref[which, m] + m * stretch - col, bound)
            s = jnp.where(row + bound >= 0, s, LOWEST)
        return s

    def highest(s):
        parts = [s[:, c : c + HEAD_SIZE] for c in range(0, s.shape[1], HEAD_SIZE)]
        return functools.reduce(jnp.maximum, parts)

    def spread(top):
        return jnp.broadcast_to(jnp.max(top, axis=1, keepdims=True), (rows, HEAD_SIZE)) * SCALE

    def weigh(s, top):
        parts = [jnp.exp2(s[:, c : c + HEAD_SIZE] * SCALE - top) for c in range(0, s.shape[1], HEAD_SIZE)]
        return jnp.concatenate(parts, axis=1).astype(BF16), functools.reduce(jnp.add, parts)

    top = spread(highest(score(k_ref[:, :chunk], False)))
    total, weight = None, None
    begun = 0
    for at in range(0, keys, chunk):
        p_ref[:, at : at + chunk], part = weigh(score(k_ref[:, at : at + chunk], at >= sets * CONTEXT_DEV), top)
        weight = part if weight is None else weight + part
        done = at + chunk
        if done - begun >= span and keys - done >= chunk * 2 or done == keys:
            part = dot_nn(p_ref[:, begun:done], v_ref[begun:done, :])
            total = part if total is None else total + part
            begun = done
    total_ref[...] = total
    sum_ref[...] = weight
    top_ref[...] = top

    @pl.when(jnp.logical_not(jnp.max(weight) < 1e35))
    def again():
        last = score(k_ref[:, keys - chunk :], True)

        def climb(n, top):
            k = k_ref[:, pl.ds(pl.multiple_of(n * chunk, chunk), chunk)]
            return jnp.maximum(top, highest(score(k, False)))

        count = (keys - chunk) // chunk
        top_ref[...] = spread(lax.fori_loop(0, count, climb, highest(last)))
        p, part = weigh(last, top_ref[...])
        sum_ref[...] = part
        total_ref[...] = dot_nn(p, v_ref[keys - chunk :, :])

        def add(n, carry):
            at = pl.ds(pl.multiple_of(n * chunk, chunk), chunk)
            p, part = weigh(score(k_ref[:, at], False), top_ref[...])
            sum_ref[...] += part
            total_ref[...] += dot_nn(p, v_ref[at, :])
            return carry

        lax.fori_loop(0, count, add, 0)

    weight = jnp.broadcast_to(jnp.sum(sum_ref[...], axis=1, keepdims=True), (rows, HEAD_SIZE))
    output, level = total_ref[...] / weight, top_ref[...] + jnp.log2(weight)
    if arrived:
        other, other_level = read_part(part_ref, stretch)
        output, level = join([output, other], [level, other_level])
    write_outputs(out_ref, output, stretch)
    write_level(out_ref, level, stretch)


def attend(which, deltas, queries, keys, values, part=None):
    stretch, width = queries.shape
    rows = width // HEAD_SIZE * stretch
    count = values.shape[0]
    operands = [deltas, queries, keys, values] + ([] if part is None else [part])
    return pl.pallas_call(
        functools.partial(attend_body, which, part is not None),
        out_shape=jax.ShapeDtypeStruct((stretch + 16, width), BF16),
        in_specs=[SMEM] + [VMEM] * (len(operands) - 1),
        out_specs=VMEM,
        scratch_shapes=[
            pltpu.VMEM((rows, count), BF16),
            pltpu.VMEM((rows, HEAD_SIZE), F32),
            pltpu.VMEM((rows, HEAD_SIZE), F32),
            pltpu.VMEM((rows, HEAD_SIZE), F32),
        ],
        compiler_params=params(32),
        cost_estimate=pl.CostEstimate(
            flops=8 * rows * count * HEAD_SIZE,
            bytes_accessed=4 * count * HEAD_SIZE,
            transcendentals=rows * count,
        ),
        name="attend",
    )(*operands)


def merge_body(*refs):
    part_refs, out_ref = refs[:-1], refs[-1]
    stretch = out_ref.shape[0]
    read = [read_part(ref, stretch) for ref in part_refs]
    output, _ = join([x for x, _ in read], [x for _, x in read])
    write_outputs(out_ref, output, stretch)


def merge(parts, stretch):
    return pl.pallas_call(
        merge_body,
        out_shape=jax.ShapeDtypeStruct((stretch, parts[0].shape[1]), BF16),
        in_specs=[VMEM] * len(parts),
        out_specs=VMEM,
        compiler_params=params(16),
        name="merge",
    )(*parts)


def look_body(place_ref, ask_ref, pool_hbm, out_ref, s_ref, p_ref, pool_ref, sem):
    owners = ask_ref.shape[0]
    copies = []
    for d in range(owners):
        copies.append(pltpu.make_async_copy(pool_hbm.at[place_ref[d]], pool_ref.at[d], sem.at[d]))
        copies[d].start()
    half = ask_ref.shape[1] // 2
    span = pool_ref.shape[1]
    for d in range(owners):
        copies[d].wait()
        s_ref[d * half : (d + 1) * half, :] = dot_nt(ask_ref[d, :half, :], pool_ref[d])
    col = lax.broadcasted_iota(jnp.int32, (half, span), 1)
    lane = lax.broadcasted_iota(jnp.int32, (half, HEAD_SIZE), 1)
    even = (col & 1) == 0
    for d in range(owners):
        limit = ask_ref[d, half:, :].astype(F32) * 2.0
        limit = jnp.concatenate([limit] * (span // HEAD_SIZE), axis=1)
        allowed = even & (col.astype(F32) < limit)
        s = jnp.where(allowed, s_ref[d * half : (d + 1) * half, :], LOWEST)
        top = jnp.max(s, axis=1, keepdims=True)
        p = jnp.where(allowed, jnp.exp2((s - top) * SCALE), 0.0)
        total = jnp.sum(p, axis=1, keepdims=True)
        p_ref[d * half : (d + 1) * half, :] = pltpu.roll(p, 1, 1).astype(BF16)
        seen = total > 0.0
        level = jnp.where(seen, top * SCALE + jnp.log2(jnp.where(seen, total, 1.0)), LOWEST)
        level = jnp.broadcast_to(level, (half, HEAD_SIZE))
        high = level.astype(BF16).astype(F32)
        rest = level - high
        middle = rest.astype(BF16).astype(F32)
        low = rest - middle
        stat = jnp.where(lane == 0, high, jnp.where(lane == 1, middle, jnp.where(lane == 2, low, 0.0)))
        out_ref[d, half:, :] = stat.astype(BF16)
        s_ref[d * half : (d + 1) * half, :HEAD_SIZE] = jnp.broadcast_to(
            jnp.where(seen, 1.0 / jnp.where(seen, total, 1.0), 0.0), (half, HEAD_SIZE)
        )
    for d in range(owners):
        o = dot_nn(p_ref[d * half : (d + 1) * half, :], pool_ref[d])
        out_ref[d, :half, :] = (o * s_ref[d * half : (d + 1) * half, :HEAD_SIZE]).astype(BF16)


def look(place, ask, pool):
    owners, rows, width = ask.shape
    span = pool.shape[1]
    return pl.pallas_call(
        look_body,
        out_shape=jax.ShapeDtypeStruct(ask.shape, BF16),
        in_specs=[SMEM, VMEM, HBM],
        out_specs=VMEM,
        scratch_shapes=[
            pltpu.VMEM((owners * rows // 2, span), F32),
            pltpu.VMEM((owners * rows // 2, span), BF16),
            pltpu.VMEM(pool.shape, BF16),
            pltpu.SemaphoreType.DMA((owners,)),
        ],
        compiler_params=params(24),
        cost_estimate=pl.CostEstimate(
            flops=16 * owners * rows * span * width, bytes_accessed=2 * owners * span * width, transcendentals=0
        ),
        name="look_in_blocks",
    )(place, ask, in_hbm(pool))


def gather_body(row_ref, answer_ref, q_ref, new_ref, out_ref, level_ref, top_ref, sum_ref, acc_ref, flat_ref):
    holders = answer_ref.shape[0]
    rows, lists = q_ref.shape[0], q_ref.shape[1]
    heads = lists // 2
    lane = lax.broadcasted_iota(jnp.int32, (lists, HEAD_SIZE), 1)
    later = lax.broadcasted_iota(jnp.int32, (lists, HEAD_SIZE), 0) >= heads
    own = []
    for r in range(rows):
        q = q_ref[r].astype(F32)
        new = new_ref[r].astype(F32)
        scores = []
        for t in range(2):
            s = jnp.sum(q * new[2 * t : 2 * t + 1, :], axis=1, keepdims=True) * SCALE
            scores.append(jnp.broadcast_to(s, (lists, HEAD_SIZE)))
        scores[1] = jnp.where(later, scores[1], LOWEST)
        top_ref[r] = jnp.maximum(scores[0], scores[1])
        own.append((scores, new))
    for d in range(holders):
        stat = answer_ref[d, lists:, :].astype(F32)
        level = jnp.sum(jnp.where(lane < 3, stat, 0.0), axis=1, keepdims=True)
        level_ref[d] = jnp.broadcast_to(level, (lists, HEAD_SIZE))
    for d in range(holders):
        r = row_ref[d]
        top_ref[r] = jnp.maximum(top_ref[r], level_ref[d])
    for r in range(rows):
        scores, new = own[r]
        first = jnp.exp2(scores[0] - top_ref[r])
        second = jnp.exp2(scores[1] - top_ref[r])
        sum_ref[r] = first + second
        acc_ref[r] = first * new[1:2, :] + second * new[3:4, :]
    for d in range(holders):
        r = row_ref[d]
        weight = jnp.exp2(level_ref[d] - top_ref[r])
        sum_ref[r] = sum_ref[r] + weight
        acc_ref[r] = acc_ref[r] + weight * answer_ref[d, :lists, :].astype(F32)
    for r in range(rows):
        o = acc_ref[r] / sum_ref[r]
        for t in range(2):
            for h in range(heads):
                flat_ref[2 * r + t : 2 * r + t + 1, h * HEAD_SIZE : (h + 1) * HEAD_SIZE] = o[
                    t * heads + h : t * heads + h + 1, :
                ]
    flat = flat_ref[...].astype(BF16)
    for d in range(holders):
        out_ref[d] = flat


def gather_answers(row_of, answer, q, new):
    rows, lists, width = q.shape
    holders = answer.shape[0]
    heads = lists // 2
    state = pltpu.VMEM((rows, lists, width), F32)
    return pl.pallas_call(
        gather_body,
        out_shape=jax.ShapeDtypeStruct((holders, 2 * rows, heads * width), BF16),
        in_specs=[SMEM, VMEM, VMEM, VMEM],
        out_specs=VMEM,
        scratch_shapes=[
            pltpu.VMEM((holders, lists, width), F32),
            state,
            state,
            state,
            pltpu.VMEM((2 * rows, heads * width), F32),
        ],
        compiler_params=params(16),
        name="gather_answers",
    )(row_of, answer, q, new)


def project_body(rows_ref, w_ref, out_ref):
    out_ref[...] = dot_nn(rows_ref[...], w_ref[...]).astype(BF16)


def project(rows, w):
    return pl.pallas_call(
        project_body,
        out_shape=jax.ShapeDtypeStruct((rows.shape[0], w.shape[1]), BF16),
        in_specs=[VMEM, VMEM],
        out_specs=VMEM,
        compiler_params=params(16),
        name="project",
    )(rows, w)


def shards(
    q_stretch,
    stretch_key_value,
    context_key_value,
    dec_q,
    dec_new,
    pool_key_value,
    block_table,
    cache_len,
    w_out,
):
    me = lax.axis_index(CTX)
    z = lax.axis_index("z")
    cycle = lax.axis_size(CTX)
    stretch = q_stretch.shape[0]
    rows_dev, nblk = dec_q.shape[0], block_table.shape[1]
    pool_dev, block_size = pool_key_value.shape[:2]

    def after(x, *others):
        return lax.optimization_barrier((x, *others))[0]

    def swap(x, name):
        return lax.ppermute(x, name, [(0, 1), (1, 0)])

    def turn(x, step):
        return lax.ppermute(x, "z", [(n, (n + step) % Z_CHIPS) for n in range(Z_CHIPS)])

    kv = split_keys_values(
        context_key_value.reshape(-1, HEAD_SIZE), stretch_key_value.reshape(-1, HEAD_SIZE)
    )
    kv_core, kv_y = swap(kv, "core"), swap(kv, "y")
    right = [q_stretch, turn(q_stretch, 1), turn(q_stretch, 2)]
    left = [q_stretch, turn(q_stretch, -1), turn(q_stretch, -2)]

    first = after(me.reshape(1).astype(jnp.int32), kv, right[1], left[1], right[2], left[2])
    ask, row_of, q_rows = question(first, block_table.T, cache_len, dec_q, cycle)
    ask = lax.all_to_all(ask, CTX, split_axis=0, concat_axis=0, tiled=True)
    table = block_table.reshape(cycle, rows_dev * nblk)
    place = jnp.sum(jnp.where(table // pool_dev == me, table % pool_dev, 0), axis=1)
    right += [turn(right[1], 2), turn(right[2], 2)]
    left.append(turn(left[1], -2))
    kv_yc = swap(after(kv_y, right[3]), "core")
    ask = after(ask, right[3], left[3])
    look_out = look(place, ask, pool_key_value.reshape(pool_dev, 2 * block_size, HEAD_SIZE))
    answer = lax.all_to_all(look_out, CTX, split_axis=0, concat_axis=0, tiled=True)
    keys, values = stack([kv, kv_core, kv_y, kv_yc])

    shifts = jnp.arange(Z_CHIPS, dtype=jnp.int32)
    corners = jnp.arange(2 * CORES, dtype=jnp.int32)
    corners = me ^ (corners // CORES * CORES * Z_CHIPS + corners % CORES)
    askers = me + ((z - shifts + Z_CHIPS) % Z_CHIPS - z) * CORES
    deltas = (askers[:, None] - corners[None, :]) * stretch

    def go(shift, previous, part=None):
        queries = right[shift] if shift >= 0 else left[-shift]
        return attend(shift % Z_CHIPS, after(deltas, previous), queries, keys, values, part)

    out = go(-3, values)
    from_left = turn(out, 1)
    out = go(4, out)
    from_right = turn(out, -1)

    attn = gather_answers(row_of, after(answer, out), q_rows, dec_new.reshape(rows_dev, 4, HEAD_SIZE))
    everyone = lax.all_to_all(attn, CTX, split_axis=0, concat_axis=0, tiled=True)
    out = go(-2, attn, from_left)
    from_left = turn(out, 1)
    out = go(3, out, from_right)
    from_right = turn(out, -1)
    out = go(-1, out, from_left)
    from_left = turn(out, 1)
    out = go(2, out, from_right)
    from_right = turn(out, -1)
    own = go(0, out)
    out = go(1, own, from_right)
    from_right = turn(out, -1)
    partial_out = project(after(everyone, out).reshape(-1, everyone.shape[2]), w_out)
    shares = lax.axis_size(("grp", "tp"))
    pieces = lax.all_to_all(
        partial_out.reshape(shares, -1, partial_out.shape[1]), ("grp", "tp"), split_axis=0, concat_axis=0, tiled=True
    )
    pre_out = merge([own, from_right, from_left], stretch)
    dec_out = jnp.sum(pieces.astype(F32), axis=0).astype(BF16)
    return (pre_out, dec_out.reshape(-1, 2, dec_out.shape[1]))


def solution(mesh):
    shape = mesh.devices.shape
    fine = jax.sharding.Mesh(mesh.devices.reshape(-1, Z_CHIPS, CORES, *shape[1:]), (*CTX, *mesh.axis_names[1:]))
    placed = (
        P(CTX, ("grp", "tp")),
        P(CTX, None, ("grp", "tp")),
        P(CTX, None, ("grp", "tp")),
        P(CTX, None, ("grp", "tp")),
        P(CTX, None, None, ("grp", "tp")),
        P(CTX, None, None, ("grp", "tp")),
        P(),
        P(CTX),
        P(("grp", "tp"), CTX),
    )
    return jax.shard_map(
        shards,
        mesh=fine,
        in_specs=placed,
        out_specs=(P(CTX, ("grp", "tp")), P(("grp", "tp"), None, CTX)),
        check_vma=False,
    )
```

```python
import functools
import math

import jax
import jax.numpy as jnp
from jax import lax
from jax.experimental import pallas as pl
from jax.experimental.pallas import tpu as pltpu
from jax.sharding import PartitionSpec as P

HEAD_SIZE = 128
CORES = 2
Z_CHIPS = 8
CONTEXT_DEV = 1280
BLOCK = 128
CTX = ("y", "z", "core")
SCALE = math.log2(math.e) / math.sqrt(HEAD_SIZE)
LOWEST = -1e30
F32 = jnp.float32
BF16 = jnp.bfloat16
VMEM = pl.BlockSpec(memory_space=pltpu.VMEM)
SMEM = pl.BlockSpec(memory_space=pltpu.SMEM)
HBM = pl.BlockSpec(memory_space=pltpu.HBM)


def params(mib):
    return pltpu.CompilerParams(vmem_limit_bytes=mib * 1024 * 1024)


def in_hbm(x):
    return pltpu.with_memory_space_constraint(x, pltpu.HBM)


def dot_nt(a, b):
    return lax.dot_general(a, b, (((1,), (1,)), ((), ())), preferred_element_type=F32)


def dot_nn(a, b):
    return lax.dot_general(a, b, (((1,), (0,)), ((), ())), preferred_element_type=F32)


def split_body(context_hbm, stretch_hbm, kv_ref, context_ref, stretch_ref, sem):
    copies = []
    total = context_ref.shape[0]
    step = total // 5
    for n in range(5):
        rows = pl.ds(n * step, step)
        copies.append(pltpu.make_async_copy(context_hbm.at[rows], context_ref.at[rows], sem.at[n]))
    copies.append(pltpu.make_async_copy(stretch_hbm, stretch_ref, sem.at[5]))
    for copy in copies:
        copy.start()

    def split(rows, at):
        count = rows.shape[0]
        half = count // 2
        i = lax.broadcasted_iota(jnp.int32, (count, count), 0)
        j = lax.broadcasted_iota(jnp.int32, (count, count), 1)
        source = jnp.where(i < half, 2 * i, 2 * (i - half) + 1)
        pick = jnp.where(j == source, 1.0, 0.0).astype(BF16)
        parted = dot_nn(pick, rows).astype(BF16)
        kv_ref[0, at : at + half, :] = parted[:half]
        kv_ref[1, at : at + half, :] = parted[half:]

    for n in range(5):
        copies[n].wait()
        for start in range(n * step, (n + 1) * step, 256):
            split(context_ref[start : start + 256, :], start // 2)
    copies[5].wait()
    split(stretch_ref[...], total // 2)


def split_keys_values(context, stretch):
    rows = (context.shape[0] + stretch.shape[0]) // 2
    return pl.pallas_call(
        split_body,
        out_shape=jax.ShapeDtypeStruct((2, rows, HEAD_SIZE), BF16),
        in_specs=[HBM, HBM],
        out_specs=VMEM,
        scratch_shapes=[
            pltpu.VMEM(context.shape, BF16),
            pltpu.VMEM(stretch.shape, BF16),
            pltpu.SemaphoreType.DMA((6,)),
        ],
        compiler_params=params(16),
        name="split_keys_values",
    )(in_hbm(context), in_hbm(stretch))


def question_body(
    me_ref, table_hbm, length_ref, q_hbm, ask_ref, row_ref, rows_ref, list_ref, table_ref, q_ref, sem
):
    copies = [
        pltpu.make_async_copy(q_hbm, q_ref, sem.at[0]),
        pltpu.make_async_copy(table_hbm, table_ref, sem.at[1]),
    ]
    for copy in copies:
        copy.start()
    rows_dev = length_ref.shape[0]
    nblk = table_ref.shape[0]
    lists = ask_ref.shape[1] // 2
    heads = lists // 2
    pool_dev = ask_ref.shape[0]
    copies[0].wait()
    for r in range(rows_dev):
        q = q_ref[r].astype(F32)
        for t in range(2):
            for h in range(heads):
                at = t * heads + h
                list_ref[r, at : at + 1, :] = q[t : t + 1, h * HEAD_SIZE : (h + 1) * HEAD_SIZE]
    copies[1].wait()
    for r in range(rows_dev):
        asked = list_ref[r].astype(BF16)
        rows_ref[r] = asked
        for n in range(nblk):
            holder = table_ref[n, me_ref[0] * rows_dev + r] // pool_dev
            left = jnp.clip(length_ref[r] - n * BLOCK, 0, BLOCK).astype(F32)
            ask_ref[holder, :lists, :] = asked
            ask_ref[holder, lists:, :] = jnp.full((lists, HEAD_SIZE), left, F32).astype(BF16)
            row_ref[holder] = r


def question(me, table, length, q, holders):
    rows_dev = length.shape[0]
    lists = 2 * q.shape[2] // HEAD_SIZE
    return pl.pallas_call(
        question_body,
        out_shape=[
            jax.ShapeDtypeStruct((holders, 2 * lists, HEAD_SIZE), BF16),
            jax.ShapeDtypeStruct((holders,), jnp.int32),
            jax.ShapeDtypeStruct((rows_dev, lists, HEAD_SIZE), BF16),
        ],
        in_specs=[SMEM, HBM, SMEM, HBM],
        out_specs=[VMEM, SMEM, VMEM],
        scratch_shapes=[
            pltpu.VMEM((rows_dev, lists, HEAD_SIZE), F32),
            pltpu.SMEM(table.shape, jnp.int32),
            pltpu.VMEM(q.shape, BF16),
            pltpu.SemaphoreType.DMA((2,)),
        ],
        compiler_params=params(16),
        name="question",
    )(me, in_hbm(table), length, in_hbm(q))


def stack_body(*refs):
    kv_refs, k_ref, v_ref = refs[:-2], refs[-2], refs[-1]
    sets = len(kv_refs)
    stretch = v_ref.shape[0] // sets - CONTEXT_DEV
    one = jnp.where(diagonal(), 1.0, 0.0).astype(BF16)
    v_ref[:, HEAD_SIZE:] = jnp.ones((v_ref.shape[0], HEAD_SIZE), BF16)
    for n, ref in enumerate(kv_refs):
        first, last = n * CONTEXT_DEV, sets * CONTEXT_DEV + n * stretch
        for at in range(0, CONTEXT_DEV, 256):
            k_ref[:, first + at : first + at + 256] = dot_nt(one, ref[0, at : at + 256, :]).astype(BF16)
        v_ref[first : first + CONTEXT_DEV, :HEAD_SIZE] = ref[1, :CONTEXT_DEV, :]
        v_ref[last : last + stretch, :HEAD_SIZE] = ref[1, CONTEXT_DEV:, :]
    k = jnp.concatenate([ref[0, CONTEXT_DEV:, :] for ref in kv_refs], axis=0)
    k_ref[:, sets * CONTEXT_DEV :] = dot_nt(one, k).astype(BF16)


def stack(sets):
    keys = len(sets) * sets[0].shape[1]
    return pl.pallas_call(
        stack_body,
        out_shape=[
            jax.ShapeDtypeStruct((HEAD_SIZE, keys), BF16),
            jax.ShapeDtypeStruct((keys, 2 * HEAD_SIZE), BF16),
        ],
        in_specs=[VMEM] * len(sets),
        out_specs=[VMEM, VMEM],
        compiler_params=params(16),
        name="stack",
    )(*sets)


def diagonal():
    i = lax.broadcasted_iota(jnp.int32, (HEAD_SIZE, HEAD_SIZE), 0)
    j = lax.broadcasted_iota(jnp.int32, (HEAD_SIZE, HEAD_SIZE), 1)
    return i == j


def read_part(ref, stretch):
    width = ref.shape[1]
    rows = width // HEAD_SIZE * stretch
    outputs = jnp.concatenate([ref[:stretch, c : c + HEAD_SIZE] for c in range(0, width, HEAD_SIZE)], axis=0)
    stat = ref[stretch : stretch + 16, :rows].astype(F32)
    level = stat[0:1] + stat[1:2] + stat[2:3]
    columns = []
    for g in range(0, rows, HEAD_SIZE):
        column = jnp.sum(jnp.where(diagonal(), level[:, g : g + HEAD_SIZE], 0.0), axis=1, keepdims=True)
        columns.append(jnp.broadcast_to(column, (HEAD_SIZE, HEAD_SIZE)))
    return outputs.astype(F32), jnp.concatenate(columns, axis=0)


def join(outputs, levels):
    top = functools.reduce(jnp.maximum, levels)
    weights = [jnp.exp2(level - top) for level in levels]
    total = functools.reduce(jnp.add, weights)
    mixed = functools.reduce(jnp.add, [weight * output for weight, output in zip(weights, outputs)])
    return mixed / total, top + jnp.log2(total)


def write_outputs(ref, outputs, stretch):
    outputs = outputs.astype(BF16)
    for h in range(outputs.shape[0] // stretch):
        ref[:stretch, h * HEAD_SIZE : (h + 1) * HEAD_SIZE] = outputs[h * stretch : (h + 1) * stretch]


def write_level(ref, level, stretch):
    rows = level.shape[0]
    lines = []
    for g in range(0, rows, HEAD_SIZE):
        lines.append(jnp.sum(jnp.where(diagonal(), level[g : g + HEAD_SIZE], 0.0), axis=0, keepdims=True))
    level = jnp.concatenate(lines, axis=1)
    high = level.astype(BF16).astype(F32)
    rest = level - high
    middle = rest.astype(BF16).astype(F32)
    row = lax.broadcasted_iota(jnp.int32, (16, rows), 0)
    stat = jnp.where(row == 0, high, jnp.where(row == 1, middle, jnp.where(row == 2, rest - middle, 0.0)))
    ref[stretch : stretch + 16, :rows] = stat.astype(BF16)
    ref[stretch : stretch + 16, rows:] = jnp.zeros((16, ref.shape[1] - rows), BF16)


def attend_body(which, arrived, delta_ref, q_ref, k_ref, v_ref, *refs):
    refs = list(refs)
    part_ref = refs.pop(0) if arrived else None
    out_ref, p_ref, total_ref, top_ref = refs
    stretch, width = q_ref.shape
    sets = delta_ref.shape[1]
    keys = v_ref.shape[0]
    rows = width // HEAD_SIZE * stretch
    chunk = 256
    span = CONTEXT_DEV
    q = jnp.concatenate([q_ref[:, c : c + HEAD_SIZE] for c in range(0, width, HEAD_SIZE)], axis=0)

    def score(k, masked):
        s = dot_nn(q, k)
        if masked:
            row = lax.rem(lax.broadcasted_iota(jnp.int32, s.shape, 0), stretch)
            col = lax.broadcasted_iota(jnp.int32, s.shape, 1)
            bound = delta_ref[which, sets - 1] + (sets - 1) * stretch - col
            for m in reversed(range(sets - 1)):
                bound = jnp.where(col < (m + 1) * stretch, delta_ref[which, m] + m * stretch - col, bound)
            s = jnp.where(row + bound >= 0, s, LOWEST)
        return s

    def highest(s):
        parts = [s[:, c : c + HEAD_SIZE] for c in range(0, s.shape[1], HEAD_SIZE)]
        return functools.reduce(jnp.maximum, parts)

    def spread(top):
        return jnp.broadcast_to(jnp.max(top, axis=1, keepdims=True), (rows, HEAD_SIZE)) * SCALE

    def weigh(s, top):
        parts = [s[:, c : c + HEAD_SIZE] for c in range(0, s.shape[1], HEAD_SIZE)]
        return jnp.concatenate([jnp.exp2(part * SCALE - top) for part in parts], axis=1).astype(BF16)

    top = spread(highest(score(k_ref[:, :chunk], False)))
    total = None
    begun = 0
    for at in range(0, keys, chunk):
        p_ref[:, at : at + chunk] = weigh(score(k_ref[:, at : at + chunk], at >= sets * CONTEXT_DEV), top)
        done = at + chunk
        if done - begun >= span and keys - done >= chunk * 2 or done == keys:
            part = dot_nn(p_ref[:, begun:done], v_ref[begun:done, :])
            total = part if total is None else total + part
            begun = done
    total_ref[...] = total
    top_ref[...] = top

    @pl.when(jnp.logical_not(jnp.max(total[:, HEAD_SIZE:]) < 1e37))
    def again():
        last = score(k_ref[:, keys - chunk :], True)

        def climb(n, top):
            k = k_ref[:, pl.ds(pl.multiple_of(n * chunk, chunk), chunk)]
            return jnp.maximum(top, highest(score(k, False)))

        count = (keys - chunk) // chunk
        top_ref[...] = spread(lax.fori_loop(0, count, climb, highest(last)))
        total_ref[...] = dot_nn(weigh(last, top_ref[...]), v_ref[keys - chunk :, :])

        def add(n, carry):
            at = pl.ds(pl.multiple_of(n * chunk, chunk), chunk)
            total_ref[...] += dot_nn(weigh(score(k_ref[:, at], False), top_ref[...]), v_ref[at, :])
            return carry

        lax.fori_loop(0, count, add, 0)

    weight = total_ref[:, HEAD_SIZE:]
    output, level = total_ref[:, :HEAD_SIZE] / weight, top_ref[...] + jnp.log2(weight)
    if arrived:
        other, other_level = read_part(part_ref, stretch)
        output, level = join([output, other], [level, other_level])
    write_outputs(out_ref, output, stretch)
    write_level(out_ref, level, stretch)


def attend(which, deltas, queries, keys, values, part=None):
    stretch, width = queries.shape
    rows = width // HEAD_SIZE * stretch
    count = values.shape[0]
    operands = [deltas, queries, keys, values] + ([] if part is None else [part])
    return pl.pallas_call(
        functools.partial(attend_body, which, part is not None),
        out_shape=jax.ShapeDtypeStruct((stretch + 16, width), BF16),
        in_specs=[SMEM] + [VMEM] * (len(operands) - 1),
        out_specs=VMEM,
        scratch_shapes=[
            pltpu.VMEM((rows, count), BF16),
            pltpu.VMEM((rows, 2 * HEAD_SIZE), F32),
            pltpu.VMEM((rows, HEAD_SIZE), F32),
        ],
        compiler_params=params(32),
        cost_estimate=pl.CostEstimate(
            flops=8 * rows * count * HEAD_SIZE,
            bytes_accessed=4 * count * HEAD_SIZE,
            transcendentals=rows * count,
        ),
        name="attend",
    )(*operands)


def merge_body(*refs):
    part_refs, out_ref = refs[:-1], refs[-1]
    stretch = out_ref.shape[0]
    read = [read_part(ref, stretch) for ref in part_refs]
    output, _ = join([x for x, _ in read], [x for _, x in read])
    write_outputs(out_ref, output, stretch)


def merge(parts, stretch):
    return pl.pallas_call(
        merge_body,
        out_shape=jax.ShapeDtypeStruct((stretch, parts[0].shape[1]), BF16),
        in_specs=[VMEM] * len(parts),
        out_specs=VMEM,
        compiler_params=params(16),
        name="merge",
    )(*parts)


def look_body(place_ref, ask_ref, pool_hbm, out_ref, s_ref, p_ref, pool_ref, sem):
    owners = ask_ref.shape[0]
    copies = []
    step = owners // sem.shape[0]
    for n in range(sem.shape[0]):
        blocks = pl.ds(n * step, step)
        copies.append(pltpu.make_async_copy(pool_hbm.at[blocks], pool_ref.at[blocks], sem.at[n]))
        copies[n].start()
    for copy in copies:
        copy.wait()
    half = ask_ref.shape[1] // 2
    span = pool_ref.shape[1]
    for d in range(owners):
        s_ref[d * half : (d + 1) * half, :] = dot_nt(ask_ref[d, :half, :], pool_ref[place_ref[d]])
    col = lax.broadcasted_iota(jnp.int32, (half, span), 1)
    lane = lax.broadcasted_iota(jnp.int32, (half, HEAD_SIZE), 1)
    even = (col & 1) == 0
    for d in range(owners):
        limit = ask_ref[d, half:, :].astype(F32) * 2.0
        limit = jnp.concatenate([limit] * (span // HEAD_SIZE), axis=1)
        allowed = even & (col.astype(F32) < limit)
        s = jnp.where(allowed, s_ref[d * half : (d + 1) * half, :], LOWEST)
        top = jnp.max(s, axis=1, keepdims=True)
        p = jnp.where(allowed, jnp.exp2((s - top) * SCALE), 0.0)
        total = jnp.sum(p, axis=1, keepdims=True)
        p_ref[d * half : (d + 1) * half, :] = pltpu.roll(p, 1, 1).astype(BF16)
        seen = total > 0.0
        level = jnp.where(seen, top * SCALE + jnp.log2(jnp.where(seen, total, 1.0)), LOWEST)
        level = jnp.broadcast_to(level, (half, HEAD_SIZE))
        high = level.astype(BF16).astype(F32)
        rest = level - high
        middle = rest.astype(BF16).astype(F32)
        low = rest - middle
        stat = jnp.where(lane == 0, high, jnp.where(lane == 1, middle, jnp.where(lane == 2, low, 0.0)))
        out_ref[d, half:, :] = stat.astype(BF16)
        s_ref[d * half : (d + 1) * half, :HEAD_SIZE] = jnp.broadcast_to(
            jnp.where(seen, 1.0 / jnp.where(seen, total, 1.0), 0.0), (half, HEAD_SIZE)
        )
    for d in range(owners):
        o = dot_nn(p_ref[d * half : (d + 1) * half, :], pool_ref[place_ref[d]])
        out_ref[d, :half, :] = (o * s_ref[d * half : (d + 1) * half, :HEAD_SIZE]).astype(BF16)


def look(place, ask, pool):
    owners, rows, width = ask.shape
    span = pool.shape[1]
    return pl.pallas_call(
        look_body,
        out_shape=jax.ShapeDtypeStruct(ask.shape, BF16),
        in_specs=[SMEM, VMEM, HBM],
        out_specs=VMEM,
        scratch_shapes=[
            pltpu.VMEM((owners * rows // 2, span), F32),
            pltpu.VMEM((owners * rows // 2, span), BF16),
            pltpu.VMEM(pool.shape, BF16),
            pltpu.SemaphoreType.DMA((4,)),
        ],
        compiler_params=params(24),
        cost_estimate=pl.CostEstimate(
            flops=16 * owners * rows * span * width, bytes_accessed=2 * owners * span * width, transcendentals=0
        ),
        name="look_in_blocks",
    )(place, ask, in_hbm(pool))


def gather_body(row_ref, answer_ref, q_ref, new_ref, out_ref, level_ref, top_ref, sum_ref, acc_ref, flat_ref):
    holders = answer_ref.shape[0]
    rows, lists = q_ref.shape[0], q_ref.shape[1]
    heads = lists // 2
    lane = lax.broadcasted_iota(jnp.int32, (lists, HEAD_SIZE), 1)
    later = lax.broadcasted_iota(jnp.int32, (lists, HEAD_SIZE), 0) >= heads
    own = []
    for r in range(rows):
        q = q_ref[r].astype(F32)
        new = new_ref[r].astype(F32)
        scores = []
        for t in range(2):
            s = jnp.sum(q * new[2 * t : 2 * t + 1, :], axis=1, keepdims=True) * SCALE
            scores.append(jnp.broadcast_to(s, (lists, HEAD_SIZE)))
        scores[1] = jnp.where(later, scores[1], LOWEST)
        top_ref[r] = jnp.maximum(scores[0], scores[1])
        own.append((scores, new))
    for d in range(holders):
        stat = answer_ref[d, lists:, :].astype(F32)
        level = jnp.sum(jnp.where(lane < 3, stat, 0.0), axis=1, keepdims=True)
        level_ref[d] = jnp.broadcast_to(level, (lists, HEAD_SIZE))
    for d in range(holders):
        r = row_ref[d]
        top_ref[r] = jnp.maximum(top_ref[r], level_ref[d])
    for r in range(rows):
        scores, new = own[r]
        first = jnp.exp2(scores[0] - top_ref[r])
        second = jnp.exp2(scores[1] - top_ref[r])
        sum_ref[r] = first + second
        acc_ref[r] = first * new[1:2, :] + second * new[3:4, :]
    for d in range(holders):
        r = row_ref[d]
        weight = jnp.exp2(level_ref[d] - top_ref[r])
        sum_ref[r] = sum_ref[r] + weight
        acc_ref[r] = acc_ref[r] + weight * answer_ref[d, :lists, :].astype(F32)
    for r in range(rows):
        o = acc_ref[r] / sum_ref[r]
        for t in range(2):
            for h in range(heads):
                flat_ref[2 * r + t : 2 * r + t + 1, h * HEAD_SIZE : (h + 1) * HEAD_SIZE] = o[
                    t * heads + h : t * heads + h + 1, :
                ]
    flat = flat_ref[...].astype(BF16)
    for d in range(holders):
        out_ref[d] = flat


def gather_answers(row_of, answer, q, new):
    rows, lists, width = q.shape
    holders = answer.shape[0]
    heads = lists // 2
    state = pltpu.VMEM((rows, lists, width), F32)
    return pl.pallas_call(
        gather_body,
        out_shape=jax.ShapeDtypeStruct((holders, 2 * rows, heads * width), BF16),
        in_specs=[SMEM, VMEM, VMEM, VMEM],
        out_specs=VMEM,
        scratch_shapes=[
            pltpu.VMEM((holders, lists, width), F32),
            state,
            state,
            state,
            pltpu.VMEM((2 * rows, heads * width), F32),
        ],
        compiler_params=params(16),
        name="gather_answers",
    )(row_of, answer, q, new)


def project_body(rows_ref, w_ref, out_ref):
    out_ref[...] = dot_nn(rows_ref[...], w_ref[...]).astype(BF16)


def project(rows, w):
    return pl.pallas_call(
        project_body,
        out_shape=jax.ShapeDtypeStruct((rows.shape[0], w.shape[1]), BF16),
        in_specs=[VMEM, VMEM],
        out_specs=VMEM,
        compiler_params=params(16),
        name="project",
    )(rows, w)


def shards(
    q_stretch,
    stretch_key_value,
    context_key_value,
    dec_q,
    dec_new,
    pool_key_value,
    block_table,
    cache_len,
    w_out,
):
    me = lax.axis_index(CTX)
    z = lax.axis_index("z")
    cycle = lax.axis_size(CTX)
    stretch = q_stretch.shape[0]
    rows_dev, nblk = dec_q.shape[0], block_table.shape[1]
    pool_dev, block_size = pool_key_value.shape[:2]

    def after(x, *others):
        return lax.optimization_barrier((x, *others))[0]

    def swap(x, name):
        return lax.ppermute(x, name, [(0, 1), (1, 0)])

    def turn(x, step):
        return lax.ppermute(x, "z", [(n, (n + step) % Z_CHIPS) for n in range(Z_CHIPS)])

    ask, row_of, q_rows = question(me.reshape(1).astype(jnp.int32), block_table.T, cache_len, dec_q, cycle)
    context, fresh, q_stretch, ask = lax.optimization_barrier(
        (context_key_value, stretch_key_value, q_stretch, ask)
    )
    ask = lax.all_to_all(ask, CTX, split_axis=0, concat_axis=0, tiled=True)
    table = block_table.reshape(cycle, rows_dev * nblk)
    place = jnp.sum(jnp.where(table // pool_dev == me, table % pool_dev, 0), axis=1)

    kv = split_keys_values(context.reshape(-1, HEAD_SIZE), fresh.reshape(-1, HEAD_SIZE))
    kv_core, kv_y = swap(kv, "core"), swap(kv, "y")
    right = [q_stretch, turn(q_stretch, 1), turn(q_stretch, 2)]
    left = [q_stretch, turn(q_stretch, -1), turn(q_stretch, -2)]
    look_out = look(place, ask, pool_key_value.reshape(pool_dev, 2 * block_size, HEAD_SIZE))
    right[1], right[2], left[1], left[2], look_out = lax.optimization_barrier(
        (right[1], right[2], left[1], left[2], look_out)
    )
    answer = lax.all_to_all(look_out, CTX, split_axis=0, concat_axis=0, tiled=True)
    right += [turn(right[1], 2), turn(right[2], 2)]
    left.append(turn(left[1], -2))
    kv_yc = swap(after(kv_y, look_out), "core")
    keys, values = stack([kv, kv_core, kv_y, kv_yc])

    shifts = jnp.arange(Z_CHIPS, dtype=jnp.int32)
    corners = jnp.arange(2 * CORES, dtype=jnp.int32)
    corners = me ^ (corners // CORES * CORES * Z_CHIPS + corners % CORES)
    askers = me + ((z - shifts + Z_CHIPS) % Z_CHIPS - z) * CORES
    deltas = (askers[:, None] - corners[None, :]) * stretch

    def go(shift, previous, part=None):
        queries = right[shift] if shift >= 0 else left[-shift]
        return attend(shift % Z_CHIPS, after(deltas, previous), queries, keys, values, part)

    out = go(-3, values)
    from_left = turn(out, 1)
    out = go(4, out)
    from_right = turn(out, -1)

    attn = gather_answers(row_of, after(answer, out), q_rows, dec_new.reshape(rows_dev, 4, HEAD_SIZE))
    everyone = lax.all_to_all(attn, CTX, split_axis=0, concat_axis=0, tiled=True)
    out = go(-2, attn, from_left)
    from_left = turn(out, 1)
    out = go(3, out, from_right)
    from_right = turn(out, -1)
    out = go(-1, out, from_left)
    from_left = turn(out, 1)
    out = go(2, out, from_right)
    from_right = turn(out, -1)
    partial_out = project(after(everyone, out).reshape(-1, everyone.shape[2]), w_out)
    shares = lax.axis_size(("grp", "tp"))
    pieces = lax.all_to_all(
        partial_out.reshape(shares, -1, partial_out.shape[1]), ("grp", "tp"), split_axis=0, concat_axis=0, tiled=True
    )
    out = go(1, partial_out, from_right)
    from_right = turn(out, -1)
    own = go(0, out)
    pre_out = merge([own, from_right, from_left], stretch)
    dec_out = jnp.sum(pieces.astype(F32), axis=0).astype(BF16)
    return (pre_out, dec_out.reshape(-1, 2, dec_out.shape[1]))


def solution(mesh):
    shape = mesh.devices.shape
    fine = jax.sharding.Mesh(mesh.devices.reshape(-1, Z_CHIPS, CORES, *shape[1:]), (*CTX, *mesh.axis_names[1:]))
    placed = (
        P(CTX, ("grp", "tp")),
        P(CTX, None, ("grp", "tp")),
        P(CTX, None, ("grp", "tp")),
        P(CTX, None, ("grp", "tp")),
        P(CTX, None, None, ("grp", "tp")),
        P(CTX, None, None, ("grp", "tp")),
        P(),
        P(CTX),
        P(("grp", "tp"), CTX),
    )
    return jax.shard_map(
        shards,
        mesh=fine,
        in_specs=placed,
        out_specs=(P(CTX, ("grp", "tp")), P(("grp", "tp"), None, CTX)),
        check_vma=False,
    )
```

```python
import functools
import math

import jax
import jax.numpy as jnp
from jax import lax
from jax.experimental import pallas as pl
from jax.experimental.pallas import tpu as pltpu
from jax.sharding import PartitionSpec as P

HEAD_SIZE = 128
CORES = 2
Z_CHIPS = 8
CONTEXT_DEV = 1280
BLOCK = 128
CTX = ("y", "z", "core")
SCALE = math.log2(math.e) / math.sqrt(HEAD_SIZE)
LOWEST = -1e30
F32 = jnp.float32
BF16 = jnp.bfloat16
VMEM = pl.BlockSpec(memory_space=pltpu.VMEM)
SMEM = pl.BlockSpec(memory_space=pltpu.SMEM)
HBM = pl.BlockSpec(memory_space=pltpu.HBM)


def params(mib):
    return pltpu.CompilerParams(vmem_limit_bytes=mib * 1024 * 1024)


def in_hbm(x):
    return pltpu.with_memory_space_constraint(x, pltpu.HBM)


def dot_nt(a, b):
    return lax.dot_general(a, b, (((1,), (1,)), ((), ())), preferred_element_type=F32)


def dot_nn(a, b):
    return lax.dot_general(a, b, (((1,), (0,)), ((), ())), preferred_element_type=F32)


def split_body(context_hbm, stretch_hbm, kv_ref, context_ref, stretch_ref, sem):
    copies = []
    total = context_ref.shape[0]
    step = total // 5
    for n in range(5):
        rows = pl.ds(n * step, step)
        copies.append(pltpu.make_async_copy(context_hbm.at[rows], context_ref.at[rows], sem.at[n]))
    copies.append(pltpu.make_async_copy(stretch_hbm, stretch_ref, sem.at[5]))
    for copy in copies:
        copy.start()

    def split(rows, at):
        count = rows.shape[0]
        half = count // 2
        i = lax.broadcasted_iota(jnp.int32, (count, count), 0)
        j = lax.broadcasted_iota(jnp.int32, (count, count), 1)
        source = jnp.where(i < half, 2 * i, 2 * (i - half) + 1)
        pick = jnp.where(j == source, 1.0, 0.0).astype(BF16)
        parted = dot_nn(pick, rows).astype(BF16)
        kv_ref[0, at : at + half, :] = parted[:half]
        kv_ref[1, at : at + half, :] = parted[half:]

    for n in range(5):
        copies[n].wait()
        for start in range(n * step, (n + 1) * step, 256):
            split(context_ref[start : start + 256, :], start // 2)
    copies[5].wait()
    split(stretch_ref[...], total // 2)


def split_keys_values(context, stretch):
    rows = (context.shape[0] + stretch.shape[0]) // 2
    return pl.pallas_call(
        split_body,
        out_shape=jax.ShapeDtypeStruct((2, rows, HEAD_SIZE), BF16),
        in_specs=[HBM, HBM],
        out_specs=VMEM,
        scratch_shapes=[
            pltpu.VMEM(context.shape, BF16),
            pltpu.VMEM(stretch.shape, BF16),
            pltpu.SemaphoreType.DMA((6,)),
        ],
        compiler_params=params(16),
        name="split_keys_values",
    )(in_hbm(context), in_hbm(stretch))


def question_body(
    me_ref, table_hbm, length_ref, q_hbm, ask_ref, row_ref, rows_ref, list_ref, table_ref, q_ref, sem
):
    copies = [
        pltpu.make_async_copy(q_hbm, q_ref, sem.at[0]),
        pltpu.make_async_copy(table_hbm, table_ref, sem.at[1]),
    ]
    for copy in copies:
        copy.start()
    rows_dev = length_ref.shape[0]
    nblk = table_ref.shape[0]
    lists = ask_ref.shape[1] // 2
    heads = lists // 2
    pool_dev = ask_ref.shape[0]
    copies[0].wait()
    for r in range(rows_dev):
        q = q_ref[r].astype(F32)
        for t in range(2):
            for h in range(heads):
                at = t * heads + h
                list_ref[r, at : at + 1, :] = q[t : t + 1, h * HEAD_SIZE : (h + 1) * HEAD_SIZE]
    copies[1].wait()
    for r in range(rows_dev):
        asked = list_ref[r].astype(BF16)
        rows_ref[r] = asked
        for n in range(nblk):
            holder = table_ref[n, me_ref[0] * rows_dev + r] // pool_dev
            left = jnp.clip(length_ref[r] - n * BLOCK, 0, BLOCK).astype(F32)
            ask_ref[holder, :lists, :] = asked
            ask_ref[holder, lists:, :] = jnp.full((lists, HEAD_SIZE), left, F32).astype(BF16)
            row_ref[holder] = r


def question(me, table, length, q, holders):
    rows_dev = length.shape[0]
    lists = 2 * q.shape[2] // HEAD_SIZE
    return pl.pallas_call(
        question_body,
        out_shape=[
            jax.ShapeDtypeStruct((holders, 2 * lists, HEAD_SIZE), BF16),
            jax.ShapeDtypeStruct((holders,), jnp.int32),
            jax.ShapeDtypeStruct((rows_dev, lists, HEAD_SIZE), BF16),
        ],
        in_specs=[SMEM, HBM, SMEM, HBM],
        out_specs=[VMEM, SMEM, VMEM],
        scratch_shapes=[
            pltpu.VMEM((rows_dev, lists, HEAD_SIZE), F32),
            pltpu.SMEM(table.shape, jnp.int32),
            pltpu.VMEM(q.shape, BF16),
            pltpu.SemaphoreType.DMA((2,)),
        ],
        compiler_params=params(16),
        name="question",
    )(me, in_hbm(table), length, in_hbm(q))


def stack_body(*refs):
    kv_refs, k_ref, v_ref = refs[:-2], refs[-2], refs[-1]
    sets = len(kv_refs)
    stretch = v_ref.shape[0] // sets - CONTEXT_DEV
    one = jnp.where(diagonal(), 1.0, 0.0).astype(BF16)
    v_ref[:, HEAD_SIZE:] = jnp.ones((v_ref.shape[0], HEAD_SIZE), BF16)
    for n, ref in enumerate(kv_refs):
        first, last = n * CONTEXT_DEV, sets * CONTEXT_DEV + n * stretch
        for at in range(0, CONTEXT_DEV, 256):
            k_ref[:, first + at : first + at + 256] = dot_nt(one, ref[0, at : at + 256, :]).astype(BF16)
        v_ref[first : first + CONTEXT_DEV, :HEAD_SIZE] = ref[1, :CONTEXT_DEV, :]
        v_ref[last : last + stretch, :HEAD_SIZE] = ref[1, CONTEXT_DEV:, :]
    k = jnp.concatenate([ref[0, CONTEXT_DEV:, :] for ref in kv_refs], axis=0)
    k_ref[:, sets * CONTEXT_DEV :] = dot_nt(one, k).astype(BF16)


def stack(sets):
    keys = len(sets) * sets[0].shape[1]
    return pl.pallas_call(
        stack_body,
        out_shape=[
            jax.ShapeDtypeStruct((HEAD_SIZE, keys), BF16),
            jax.ShapeDtypeStruct((keys, 2 * HEAD_SIZE), BF16),
        ],
        in_specs=[VMEM] * len(sets),
        out_specs=[VMEM, VMEM],
        compiler_params=params(16),
        name="stack",
    )(*sets)


def diagonal():
    i = lax.broadcasted_iota(jnp.int32, (HEAD_SIZE, HEAD_SIZE), 0)
    j = lax.broadcasted_iota(jnp.int32, (HEAD_SIZE, HEAD_SIZE), 1)
    return i == j


def read_part(ref, stretch):
    width = ref.shape[1]
    rows = width // HEAD_SIZE * stretch
    outputs = jnp.concatenate([ref[:stretch, c : c + HEAD_SIZE] for c in range(0, width, HEAD_SIZE)], axis=0)
    stat = ref[stretch : stretch + 16, :rows].astype(F32)
    level = stat[0:1] + stat[1:2] + stat[2:3]
    columns = []
    for g in range(0, rows, HEAD_SIZE):
        column = jnp.sum(jnp.where(diagonal(), level[:, g : g + HEAD_SIZE], 0.0), axis=1, keepdims=True)
        columns.append(jnp.broadcast_to(column, (HEAD_SIZE, HEAD_SIZE)))
    return outputs.astype(F32), jnp.concatenate(columns, axis=0)


def join(outputs, levels):
    top = functools.reduce(jnp.maximum, levels)
    weights = [jnp.exp2(level - top) for level in levels]
    total = functools.reduce(jnp.add, weights)
    mixed = functools.reduce(jnp.add, [weight * output for weight, output in zip(weights, outputs)])
    return mixed / total, top + jnp.log2(total)


def write_outputs(ref, outputs, stretch):
    outputs = outputs.astype(BF16)
    for h in range(outputs.shape[0] // stretch):
        ref[:stretch, h * HEAD_SIZE : (h + 1) * HEAD_SIZE] = outputs[h * stretch : (h + 1) * stretch]


def write_level(ref, level, stretch):
    rows = level.shape[0]
    lines = []
    for g in range(0, rows, HEAD_SIZE):
        lines.append(jnp.sum(jnp.where(diagonal(), level[g : g + HEAD_SIZE], 0.0), axis=0, keepdims=True))
    level = jnp.concatenate(lines, axis=1)
    high = level.astype(BF16).astype(F32)
    rest = level - high
    middle = rest.astype(BF16).astype(F32)
    row = lax.broadcasted_iota(jnp.int32, (16, rows), 0)
    stat = jnp.where(row == 0, high, jnp.where(row == 1, middle, jnp.where(row == 2, rest - middle, 0.0)))
    ref[stretch : stretch + 16, :rows] = stat.astype(BF16)
    ref[stretch : stretch + 16, rows:] = jnp.zeros((16, ref.shape[1] - rows), BF16)


def attend_body(shifts, arrived, delta_ref, q_ref, k_ref, v_ref, *refs):
    refs = list(refs)
    count = len(shifts)
    part_refs = [refs.pop(0) for _ in range(count)] if arrived else None
    out_refs = [refs.pop(0) for _ in range(count)]
    p_ref, total_ref, top_ref = refs
    stretch, width = q_ref.shape[1:]
    sets = delta_ref.shape[1] - 1
    keys = v_ref.shape[0]
    rows = width // HEAD_SIZE * stretch
    chunk = 256
    span = CONTEXT_DEV

    def queries(n):
        q = q_ref.at[delta_ref[shifts[n], sets]]
        return jnp.concatenate([q[:, c : c + HEAD_SIZE] for c in range(0, width, HEAD_SIZE)], axis=0)

    def score(n, q, k, masked):
        s = dot_nn(q, k)
        if masked:
            row = lax.rem(lax.broadcasted_iota(jnp.int32, s.shape, 0), stretch)
            col = lax.broadcasted_iota(jnp.int32, s.shape, 1)
            bound = delta_ref[shifts[n], sets - 1] + (sets - 1) * stretch - col
            for m in reversed(range(sets - 1)):
                bound = jnp.where(col < (m + 1) * stretch, delta_ref[shifts[n], m] + m * stretch - col, bound)
            s = jnp.where(row + bound >= 0, s, LOWEST)
        return s

    def highest(s):
        parts = [s[:, c : c + HEAD_SIZE] for c in range(0, s.shape[1], HEAD_SIZE)]
        return functools.reduce(jnp.maximum, parts)

    def spread(top):
        return jnp.broadcast_to(jnp.max(top, axis=1, keepdims=True), (rows, HEAD_SIZE)) * SCALE

    def weigh(s, top):
        parts = [s[:, c : c + HEAD_SIZE] for c in range(0, s.shape[1], HEAD_SIZE)]
        return jnp.concatenate([jnp.exp2(part * SCALE - top) for part in parts], axis=1).astype(BF16)

    sums = []
    for n in range(count):
        q = queries(n)
        top = spread(highest(score(n, q, k_ref[:, :chunk], False)))
        total = None
        begun = 0
        for at in range(0, keys, chunk):
            masked = at >= sets * CONTEXT_DEV
            p_ref[n, :, at : at + chunk] = weigh(score(n, q, k_ref[:, at : at + chunk], masked), top)
            done = at + chunk
            if done - begun >= span and keys - done >= chunk * 2 or done == keys:
                part = dot_nn(p_ref[n, :, begun:done], v_ref[begun:done, :])
                total = part if total is None else total + part
                begun = done
        total_ref[n] = total
        top_ref[n] = top
        sums.append(total[:, HEAD_SIZE:])

    @pl.when(jnp.logical_not(jnp.max(functools.reduce(jnp.maximum, sums)) < 1e37))
    def again():
        for n in range(count):
            q = queries(n)
            last = score(n, q, k_ref[:, keys - chunk :], True)

            def climb(m, top):
                k = k_ref[:, pl.ds(pl.multiple_of(m * chunk, chunk), chunk)]
                return jnp.maximum(top, highest(score(n, q, k, False)))

            steps = (keys - chunk) // chunk
            top_ref[n] = spread(lax.fori_loop(0, steps, climb, highest(last)))
            total_ref[n] = dot_nn(weigh(last, top_ref[n]), v_ref[keys - chunk :, :])

            def add(m, carry):
                at = pl.ds(pl.multiple_of(m * chunk, chunk), chunk)
                total_ref[n] += dot_nn(weigh(score(n, q, k_ref[:, at], False), top_ref[n]), v_ref[at, :])
                return carry

            lax.fori_loop(0, steps, add, 0)

    for n in range(count):
        weight = total_ref[n, :, HEAD_SIZE:]
        output, level = total_ref[n, :, :HEAD_SIZE] / weight, top_ref[n] + jnp.log2(weight)
        if arrived:
            other, other_level = read_part(part_refs[n], stretch)
            output, level = join([output, other], [level, other_level])
        write_outputs(out_refs[n], output, stretch)
        write_level(out_refs[n], level, stretch)


def attend(shifts, deltas, queries, keys, values, parts=()):
    stretch, width = queries.shape[1:]
    rows = width // HEAD_SIZE * stretch
    keys_count = values.shape[0]
    count = len(shifts)
    operands = [deltas, queries, keys, values, *parts]
    return pl.pallas_call(
        functools.partial(attend_body, shifts, len(parts) > 0),
        out_shape=[jax.ShapeDtypeStruct((stretch + 16, width), BF16)] * count,
        in_specs=[SMEM] + [VMEM] * (len(operands) - 1),
        out_specs=[VMEM] * count,
        scratch_shapes=[
            pltpu.VMEM((count, rows, keys_count), BF16),
            pltpu.VMEM((count, rows, 2 * HEAD_SIZE), F32),
            pltpu.VMEM((count, rows, HEAD_SIZE), F32),
        ],
        compiler_params=params(32),
        cost_estimate=pl.CostEstimate(
            flops=8 * count * rows * keys_count * HEAD_SIZE,
            bytes_accessed=4 * keys_count * HEAD_SIZE,
            transcendentals=count * rows * keys_count,
        ),
        name="attend",
    )(*operands)


def merge_body(*refs):
    part_refs, out_ref = refs[:-1], refs[-1]
    stretch = out_ref.shape[0]
    read = [read_part(ref, stretch) for ref in part_refs]
    output, _ = join([x for x, _ in read], [x for _, x in read])
    write_outputs(out_ref, output, stretch)


def merge(parts, stretch):
    return pl.pallas_call(
        merge_body,
        out_shape=jax.ShapeDtypeStruct((stretch, parts[0].shape[1]), BF16),
        in_specs=[VMEM] * len(parts),
        out_specs=VMEM,
        compiler_params=params(16),
        name="merge",
    )(*parts)


def look_body(place_ref, ask_ref, pool_hbm, out_ref, s_ref, p_ref, pool_ref, sem):
    owners = ask_ref.shape[0]
    copies = []
    step = owners // sem.shape[0]
    for n in range(sem.shape[0]):
        blocks = pl.ds(n * step, step)
        copies.append(pltpu.make_async_copy(pool_hbm.at[blocks], pool_ref.at[blocks], sem.at[n]))
        copies[n].start()
    for copy in copies:
        copy.wait()
    half = ask_ref.shape[1] // 2
    span = pool_ref.shape[1]
    for d in range(owners):
        s_ref[d * half : (d + 1) * half, :] = dot_nt(ask_ref[d, :half, :], pool_ref[place_ref[d]])
    col = lax.broadcasted_iota(jnp.int32, (half, span), 1)
    lane = lax.broadcasted_iota(jnp.int32, (half, HEAD_SIZE), 1)
    even = (col & 1) == 0
    for d in range(owners):
        limit = ask_ref[d, half:, :].astype(F32) * 2.0
        limit = jnp.concatenate([limit] * (span // HEAD_SIZE), axis=1)
        allowed = even & (col.astype(F32) < limit)
        s = jnp.where(allowed, s_ref[d * half : (d + 1) * half, :], LOWEST)
        top = jnp.max(s, axis=1, keepdims=True)
        p = jnp.where(allowed, jnp.exp2((s - top) * SCALE), 0.0)
        total = jnp.sum(p, axis=1, keepdims=True)
        p_ref[d * half : (d + 1) * half, :] = pltpu.roll(p, 1, 1).astype(BF16)
        seen = total > 0.0
        level = jnp.where(seen, top * SCALE + jnp.log2(jnp.where(seen, total, 1.0)), LOWEST)
        level = jnp.broadcast_to(level, (half, HEAD_SIZE))
        high = level.astype(BF16).astype(F32)
        rest = level - high
        middle = rest.astype(BF16).astype(F32)
        low = rest - middle
        stat = jnp.where(lane == 0, high, jnp.where(lane == 1, middle, jnp.where(lane == 2, low, 0.0)))
        out_ref[d, half:, :] = stat.astype(BF16)
        s_ref[d * half : (d + 1) * half, :HEAD_SIZE] = jnp.broadcast_to(
            jnp.where(seen, 1.0 / jnp.where(seen, total, 1.0), 0.0), (half, HEAD_SIZE)
        )
    for d in range(owners):
        o = dot_nn(p_ref[d * half : (d + 1) * half, :], pool_ref[place_ref[d]])
        out_ref[d, :half, :] = (o * s_ref[d * half : (d + 1) * half, :HEAD_SIZE]).astype(BF16)


def look(place, ask, pool):
    owners, rows, width = ask.shape
    span = pool.shape[1]
    return pl.pallas_call(
        look_body,
        out_shape=jax.ShapeDtypeStruct(ask.shape, BF16),
        in_specs=[SMEM, VMEM, HBM],
        out_specs=VMEM,
        scratch_shapes=[
            pltpu.VMEM((owners * rows // 2, span), F32),
            pltpu.VMEM((owners * rows // 2, span), BF16),
            pltpu.VMEM(pool.shape, BF16),
            pltpu.SemaphoreType.DMA((4,)),
        ],
        compiler_params=params(24),
        cost_estimate=pl.CostEstimate(
            flops=16 * owners * rows * span * width, bytes_accessed=2 * owners * span * width, transcendentals=0
        ),
        name="look_in_blocks",
    )(place, ask, in_hbm(pool))


def gather_body(row_ref, answer_ref, q_ref, new_ref, out_ref, level_ref, top_ref, sum_ref, acc_ref, flat_ref):
    holders = answer_ref.shape[0]
    rows, lists = q_ref.shape[0], q_ref.shape[1]
    heads = lists // 2
    lane = lax.broadcasted_iota(jnp.int32, (lists, HEAD_SIZE), 1)
    later = lax.broadcasted_iota(jnp.int32, (lists, HEAD_SIZE), 0) >= heads
    own = []
    for r in range(rows):
        q = q_ref[r].astype(F32)
        new = new_ref[r].astype(F32)
        scores = []
        for t in range(2):
            s = jnp.sum(q * new[2 * t : 2 * t + 1, :], axis=1, keepdims=True) * SCALE
            scores.append(jnp.broadcast_to(s, (lists, HEAD_SIZE)))
        scores[1] = jnp.where(later, scores[1], LOWEST)
        top_ref[r] = jnp.maximum(scores[0], scores[1])
        own.append((scores, new))
    for d in range(holders):
        stat = answer_ref[d, lists:, :].astype(F32)
        level = jnp.sum(jnp.where(lane < 3, stat, 0.0), axis=1, keepdims=True)
        level_ref[d] = jnp.broadcast_to(level, (lists, HEAD_SIZE))
    for d in range(holders):
        r = row_ref[d]
        top_ref[r] = jnp.maximum(top_ref[r], level_ref[d])
    for r in range(rows):
        scores, new = own[r]
        first = jnp.exp2(scores[0] - top_ref[r])
        second = jnp.exp2(scores[1] - top_ref[r])
        sum_ref[r] = first + second
        acc_ref[r] = first * new[1:2, :] + second * new[3:4, :]
    for d in range(holders):
        r = row_ref[d]
        weight = jnp.exp2(level_ref[d] - top_ref[r])
        sum_ref[r] = sum_ref[r] + weight
        acc_ref[r] = acc_ref[r] + weight * answer_ref[d, :lists, :].astype(F32)
    for r in range(rows):
        o = acc_ref[r] / sum_ref[r]
        for t in range(2):
            for h in range(heads):
                flat_ref[2 * r + t : 2 * r + t + 1, h * HEAD_SIZE : (h + 1) * HEAD_SIZE] = o[
                    t * heads + h : t * heads + h + 1, :
                ]
    flat = flat_ref[...].astype(BF16)
    for d in range(holders):
        out_ref[d] = flat


def gather_answers(row_of, answer, q, new):
    rows, lists, width = q.shape
    holders = answer.shape[0]
    heads = lists // 2
    state = pltpu.VMEM((rows, lists, width), F32)
    return pl.pallas_call(
        gather_body,
        out_shape=jax.ShapeDtypeStruct((holders, 2 * rows, heads * width), BF16),
        in_specs=[SMEM, VMEM, VMEM, VMEM],
        out_specs=VMEM,
        scratch_shapes=[
            pltpu.VMEM((holders, lists, width), F32),
            state,
            state,
            state,
            pltpu.VMEM((2 * rows, heads * width), F32),
        ],
        compiler_params=params(16),
        name="gather_answers",
    )(row_of, answer, q, new)


def project_body(rows_ref, w_ref, out_ref):
    out_ref[...] = dot_nn(rows_ref[...], w_ref[...]).astype(BF16)


def project(rows, w):
    return pl.pallas_call(
        project_body,
        out_shape=jax.ShapeDtypeStruct((rows.shape[0], w.shape[1]), BF16),
        in_specs=[VMEM, VMEM],
        out_specs=VMEM,
        compiler_params=params(16),
        name="project",
    )(rows, w)


def shards(
    q_stretch,
    stretch_key_value,
    context_key_value,
    dec_q,
    dec_new,
    pool_key_value,
    block_table,
    cache_len,
    w_out,
):
    me = lax.axis_index(CTX)
    z = lax.axis_index("z")
    cycle = lax.axis_size(CTX)
    stretch = q_stretch.shape[0]
    rows_dev, nblk = dec_q.shape[0], block_table.shape[1]
    pool_dev, block_size = pool_key_value.shape[:2]

    def after(x, *others):
        return lax.optimization_barrier((x, *others))[0]

    def swap(x, name):
        return lax.ppermute(x, name, [(0, 1), (1, 0)])

    def turn(x, step):
        return lax.ppermute(x, "z", [(n, (n + step) % Z_CHIPS) for n in range(Z_CHIPS)])

    queries = lax.all_gather(q_stretch, "z", axis=0)

    ask, row_of, q_rows = question(me.reshape(1).astype(jnp.int32), block_table.T, cache_len, dec_q, cycle)
    ask = lax.all_to_all(ask, CTX, split_axis=0, concat_axis=0, tiled=True)
    table = block_table.reshape(cycle, rows_dev * nblk)
    place = jnp.sum(jnp.where(table // pool_dev == me, table % pool_dev, 0), axis=1)

    kv = split_keys_values(
        context_key_value.reshape(-1, HEAD_SIZE), stretch_key_value.reshape(-1, HEAD_SIZE)
    )
    kv_core, kv_y = swap(kv, "core"), swap(kv, "y")
    look_out = look(place, ask, pool_key_value.reshape(pool_dev, 2 * block_size, HEAD_SIZE))
    answer = lax.all_to_all(look_out, CTX, split_axis=0, concat_axis=0, tiled=True)
    kv_yc = swap(after(kv_y, look_out), "core")
    keys, values = stack([kv, kv_core, kv_y, kv_yc])

    shifts = jnp.arange(Z_CHIPS, dtype=jnp.int32)
    corners = jnp.arange(2 * CORES, dtype=jnp.int32)
    corners = me ^ (corners // CORES * CORES * Z_CHIPS + corners % CORES)
    whose = (z - shifts + Z_CHIPS) % Z_CHIPS
    askers = me + (whose - z) * CORES
    deltas = (askers[:, None] - corners[None, :]) * stretch
    deltas = jnp.concatenate([deltas, whose[:, None]], axis=1).astype(jnp.int32)

    def go(group, previous, parts=()):
        group = tuple(shift % Z_CHIPS for shift in group)
        return attend(group, after(deltas, *previous), queries, keys, values, parts)

    out = go((-3, 4), [values])
    parts = [turn(out[0], 1), turn(out[1], -1)]

    attn = gather_answers(row_of, after(answer, *out), q_rows, dec_new.reshape(rows_dev, 4, HEAD_SIZE))
    everyone = lax.all_to_all(attn, CTX, split_axis=0, concat_axis=0, tiled=True)
    out = go((-2, 3), [attn], parts)
    parts = [turn(out[0], 1), turn(out[1], -1)]
    own = go((0,), out)
    out = go((-1, 2), own, parts)
    parts = [turn(out[0], 1), turn(out[1], -1)]
    partial_out = project(after(everyone, *out).reshape(-1, everyone.shape[2]), w_out)
    shares = lax.axis_size(("grp", "tp"))
    pieces = lax.all_to_all(
        partial_out.reshape(shares, -1, partial_out.shape[1]), ("grp", "tp"), split_axis=0, concat_axis=0, tiled=True
    )
    out = go((1,), [partial_out], parts[1:])
    pre_out = merge([own[0], parts[0], turn(out[0], -1)], stretch)
    dec_out = jnp.sum(pieces.astype(F32), axis=0).astype(BF16)
    return (pre_out, dec_out.reshape(-1, 2, dec_out.shape[1]))


def solution(mesh):
    shape = mesh.devices.shape
    fine = jax.sharding.Mesh(mesh.devices.reshape(-1, Z_CHIPS, CORES, *shape[1:]), (*CTX, *mesh.axis_names[1:]))
    placed = (
        P(CTX, ("grp", "tp")),
        P(CTX, None, ("grp", "tp")),
        P(CTX, None, ("grp", "tp")),
        P(CTX, None, ("grp", "tp")),
        P(CTX, None, None, ("grp", "tp")),
        P(CTX, None, None, ("grp", "tp")),
        P(),
        P(CTX),
        P(("grp", "tp"), CTX),
    )
    return jax.shard_map(
        shards,
        mesh=fine,
        in_specs=placed,
        out_specs=(P(CTX, ("grp", "tp")), P(("grp", "tp"), None, CTX)),
        check_vma=False,
    )
```

```python
import functools
import math

import jax
import jax.numpy as jnp
from jax import lax
from jax.experimental import pallas as pl
from jax.experimental.pallas import tpu as pltpu
from jax.sharding import PartitionSpec as P

HEAD_SIZE = 128
CORES = 2
Z_CHIPS = 8
CONTEXT_DEV = 1280
BLOCK = 128
CTX = ("y", "z", "core")
SCALE = math.log2(math.e) / math.sqrt(HEAD_SIZE)
LOWEST = -1e30
F32 = jnp.float32
BF16 = jnp.bfloat16
VMEM = pl.BlockSpec(memory_space=pltpu.VMEM)
SMEM = pl.BlockSpec(memory_space=pltpu.SMEM)
HBM = pl.BlockSpec(memory_space=pltpu.HBM)


def params(mib):
    return pltpu.CompilerParams(vmem_limit_bytes=mib * 1024 * 1024)


def in_hbm(x):
    return pltpu.with_memory_space_constraint(x, pltpu.HBM)


def in_vmem(x):
    return pltpu.with_memory_space_constraint(x, pltpu.VMEM)


def dot_nt(a, b):
    return lax.dot_general(a, b, (((1,), (1,)), ((), ())), preferred_element_type=F32)


def dot_nn(a, b):
    return lax.dot_general(a, b, (((1,), (0,)), ((), ())), preferred_element_type=F32)


def split_body(context_hbm, stretch_hbm, kv_ref, context_ref, stretch_ref, sem):
    copies = []
    total = context_ref.shape[0]
    step = total // 5
    for n in range(5):
        rows = pl.ds(n * step, step)
        copies.append(pltpu.make_async_copy(context_hbm.at[rows], context_ref.at[rows], sem.at[n]))
    copies.append(pltpu.make_async_copy(stretch_hbm, stretch_ref, sem.at[5]))
    for copy in copies:
        copy.start()

    def split(rows, at):
        count = rows.shape[0]
        half = count // 2
        i = lax.broadcasted_iota(jnp.int32, (count, count), 0)
        j = lax.broadcasted_iota(jnp.int32, (count, count), 1)
        source = jnp.where(i < half, 2 * i, 2 * (i - half) + 1)
        pick = jnp.where(j == source, 1.0, 0.0).astype(BF16)
        parted = dot_nn(pick, rows).astype(BF16)
        kv_ref[0, at : at + half, :] = parted[:half]
        kv_ref[1, at : at + half, :] = parted[half:]

    for n in range(5):
        copies[n].wait()
        for start in range(n * step, (n + 1) * step, 256):
            split(context_ref[start : start + 256, :], start // 2)
    copies[5].wait()
    split(stretch_ref[...], total // 2)


def split_keys_values(context, stretch):
    rows = (context.shape[0] + stretch.shape[0]) // 2
    return pl.pallas_call(
        split_body,
        out_shape=jax.ShapeDtypeStruct((2, rows, HEAD_SIZE), BF16),
        in_specs=[HBM, HBM],
        out_specs=VMEM,
        scratch_shapes=[
            pltpu.VMEM(context.shape, BF16),
            pltpu.VMEM(stretch.shape, BF16),
            pltpu.SemaphoreType.DMA((6,)),
        ],
        compiler_params=params(16),
        name="split_keys_values",
    )(in_hbm(context), in_hbm(stretch))


def question_body(
    me_ref, table_hbm, length_ref, q_hbm, ask_ref, row_ref, rows_ref, list_ref, table_ref, q_ref, sem
):
    copies = [
        pltpu.make_async_copy(q_hbm, q_ref, sem.at[0]),
        pltpu.make_async_copy(table_hbm, table_ref, sem.at[1]),
    ]
    for copy in copies:
        copy.start()
    rows_dev = length_ref.shape[0]
    nblk = table_ref.shape[0]
    lists = rows_ref.shape[1]
    heads = lists // 2
    pool_dev = ask_ref.shape[0]
    copies[0].wait()
    for r in range(rows_dev):
        q = q_ref[r].astype(F32)
        for t in range(2):
            for h in range(heads):
                at = t * heads + h
                list_ref[r, at : at + 1, :] = q[t : t + 1, h * HEAD_SIZE : (h + 1) * HEAD_SIZE]
    copies[1].wait()
    for r in range(rows_dev):
        listed = list_ref[r]
        rows_ref[r] = listed.astype(BF16)
        asked = jnp.concatenate([listed[:heads], listed[heads:]], axis=1).astype(BF16)
        for n in range(nblk):
            holder = table_ref[n, me_ref[0] * rows_dev + r] // pool_dev
            left = jnp.clip(length_ref[r] - n * BLOCK, 0, BLOCK).astype(F32)
            ask_ref[holder, :, : 2 * HEAD_SIZE] = asked
            ask_ref[holder, :, 2 * HEAD_SIZE :] = jnp.full((heads, HEAD_SIZE), left, F32).astype(BF16)
            row_ref[holder] = r


def question(me, table, length, q, holders):
    rows_dev = length.shape[0]
    lists = 2 * q.shape[2] // HEAD_SIZE
    return pl.pallas_call(
        question_body,
        out_shape=[
            jax.ShapeDtypeStruct((holders, lists // 2, 3 * HEAD_SIZE), BF16),
            jax.ShapeDtypeStruct((holders,), jnp.int32),
            jax.ShapeDtypeStruct((rows_dev, lists, HEAD_SIZE), BF16),
        ],
        in_specs=[SMEM, HBM, SMEM, HBM],
        out_specs=[VMEM, SMEM, VMEM],
        scratch_shapes=[
            pltpu.VMEM((rows_dev, lists, HEAD_SIZE), F32),
            pltpu.SMEM(table.shape, jnp.int32),
            pltpu.VMEM(q.shape, BF16),
            pltpu.SemaphoreType.DMA((2,)),
        ],
        compiler_params=params(16),
        name="question",
    )(me, in_hbm(table), length, in_hbm(q))


def stack_body(*refs):
    kv_refs, k_ref, v_ref = refs[:-2], refs[-2], refs[-1]
    sets = len(kv_refs)
    stretch = v_ref.shape[0] // sets - CONTEXT_DEV
    one = jnp.where(diagonal(), 1.0, 0.0).astype(BF16)
    v_ref[:, HEAD_SIZE:] = jnp.ones((v_ref.shape[0], HEAD_SIZE), BF16)
    for n, ref in enumerate(kv_refs):
        first, last = n * CONTEXT_DEV, sets * CONTEXT_DEV + n * stretch
        for at in range(0, CONTEXT_DEV, 256):
            k_ref[:, first + at : first + at + 256] = dot_nt(one, ref[0, at : at + 256, :]).astype(BF16)
        v_ref[first : first + CONTEXT_DEV, :HEAD_SIZE] = ref[1, :CONTEXT_DEV, :]
        v_ref[last : last + stretch, :HEAD_SIZE] = ref[1, CONTEXT_DEV:, :]
    k = jnp.concatenate([ref[0, CONTEXT_DEV:, :] for ref in kv_refs], axis=0)
    k_ref[:, sets * CONTEXT_DEV :] = dot_nt(one, k).astype(BF16)


def stack(sets):
    keys = len(sets) * sets[0].shape[1]
    return pl.pallas_call(
        stack_body,
        out_shape=[
            jax.ShapeDtypeStruct((HEAD_SIZE, keys), BF16),
            jax.ShapeDtypeStruct((keys, 2 * HEAD_SIZE), BF16),
        ],
        in_specs=[VMEM] * len(sets),
        out_specs=[VMEM, VMEM],
        compiler_params=params(16),
        name="stack",
    )(*sets)


def diagonal():
    i = lax.broadcasted_iota(jnp.int32, (HEAD_SIZE, HEAD_SIZE), 0)
    j = lax.broadcasted_iota(jnp.int32, (HEAD_SIZE, HEAD_SIZE), 1)
    return i == j


def read_part(ref, stretch):
    width = ref.shape[1]
    rows = width // HEAD_SIZE * stretch
    outputs = jnp.concatenate([ref[:stretch, c : c + HEAD_SIZE] for c in range(0, width, HEAD_SIZE)], axis=0)
    stat = ref[stretch : stretch + 16, :rows].astype(F32)
    level = stat[0:1] + stat[1:2] + stat[2:3]
    columns = []
    for g in range(0, rows, HEAD_SIZE):
        column = jnp.sum(jnp.where(diagonal(), level[:, g : g + HEAD_SIZE], 0.0), axis=1, keepdims=True)
        columns.append(jnp.broadcast_to(column, (HEAD_SIZE, HEAD_SIZE)))
    return outputs.astype(F32), jnp.concatenate(columns, axis=0)


def join(outputs, levels):
    top = functools.reduce(jnp.maximum, levels)
    weights = [jnp.exp2(level - top) for level in levels]
    total = functools.reduce(jnp.add, weights)
    mixed = functools.reduce(jnp.add, [weight * output for weight, output in zip(weights, outputs)])
    return mixed / total, top + jnp.log2(total)


def write_outputs(ref, outputs, stretch):
    outputs = outputs.astype(BF16)
    for h in range(outputs.shape[0] // stretch):
        ref[:stretch, h * HEAD_SIZE : (h + 1) * HEAD_SIZE] = outputs[h * stretch : (h + 1) * stretch]


def write_level(ref, level, stretch):
    rows = level.shape[0]
    lines = []
    for g in range(0, rows, HEAD_SIZE):
        lines.append(jnp.sum(jnp.where(diagonal(), level[g : g + HEAD_SIZE], 0.0), axis=0, keepdims=True))
    level = jnp.concatenate(lines, axis=1)
    high = level.astype(BF16).astype(F32)
    rest = level - high
    middle = rest.astype(BF16).astype(F32)
    row = lax.broadcasted_iota(jnp.int32, (16, rows), 0)
    stat = jnp.where(row == 0, high, jnp.where(row == 1, middle, jnp.where(row == 2, rest - middle, 0.0)))
    ref[stretch : stretch + 16, :rows] = stat.astype(BF16)
    ref[stretch : stretch + 16, rows:] = jnp.zeros((16, ref.shape[1] - rows), BF16)


def attend_body(shifts, arrived, riders, delta_ref, k_ref, v_ref, *refs):
    refs = list(refs)
    count = len(shifts)
    q_refs = [refs.pop(0) for _ in range(count)]
    part_refs = [refs.pop(0) for _ in range(count)] if arrived else None
    rider_ref = refs.pop(0) if riders == "own" else None
    out_refs = [refs.pop(0) for _ in range(count)]
    p_ref, total_ref, top_ref = refs
    stretch, width = q_refs[0].shape
    sets = delta_ref.shape[1]
    keys = v_ref.shape[0]
    rows = width // HEAD_SIZE * stretch
    chunk = 256
    span = CONTEXT_DEV

    def queries(n):
        return jnp.concatenate([q_refs[n][:, c : c + HEAD_SIZE] for c in range(0, width, HEAD_SIZE)], axis=0)

    def score(n, q, k, masked):
        s = dot_nn(q, k)
        if masked:
            row = lax.rem(lax.broadcasted_iota(jnp.int32, s.shape, 0), stretch)
            col = lax.broadcasted_iota(jnp.int32, s.shape, 1)
            bound = delta_ref[shifts[n], sets - 1] + (sets - 1) * stretch - col
            for m in reversed(range(sets - 1)):
                bound = jnp.where(col < (m + 1) * stretch, delta_ref[shifts[n], m] + m * stretch - col, bound)
            s = jnp.where(row + bound >= 0, s, LOWEST)
        return s

    def highest(s):
        parts = [s[:, c : c + HEAD_SIZE] for c in range(0, s.shape[1], HEAD_SIZE)]
        return functools.reduce(jnp.maximum, parts)

    def spread(top):
        return jnp.broadcast_to(jnp.max(top, axis=1, keepdims=True), (rows, HEAD_SIZE)) * SCALE

    def weigh(s, top):
        parts = [s[:, c : c + HEAD_SIZE] for c in range(0, s.shape[1], HEAD_SIZE)]
        return jnp.concatenate([jnp.exp2(part * SCALE - top) for part in parts], axis=1).astype(BF16)

    for n in range(count):
        if riders == "own":
            out_refs[n][stretch + 16 :, :] = rider_ref[...]
        elif riders == "arrived":
            out_refs[n][stretch + 16 :, :] = part_refs[n][stretch + 16 :, :]

    sums = []
    for n in range(count):
        q = queries(n)
        top = spread(highest(score(n, q, k_ref[:, :chunk], False)))
        total = None
        begun = 0
        for at in range(0, keys, chunk):
            masked = at >= sets * CONTEXT_DEV
            p_ref[n, :, at : at + chunk] = weigh(score(n, q, k_ref[:, at : at + chunk], masked), top)
            done = at + chunk
            if done - begun >= span and keys - done >= chunk * 2 or done == keys:
                part = dot_nn(p_ref[n, :, begun:done], v_ref[begun:done, :])
                total = part if total is None else total + part
                begun = done
        total_ref[n] = total
        top_ref[n] = top
        sums.append(total[:, HEAD_SIZE:])

    @pl.when(jnp.logical_not(jnp.max(functools.reduce(jnp.maximum, sums)) < 1e37))
    def again():
        for n in range(count):
            q = queries(n)
            last = score(n, q, k_ref[:, keys - chunk :], True)

            def climb(m, top):
                k = k_ref[:, pl.ds(pl.multiple_of(m * chunk, chunk), chunk)]
                return jnp.maximum(top, highest(score(n, q, k, False)))

            steps = (keys - chunk) // chunk
            top_ref[n] = spread(lax.fori_loop(0, steps, climb, highest(last)))
            total_ref[n] = dot_nn(weigh(last, top_ref[n]), v_ref[keys - chunk :, :])

            def add(m, carry):
                at = pl.ds(pl.multiple_of(m * chunk, chunk), chunk)
                total_ref[n] += dot_nn(weigh(score(n, q, k_ref[:, at], False), top_ref[n]), v_ref[at, :])
                return carry

            lax.fori_loop(0, steps, add, 0)

    for n in range(count):
        weight = total_ref[n, :, HEAD_SIZE:]
        output, level = total_ref[n, :, :HEAD_SIZE] / weight, top_ref[n] + jnp.log2(weight)
        if arrived:
            other, other_level = read_part(part_refs[n], stretch)
            output, level = join([output, other], [level, other_level])
        write_outputs(out_refs[n], output, stretch)
        write_level(out_refs[n], level, stretch)


def attend(shifts, deltas, queries, keys, values, parts=(), rider=None, carry=True):
    stretch, width = queries[0].shape
    rows = width // HEAD_SIZE * stretch
    keys_count = values.shape[0]
    count = len(shifts)
    operands = [deltas, keys, values, *queries, *parts]
    out_rows = stretch + 16
    riders = None
    if rider is not None:
        riders = "own"
        operands.append(rider)
        out_rows += rider.shape[0]
    elif parts and carry:
        riders = "arrived"
        out_rows = parts[0].shape[0]
    return pl.pallas_call(
        functools.partial(attend_body, shifts, len(parts) > 0, riders),
        out_shape=[jax.ShapeDtypeStruct((out_rows, width), BF16)] * count,
        in_specs=[SMEM] + [VMEM] * (len(operands) - 1),
        out_specs=[VMEM] * count,
        scratch_shapes=[
            pltpu.VMEM((count, rows, keys_count), BF16),
            pltpu.VMEM((count, rows, 2 * HEAD_SIZE), F32),
            pltpu.VMEM((count, rows, HEAD_SIZE), F32),
        ],
        compiler_params=params(24),
        cost_estimate=pl.CostEstimate(
            flops=8 * count * rows * keys_count * HEAD_SIZE,
            bytes_accessed=4 * keys_count * HEAD_SIZE,
            transcendentals=count * rows * keys_count,
        ),
        name="attend",
    )(*operands)


def merge_body(*refs):
    part_refs, out_ref = refs[:-1], refs[-1]
    stretch = out_ref.shape[0]
    read = [read_part(ref, stretch) for ref in part_refs]
    output, _ = join([x for x, _ in read], [x for _, x in read])
    write_outputs(out_ref, output, stretch)


def merge(parts, stretch):
    return pl.pallas_call(
        merge_body,
        out_shape=jax.ShapeDtypeStruct((stretch, parts[0].shape[1]), BF16),
        in_specs=[VMEM] * len(parts),
        out_specs=VMEM,
        compiler_params=params(16),
        name="merge",
    )(*parts)


def fetch_body(pool_hbm, pool_ref, sem):
    copies = []
    step = pool_ref.shape[0] // sem.shape[0]
    for n in range(sem.shape[0]):
        blocks = pl.ds(n * step, step)
        copies.append(pltpu.make_async_copy(pool_hbm.at[blocks], pool_ref.at[blocks], sem.at[n]))
        copies[n].start()
    for copy in copies:
        copy.wait()


def fetch(pool):
    return pl.pallas_call(
        fetch_body,
        out_shape=pltpu.VMEM(pool.shape, BF16),
        in_specs=[HBM],
        out_specs=VMEM,
        scratch_shapes=[pltpu.SemaphoreType.DMA((4,))],
        compiler_params=params(16),
        name="fetch_blocks",
    )(in_hbm(pool))


def look_body(place_ref, ask_ref, pool_ref, out_ref, s_ref, p_ref, scale_ref):
    owners, heads = ask_ref.shape[:2]
    lists = 2 * heads
    span = pool_ref.shape[1]
    for d in range(owners):
        q = ask_ref[d, :, : 2 * HEAD_SIZE].astype(F32)
        q = jnp.concatenate([q[:, :HEAD_SIZE], q[:, HEAD_SIZE:]], axis=0).astype(BF16)
        s_ref[d * lists : (d + 1) * lists, :] = dot_nt(q, pool_ref[place_ref[d]])
    col = lax.broadcasted_iota(jnp.int32, (lists, span), 1)
    lane = lax.broadcasted_iota(jnp.int32, (heads, HEAD_SIZE), 1)
    even = (col & 1) == 0
    for d in range(owners):
        limit = ask_ref[d, :, 2 * HEAD_SIZE :].astype(F32) * 2.0
        limit = jnp.concatenate([limit] * 2, axis=0)
        limit = jnp.concatenate([limit] * (span // HEAD_SIZE), axis=1)
        allowed = even & (col.astype(F32) < limit)
        s = jnp.where(allowed, s_ref[d * lists : (d + 1) * lists, :], LOWEST)
        top = jnp.max(s, axis=1, keepdims=True)
        p = jnp.where(allowed, jnp.exp2((s - top) * SCALE), 0.0)
        total = jnp.sum(p, axis=1, keepdims=True)
        p_ref[d * lists : (d + 1) * lists, :] = pltpu.roll(p, 1, 1).astype(BF16)
        seen = total > 0.0
        level = jnp.where(seen, top * SCALE + jnp.log2(jnp.where(seen, total, 1.0)), LOWEST)
        level = jnp.broadcast_to(level, (lists, HEAD_SIZE))
        high = level.astype(BF16).astype(F32)
        rest = level - high
        middle = rest.astype(BF16).astype(F32)
        stat = jnp.zeros((heads, HEAD_SIZE), F32)
        for t in range(2):
            for n, piece in enumerate((high, middle, rest - middle)):
                stat = jnp.where(lane == 3 * t + n, piece[t * heads : (t + 1) * heads], stat)
        out_ref[d, :, 2 * HEAD_SIZE :] = stat.astype(BF16)
        scale_ref[d * lists : (d + 1) * lists, :] = jnp.broadcast_to(
            jnp.where(seen, 1.0 / jnp.where(seen, total, 1.0), 0.0), (lists, HEAD_SIZE)
        )
    for d in range(owners):
        o = dot_nn(p_ref[d * lists : (d + 1) * lists, :], pool_ref[place_ref[d]])
        o = o * scale_ref[d * lists : (d + 1) * lists, :]
        out_ref[d, :, : 2 * HEAD_SIZE] = jnp.concatenate([o[:heads], o[heads:]], axis=1).astype(BF16)


def look(place, ask, pool):
    owners, heads, width = ask.shape
    span = pool.shape[1]
    rows = 2 * owners * heads
    return pl.pallas_call(
        look_body,
        out_shape=jax.ShapeDtypeStruct(ask.shape, BF16),
        in_specs=[SMEM, VMEM, VMEM],
        out_specs=VMEM,
        scratch_shapes=[
            pltpu.VMEM((rows, span), F32),
            pltpu.VMEM((rows, span), BF16),
            pltpu.VMEM((rows, HEAD_SIZE), F32),
        ],
        compiler_params=params(24),
        cost_estimate=pl.CostEstimate(
            flops=4 * rows * span * HEAD_SIZE, bytes_accessed=2 * owners * span * HEAD_SIZE, transcendentals=0
        ),
        name="look_in_blocks",
    )(place, ask, pool)


def gather_body(row_ref, answer_ref, q_ref, new_ref, out_ref, level_ref, top_ref, sum_ref, acc_ref, flat_ref):
    holders = answer_ref.shape[0]
    rows, lists = q_ref.shape[0], q_ref.shape[1]
    heads = lists // 2
    lane = lax.broadcasted_iota(jnp.int32, (lists, HEAD_SIZE), 1)
    later = lax.broadcasted_iota(jnp.int32, (lists, HEAD_SIZE), 0) >= heads
    own = []
    for r in range(rows):
        q = q_ref[r].astype(F32)
        new = new_ref[r].astype(F32)
        scores = []
        for t in range(2):
            s = jnp.sum(q * new[2 * t : 2 * t + 1, :], axis=1, keepdims=True) * SCALE
            scores.append(jnp.broadcast_to(s, (lists, HEAD_SIZE)))
        scores[1] = jnp.where(later, scores[1], LOWEST)
        top_ref[r] = jnp.maximum(scores[0], scores[1])
        own.append((scores, new))
    for d in range(holders):
        stat = answer_ref[d, :, 2 * HEAD_SIZE :].astype(F32)
        stat = jnp.concatenate([stat, stat], axis=0)
        level = jnp.sum(jnp.where((lane < 6) & ((lane >= 3) == later), stat, 0.0), axis=1, keepdims=True)
        level_ref[d] = jnp.broadcast_to(level, (lists, HEAD_SIZE))
    for d in range(holders):
        r = row_ref[d]
        top_ref[r] = jnp.maximum(top_ref[r], level_ref[d])
    for r in range(rows):
        scores, new = own[r]
        first = jnp.exp2(scores[0] - top_ref[r])
        second = jnp.exp2(scores[1] - top_ref[r])
        sum_ref[r] = first + second
        acc_ref[r] = first * new[1:2, :] + second * new[3:4, :]
    for d in range(holders):
        r = row_ref[d]
        weight = jnp.exp2(level_ref[d] - top_ref[r])
        sum_ref[r] = sum_ref[r] + weight
        o = answer_ref[d, :, : 2 * HEAD_SIZE].astype(F32)
        o = jnp.concatenate([o[:, :HEAD_SIZE], o[:, HEAD_SIZE:]], axis=0)
        acc_ref[r] = acc_ref[r] + weight * o
    for r in range(rows):
        o = acc_ref[r] / sum_ref[r]
        for t in range(2):
            for h in range(heads):
                flat_ref[2 * r + t : 2 * r + t + 1, h * HEAD_SIZE : (h + 1) * HEAD_SIZE] = o[
                    t * heads + h : t * heads + h + 1, :
                ]
    out_ref[...] = flat_ref[...].astype(BF16)


def gather_answers(row_of, answer, q, new):
    rows, lists, width = q.shape
    holders = answer.shape[0]
    heads = lists // 2
    state = pltpu.VMEM((rows, lists, width), F32)
    return pl.pallas_call(
        gather_body,
        out_shape=jax.ShapeDtypeStruct((2 * rows, heads * width), BF16),
        in_specs=[SMEM, VMEM, VMEM, VMEM],
        out_specs=VMEM,
        scratch_shapes=[
            pltpu.VMEM((holders, lists, width), F32),
            state,
            state,
            state,
            pltpu.VMEM((2 * rows, heads * width), F32),
        ],
        compiler_params=params(16),
        name="gather_answers",
    )(row_of, answer, q, new)


def project_body(place_ref, own_ref, w_ref, *refs):
    ref_list, out_ref, total_ref, rows_ref = refs[:-3], refs[-3], refs[-2], refs[-1]
    rows = own_ref.shape[0]
    rows_ref[:rows, :] = own_ref[...]
    for n, ref in enumerate(ref_list):
        rows_ref[(n + 1) * rows : (n + 2) * rows, :] = ref[ref.shape[0] - rows :, :]
    total = dot_nn(rows_ref[...], w_ref[...])
    for n in range(rows_ref.shape[0] // 8):
        at = pl.multiple_of(place_ref[n], 8)
        total_ref[pl.ds(at, 8), :] = total[8 * n : 8 * n + 8]
    out_ref[...] = total_ref[...].astype(BF16)


def project(place, own, w, parts):
    rows = own.shape[0] * (len(parts) + 1)
    return pl.pallas_call(
        project_body,
        out_shape=jax.ShapeDtypeStruct((rows, w.shape[1]), BF16),
        in_specs=[SMEM] + [VMEM] * (len(parts) + 2),
        out_specs=VMEM,
        scratch_shapes=[pltpu.VMEM((rows, w.shape[1]), F32), pltpu.VMEM((rows, own.shape[1]), BF16)],
        compiler_params=params(16),
        name="project",
    )(place, own, w, *parts)


def shards(
    q_stretch,
    stretch_key_value,
    context_key_value,
    dec_q,
    dec_new,
    pool_key_value,
    block_table,
    cache_len,
    w_out,
):
    me = lax.axis_index(CTX)
    z = lax.axis_index("z")
    cycle = lax.axis_size(CTX)
    stretch = q_stretch.shape[0]
    rows_dev, nblk = dec_q.shape[0], block_table.shape[1]
    pool_dev, block_size = pool_key_value.shape[:2]

    def after(x, *others):
        return lax.optimization_barrier((x, *others))[0]

    def swap(x, name):
        return lax.ppermute(x, name, [(0, 1), (1, 0)])

    def turn(x, step):
        return lax.ppermute(x, "z", [(n, (n + step) % Z_CHIPS) for n in range(Z_CHIPS)])

    ask, row_of, q_rows = question(me.reshape(1).astype(jnp.int32), block_table.T, cache_len, dec_q, cycle)
    context, fresh, pool, q_stretch, ask = lax.optimization_barrier(
        (context_key_value, stretch_key_value, pool_key_value, q_stretch, ask)
    )
    ask = lax.all_to_all(ask, CTX, split_axis=0, concat_axis=0, tiled=True)
    table = block_table.reshape(cycle, rows_dev * nblk)
    place = jnp.sum(jnp.where(table // pool_dev == me, table % pool_dev, 0), axis=1)

    kv = split_keys_values(context.reshape(-1, HEAD_SIZE), fresh.reshape(-1, HEAD_SIZE))
    kv_core, kv_y = swap(kv, "core"), swap(kv, "y")
    right = [q_stretch, turn(q_stretch, 1), turn(q_stretch, 2)]
    left = [q_stretch, turn(q_stretch, -1), turn(q_stretch, -2)]
    blocks = fetch(pool.reshape(pool_dev, 2 * block_size, HEAD_SIZE))
    look_out = look(place, ask, blocks)
    right[1], right[2], left[1], left[2], look_out = lax.optimization_barrier(
        (right[1], right[2], left[1], left[2], look_out)
    )
    answer = lax.all_to_all(look_out, CTX, split_axis=0, concat_axis=0, tiled=True)
    left.append(turn(left[1], -2))
    right += [turn(right[1], 2), turn(right[2], 2)]
    kv_yc = swap(after(kv_y, look_out), "core")
    right[3], right[4], left[3], kv_yc, answer = lax.optimization_barrier(
        (right[3], right[4], left[3], kv_yc, answer)
    )
    attn = gather_answers(row_of, answer, q_rows, dec_new.reshape(rows_dev, 4, HEAD_SIZE))
    attn_core = swap(attn, "core")
    sets, _ = lax.optimization_barrier(([kv, kv_core, kv_y, kv_yc], attn))
    keys, values = stack(sets)
    pair = jnp.concatenate([attn, attn_core], axis=0)
    pair_y = swap(pair, "y")

    shifts = jnp.arange(Z_CHIPS, dtype=jnp.int32)
    corners = jnp.arange(2 * CORES, dtype=jnp.int32)
    corners = me ^ (corners // CORES * CORES * Z_CHIPS + corners % CORES)
    askers = me + ((z - shifts + Z_CHIPS) % Z_CHIPS - z) * CORES
    deltas = (askers[:, None] - corners[None, :]) * stretch

    def go(shift, previous, parts=(), rider=None, carry=True):
        queries = right[shift] if shift >= 0 else left[-shift]
        return attend((shift % Z_CHIPS,), after(deltas, *previous), [queries], keys, values, parts, rider, carry)[0]

    own = go(0, [pair])
    attn = jnp.concatenate([pair, pair_y], axis=0)
    out = go(4, [own], (), attn)
    from_right = [turn(out, -1)]
    out = go(-3, [out], (), attn)
    from_left = [turn(out, 1)]
    out = go(3, [out], from_right[-1:])
    from_right.append(turn(out, -1))
    out = go(-2, [out], from_left[-1:])
    from_left.append(turn(out, 1))
    out = go(2, [out], from_right[-1:])
    from_right.append(turn(out, -1))
    out = go(-1, [out], from_left[-1:])
    from_left.append(turn(out, 1))
    rest = from_right[2][stretch + 16 :]
    farthest = turn(rest, -1)
    out = go(1, [out, rest], from_right[2:], None, False)
    last = turn(out, -1)

    relative = jnp.where(shifts > Z_CHIPS // 2, Z_CHIPS // 2 - shifts, shifts)
    there = ((z + relative + Z_CHIPS) % Z_CHIPS - z) * CORES
    holders = ((there[:, None] + corners[None, :]) * (2 * rows_dev)).reshape(-1)
    partial_out = project(holders, after(attn, out), w_out, [*from_right, farthest, *from_left])
    shares = lax.axis_size(("grp", "tp"))
    pieces = lax.all_to_all(
        partial_out.reshape(shares, -1, partial_out.shape[1]), ("grp", "tp"), split_axis=0, concat_axis=0, tiled=True
    )
    pre_out = merge([own, last, from_left[2]], stretch)
    dec_out = jnp.sum(pieces.astype(F32), axis=0).astype(BF16)
    return (pre_out, dec_out.reshape(-1, 2, dec_out.shape[1]))


def solution(mesh):
    shape = mesh.devices.shape
    fine = jax.sharding.Mesh(mesh.devices.reshape(-1, Z_CHIPS, CORES, *shape[1:]), (*CTX, *mesh.axis_names[1:]))
    placed = (
        P(CTX, ("grp", "tp")),
        P(CTX, None, ("grp", "tp")),
        P(CTX, None, ("grp", "tp")),
        P(CTX, None, ("grp", "tp")),
        P(CTX, None, None, ("grp", "tp")),
        P(CTX, None, None, ("grp", "tp")),
        P(),
        P(CTX),
        P(("grp", "tp"), CTX),
    )
    return jax.shard_map(
        shards,
        mesh=fine,
        in_specs=placed,
        out_specs=(P(CTX, ("grp", "tp")), P(("grp", "tp"), None, CTX)),
        check_vma=False,
    )
```

```python
import functools
import math

import jax
import jax.numpy as jnp
from jax import lax
from jax.experimental import pallas as pl
from jax.experimental.pallas import tpu as pltpu
from jax.sharding import PartitionSpec as P

HEAD_SIZE = 128
CORES = 2
Z_CHIPS = 8
CONTEXT_DEV = 1280
BLOCK = 128
CTX = ("y", "z", "core")
SCALE = math.log2(math.e) / math.sqrt(HEAD_SIZE)
LOWEST = -1e30
F32 = jnp.float32
BF16 = jnp.bfloat16
VMEM = pl.BlockSpec(memory_space=pltpu.VMEM)
SMEM = pl.BlockSpec(memory_space=pltpu.SMEM)
HBM = pl.BlockSpec(memory_space=pltpu.HBM)


def params(mib):
    return pltpu.CompilerParams(vmem_limit_bytes=mib * 1024 * 1024)


def in_hbm(x):
    return pltpu.with_memory_space_constraint(x, pltpu.HBM)


def in_vmem(x):
    return pltpu.with_memory_space_constraint(x, pltpu.VMEM)


def dot_nt(a, b):
    return lax.dot_general(a, b, (((1,), (1,)), ((), ())), preferred_element_type=F32)


def dot_nn(a, b):
    return lax.dot_general(a, b, (((1,), (0,)), ((), ())), preferred_element_type=F32)


def split_body(context_hbm, stretch_hbm, kv_ref, context_ref, stretch_ref, sem):
    copies = []
    total = context_ref.shape[0]
    step = total // 5
    for n in range(5):
        rows = pl.ds(n * step, step)
        copies.append(pltpu.make_async_copy(context_hbm.at[rows], context_ref.at[rows], sem.at[n]))
    copies.append(pltpu.make_async_copy(stretch_hbm, stretch_ref, sem.at[5]))
    for copy in copies:
        copy.start()

    def split(rows, at):
        count = rows.shape[0]
        half = count // 2
        i = lax.broadcasted_iota(jnp.int32, (count, count), 0)
        j = lax.broadcasted_iota(jnp.int32, (count, count), 1)
        source = jnp.where(i < half, 2 * i, 2 * (i - half) + 1)
        pick = jnp.where(j == source, 1.0, 0.0).astype(BF16)
        parted = dot_nn(pick, rows).astype(BF16)
        kv_ref[0, at : at + half, :] = parted[:half]
        kv_ref[1, at : at + half, :] = parted[half:]

    for n in range(5):
        copies[n].wait()
        for start in range(n * step, (n + 1) * step, 256):
            split(context_ref[start : start + 256, :], start // 2)
    copies[5].wait()
    split(stretch_ref[...], total // 2)


def split_keys_values(context, stretch):
    rows = (context.shape[0] + stretch.shape[0]) // 2
    return pl.pallas_call(
        split_body,
        out_shape=jax.ShapeDtypeStruct((2, rows, HEAD_SIZE), BF16),
        in_specs=[HBM, HBM],
        out_specs=VMEM,
        scratch_shapes=[
            pltpu.VMEM(context.shape, BF16),
            pltpu.VMEM(stretch.shape, BF16),
            pltpu.SemaphoreType.DMA((6,)),
        ],
        compiler_params=params(16),
        name="split_keys_values",
    )(in_hbm(context), in_hbm(stretch))


def question_body(
    me_ref, table_hbm, length_hbm, q_hbm, ask_ref, row_ref, rows_ref, list_ref, table_ref, length_ref, q_ref, sem
):
    copies = [
        pltpu.make_async_copy(q_hbm, q_ref, sem.at[0]),
        pltpu.make_async_copy(table_hbm, table_ref, sem.at[1]),
        pltpu.make_async_copy(length_hbm, length_ref, sem.at[2]),
    ]
    for copy in copies:
        copy.start()
    rows_dev = length_ref.shape[0]
    nblk = table_ref.shape[0]
    lists = rows_ref.shape[1]
    heads = lists // 2
    pool_dev = ask_ref.shape[0]
    copies[0].wait()
    for r in range(rows_dev):
        q = q_ref[r].astype(F32)
        for t in range(2):
            for h in range(heads):
                at = t * heads + h
                list_ref[r, at : at + 1, :] = q[t : t + 1, h * HEAD_SIZE : (h + 1) * HEAD_SIZE]
    copies[1].wait()
    copies[2].wait()
    for r in range(rows_dev):
        listed = list_ref[r]
        rows_ref[r] = listed.astype(BF16)
        asked = jnp.concatenate([listed[:heads], listed[heads:]], axis=1).astype(BF16)
        for n in range(nblk):
            holder = table_ref[n, me_ref[0] * rows_dev + r] // pool_dev
            left = jnp.clip(length_ref[r] - n * BLOCK, 0, BLOCK).astype(F32)
            ask_ref[holder, :, : 2 * HEAD_SIZE] = asked
            ask_ref[holder, :, 2 * HEAD_SIZE :] = jnp.full((heads, HEAD_SIZE), left, F32).astype(BF16)
            row_ref[holder] = r


def question(me, table, length, q, holders):
    rows_dev = length.shape[0]
    lists = 2 * q.shape[2] // HEAD_SIZE
    return pl.pallas_call(
        question_body,
        out_shape=[
            jax.ShapeDtypeStruct((holders, lists // 2, 3 * HEAD_SIZE), BF16),
            jax.ShapeDtypeStruct((holders,), jnp.int32),
            jax.ShapeDtypeStruct((rows_dev, lists, HEAD_SIZE), BF16),
        ],
        in_specs=[SMEM, HBM, HBM, HBM],
        out_specs=[VMEM, SMEM, VMEM],
        scratch_shapes=[
            pltpu.VMEM((rows_dev, lists, HEAD_SIZE), F32),
            pltpu.SMEM(table.shape, jnp.int32),
            pltpu.SMEM(length.shape, jnp.int32),
            pltpu.VMEM(q.shape, BF16),
            pltpu.SemaphoreType.DMA((3,)),
        ],
        compiler_params=params(16),
        name="question",
    )(me, in_hbm(table), in_hbm(length), in_hbm(q))


def stack_body(*refs):
    kv_refs, k_ref, v_ref = refs[:-2], refs[-2], refs[-1]
    sets = len(kv_refs)
    stretch = v_ref.shape[0] // sets - CONTEXT_DEV
    one = jnp.where(diagonal(), 1.0, 0.0).astype(BF16)
    v_ref[:, HEAD_SIZE:] = jnp.ones((v_ref.shape[0], HEAD_SIZE), BF16)
    for n, ref in enumerate(kv_refs):
        first, last = n * CONTEXT_DEV, sets * CONTEXT_DEV + n * stretch
        for at in range(0, CONTEXT_DEV, 256):
            k_ref[:, first + at : first + at + 256] = dot_nt(one, ref[0, at : at + 256, :]).astype(BF16)
        v_ref[first : first + CONTEXT_DEV, :HEAD_SIZE] = ref[1, :CONTEXT_DEV, :]
        v_ref[last : last + stretch, :HEAD_SIZE] = ref[1, CONTEXT_DEV:, :]
    k = jnp.concatenate([ref[0, CONTEXT_DEV:, :] for ref in kv_refs], axis=0)
    k_ref[:, sets * CONTEXT_DEV :] = dot_nt(one, k).astype(BF16)


def stack(sets):
    keys = len(sets) * sets[0].shape[1]
    return pl.pallas_call(
        stack_body,
        out_shape=[
            jax.ShapeDtypeStruct((HEAD_SIZE, keys), BF16),
            jax.ShapeDtypeStruct((keys, 2 * HEAD_SIZE), BF16),
        ],
        in_specs=[VMEM] * len(sets),
        out_specs=[VMEM, VMEM],
        compiler_params=params(16),
        name="stack",
    )(*sets)


def diagonal():
    i = lax.broadcasted_iota(jnp.int32, (HEAD_SIZE, HEAD_SIZE), 0)
    j = lax.broadcasted_iota(jnp.int32, (HEAD_SIZE, HEAD_SIZE), 1)
    return i == j


def read_part(ref, stretch, first, heads):
    columns = range(first * HEAD_SIZE, (first + heads) * HEAD_SIZE, HEAD_SIZE)
    outputs = jnp.concatenate([ref[:stretch, c : c + HEAD_SIZE] for c in columns], axis=0)
    stat = ref[stretch : stretch + 16, first * stretch : (first + heads) * stretch].astype(F32)
    level = stat[0:1] + stat[1:2] + stat[2:3]
    columns = []
    for g in range(0, heads * stretch, HEAD_SIZE):
        column = jnp.sum(jnp.where(diagonal(), level[:, g : g + HEAD_SIZE], 0.0), axis=1, keepdims=True)
        columns.append(jnp.broadcast_to(column, (HEAD_SIZE, HEAD_SIZE)))
    return outputs.astype(F32), jnp.concatenate(columns, axis=0)


def join(outputs, levels):
    top = functools.reduce(jnp.maximum, levels)
    weights = [jnp.exp2(level - top) for level in levels]
    total = functools.reduce(jnp.add, weights)
    mixed = functools.reduce(jnp.add, [weight * output for weight, output in zip(weights, outputs)])
    return mixed / total, top + jnp.log2(total)


def write_outputs(ref, outputs, stretch, first):
    outputs = outputs.astype(BF16)
    for h in range(outputs.shape[0] // stretch):
        ref[:stretch, (first + h) * HEAD_SIZE : (first + h + 1) * HEAD_SIZE] = outputs[h * stretch : (h + 1) * stretch]


def write_level(ref, level, stretch, first):
    rows = level.shape[0]
    lines = []
    for g in range(0, rows, HEAD_SIZE):
        lines.append(jnp.sum(jnp.where(diagonal(), level[g : g + HEAD_SIZE], 0.0), axis=0, keepdims=True))
    level = jnp.concatenate(lines, axis=1)
    high = level.astype(BF16).astype(F32)
    rest = level - high
    middle = rest.astype(BF16).astype(F32)
    row = lax.broadcasted_iota(jnp.int32, (16, rows), 0)
    stat = jnp.where(row == 0, high, jnp.where(row == 1, middle, jnp.where(row == 2, rest - middle, 0.0)))
    ref[stretch : stretch + 16, first * stretch : first * stretch + rows] = stat.astype(BF16)


def attend_body(which, arrived, riders, delta_ref, k_ref, v_ref, q_ref, *refs):
    refs = list(refs)
    part_ref = refs.pop(0) if arrived else None
    rider_ref = refs.pop(0) if riders == "own" else part_ref
    out_ref, p_ref, total_ref, top_ref = refs
    stretch, width = q_ref.shape
    sets = delta_ref.shape[1]
    keys = v_ref.shape[0]
    halves, rows = p_ref.shape[:2]
    heads = rows // stretch
    chunk = 256

    if riders is not None:
        start = 0 if riders == "own" else stretch + 16
        out_ref[stretch + 16 :, :] = rider_ref[start:, :]
    out_ref[stretch : stretch + 16, halves * rows :] = jnp.zeros((16, width - halves * rows), BF16)

    def queries(n):
        columns = range(n * heads * HEAD_SIZE, (n + 1) * heads * HEAD_SIZE, HEAD_SIZE)
        return jnp.concatenate([q_ref[:, c : c + HEAD_SIZE] for c in columns], axis=0)

    def score(q, k, masked):
        s = dot_nn(q, k)
        if masked:
            row = lax.rem(lax.broadcasted_iota(jnp.int32, s.shape, 0), stretch)
            col = lax.broadcasted_iota(jnp.int32, s.shape, 1)
            bound = delta_ref[which, sets - 1] + (sets - 1) * stretch - col
            for m in reversed(range(sets - 1)):
                bound = jnp.where(col < (m + 1) * stretch, delta_ref[which, m] + m * stretch - col, bound)
            s = jnp.where(row + bound >= 0, s, LOWEST)
        return s

    def highest(s):
        parts = [s[:, c : c + HEAD_SIZE] for c in range(0, s.shape[1], HEAD_SIZE)]
        return functools.reduce(jnp.maximum, parts)

    def spread(top):
        return jnp.broadcast_to(jnp.max(top, axis=1, keepdims=True), (rows, HEAD_SIZE)) * SCALE

    def weigh(s, top):
        parts = [s[:, c : c + HEAD_SIZE] for c in range(0, s.shape[1], HEAD_SIZE)]
        return jnp.concatenate([jnp.exp2(part * SCALE - top) for part in parts], axis=1).astype(BF16)

    def finish(n, total, top):
        weight = total[:, HEAD_SIZE:]
        output, level = total[:, :HEAD_SIZE] / weight, top + jnp.log2(weight)
        if arrived:
            other, other_level = read_part(part_ref, stretch, n * heads, heads)
            output, level = join([output, other], [level, other_level])
        write_outputs(out_ref, output, stretch, n * heads)
        write_level(out_ref, level, stretch, n * heads)

    steps = keys // chunk
    ends = [steps * chunk * n // 21 for n in (5, 10, 15, 18, 20, 21)]
    tops = [spread(highest(score(queries(n), k_ref[:, :chunk], False))) for n in range(halves)]
    sums = []
    for n in range(halves):
        q = queries(n)
        total = None
        begun = 0
        for at in range(0, keys, chunk):
            masked = at >= sets * CONTEXT_DEV
            p_ref[n, :, at : at + chunk] = weigh(score(q, k_ref[:, at : at + chunk], masked), tops[n])
            done = at + chunk
            if done in ends:
                part = dot_nn(p_ref[n, :, begun:done], v_ref[begun:done, :])
                total = part if total is None else total + part
                begun = done
        sums.append(total[:, HEAD_SIZE:])
        finish(n, total, tops[n])

    @pl.when(jnp.logical_not(jnp.max(functools.reduce(jnp.maximum, sums)) < 1e37))
    def again():
        for n in range(halves):
            q = queries(n)
            last = score(q, k_ref[:, keys - chunk :], True)

            def climb(m, top):
                k = k_ref[:, pl.ds(pl.multiple_of(m * chunk, chunk), chunk)]
                return jnp.maximum(top, highest(score(q, k, False)))

            top_ref[...] = spread(lax.fori_loop(0, steps - 1, climb, highest(last)))
            total_ref[...] = dot_nn(weigh(last, top_ref[...]), v_ref[keys - chunk :, :])

            def add(m, carry):
                at = pl.ds(pl.multiple_of(m * chunk, chunk), chunk)
                total_ref[...] += dot_nn(weigh(score(q, k_ref[:, at], False), top_ref[...]), v_ref[at, :])
                return carry

            lax.fori_loop(0, steps - 1, add, 0)
            finish(n, total_ref[...], top_ref[...])


def attend(which, deltas, queries, keys, values, part=None, rider=None, carry=True):
    stretch, width = queries.shape
    rows = width // HEAD_SIZE * stretch // 2
    count = values.shape[0]
    operands = [deltas, keys, values, queries]
    out_rows = stretch + 16
    riders = None
    if part is not None:
        operands.append(part)
        if carry:
            riders = "arrived"
            out_rows = part.shape[0]
    if rider is not None:
        riders = "own"
        operands.append(rider)
        out_rows += rider.shape[0]
    return pl.pallas_call(
        functools.partial(attend_body, which, part is not None, riders),
        out_shape=jax.ShapeDtypeStruct((out_rows, width), BF16),
        in_specs=[SMEM] + [VMEM] * (len(operands) - 1),
        out_specs=VMEM,
        scratch_shapes=[
            pltpu.VMEM((2, rows, count), BF16),
            pltpu.VMEM((rows, 2 * HEAD_SIZE), F32),
            pltpu.VMEM((rows, HEAD_SIZE), F32),
        ],
        compiler_params=params(24),
        cost_estimate=pl.CostEstimate(
            flops=16 * rows * count * HEAD_SIZE,
            bytes_accessed=4 * count * HEAD_SIZE,
            transcendentals=2 * rows * count,
        ),
        name="attend",
    )(*operands)


def merge_body(*refs):
    part_refs, out_ref = refs[:-1], refs[-1]
    stretch = out_ref.shape[0]
    read = [read_part(ref, stretch, 0, out_ref.shape[1] // HEAD_SIZE) for ref in part_refs]
    output, _ = join([x for x, _ in read], [x for _, x in read])
    write_outputs(out_ref, output, stretch, 0)


def merge(parts, stretch):
    return pl.pallas_call(
        merge_body,
        out_shape=jax.ShapeDtypeStruct((stretch, parts[0].shape[1]), BF16),
        in_specs=[VMEM] * len(parts),
        out_specs=VMEM,
        compiler_params=params(16),
        name="merge",
    )(*parts)


def fetch_body(pool_hbm, pool_ref, sem):
    copies = []
    step = pool_ref.shape[0] // sem.shape[0]
    for n in range(sem.shape[0]):
        blocks = pl.ds(n * step, step)
        copies.append(pltpu.make_async_copy(pool_hbm.at[blocks], pool_ref.at[blocks], sem.at[n]))
        copies[n].start()
    for copy in copies:
        copy.wait()


def fetch(pool):
    return pl.pallas_call(
        fetch_body,
        out_shape=pltpu.VMEM(pool.shape, BF16),
        in_specs=[HBM],
        out_specs=VMEM,
        scratch_shapes=[pltpu.SemaphoreType.DMA((4,))],
        compiler_params=params(16),
        name="fetch_blocks",
    )(in_hbm(pool))


def look_body(place_ref, ask_ref, pool_ref, out_ref, s_ref, p_ref, scale_ref):
    owners, heads = ask_ref.shape[:2]
    lists = 2 * heads
    span = pool_ref.shape[1]
    for d in range(owners):
        q = ask_ref[d, :, : 2 * HEAD_SIZE].astype(F32)
        q = jnp.concatenate([q[:, :HEAD_SIZE], q[:, HEAD_SIZE:]], axis=0).astype(BF16)
        s_ref[d * lists : (d + 1) * lists, :] = dot_nt(q, pool_ref[place_ref[d]])
    col = lax.broadcasted_iota(jnp.int32, (lists, span), 1)
    lane = lax.broadcasted_iota(jnp.int32, (heads, HEAD_SIZE), 1)
    even = (col & 1) == 0
    for d in range(owners):
        limit = ask_ref[d, :, 2 * HEAD_SIZE :].astype(F32) * 2.0
        limit = jnp.concatenate([limit] * 2, axis=0)
        limit = jnp.concatenate([limit] * (span // HEAD_SIZE), axis=1)
        allowed = even & (col.astype(F32) < limit)
        s = jnp.where(allowed, s_ref[d * lists : (d + 1) * lists, :], LOWEST)
        top = jnp.max(s, axis=1, keepdims=True)
        p = jnp.where(allowed, jnp.exp2((s - top) * SCALE), 0.0)
        total = jnp.sum(p, axis=1, keepdims=True)
        p_ref[d * lists : (d + 1) * lists, :] = pltpu.roll(p, 1, 1).astype(BF16)
        seen = total > 0.0
        level = jnp.where(seen, top * SCALE + jnp.log2(jnp.where(seen, total, 1.0)), LOWEST)
        level = jnp.broadcast_to(level, (lists, HEAD_SIZE))
        high = level.astype(BF16).astype(F32)
        rest = level - high
        middle = rest.astype(BF16).astype(F32)
        stat = jnp.zeros((heads, HEAD_SIZE), F32)
        for t in range(2):
            for n, piece in enumerate((high, middle, rest - middle)):
                stat = jnp.where(lane == 3 * t + n, piece[t * heads : (t + 1) * heads], stat)
        out_ref[d, :, 2 * HEAD_SIZE :] = stat.astype(BF16)
        scale_ref[d * lists : (d + 1) * lists, :] = jnp.broadcast_to(
            jnp.where(seen, 1.0 / jnp.where(seen, total, 1.0), 0.0), (lists, HEAD_SIZE)
        )
    for d in range(owners):
        o = dot_nn(p_ref[d * lists : (d + 1) * lists, :], pool_ref[place_ref[d]])
        o = o * scale_ref[d * lists : (d + 1) * lists, :]
        out_ref[d, :, : 2 * HEAD_SIZE] = jnp.concatenate([o[:heads], o[heads:]], axis=1).astype(BF16)


def look(place, ask, pool):
    owners, heads, width = ask.shape
    span = pool.shape[1]
    rows = 2 * owners * heads
    return pl.pallas_call(
        look_body,
        out_shape=jax.ShapeDtypeStruct(ask.shape, BF16),
        in_specs=[SMEM, VMEM, VMEM],
        out_specs=VMEM,
        scratch_shapes=[
            pltpu.VMEM((rows, span), F32),
            pltpu.VMEM((rows, span), BF16),
            pltpu.VMEM((rows, HEAD_SIZE), F32),
        ],
        compiler_params=params(24),
        cost_estimate=pl.CostEstimate(
            flops=4 * rows * span * HEAD_SIZE, bytes_accessed=2 * owners * span * HEAD_SIZE, transcendentals=0
        ),
        name="look_in_blocks",
    )(place, ask, pool)


def gather_body(row_ref, answer_ref, q_ref, new_ref, out_ref, level_ref, top_ref, sum_ref, acc_ref, flat_ref):
    holders = answer_ref.shape[0]
    rows, lists = q_ref.shape[0], q_ref.shape[1]
    heads = lists // 2
    lane = lax.broadcasted_iota(jnp.int32, (lists, HEAD_SIZE), 1)
    later = lax.broadcasted_iota(jnp.int32, (lists, HEAD_SIZE), 0) >= heads
    own = []
    for r in range(rows):
        q = q_ref[r].astype(F32)
        new = new_ref[r].astype(F32)
        scores = []
        for t in range(2):
            s = jnp.sum(q * new[2 * t : 2 * t + 1, :], axis=1, keepdims=True) * SCALE
            scores.append(jnp.broadcast_to(s, (lists, HEAD_SIZE)))
        scores[1] = jnp.where(later, scores[1], LOWEST)
        top_ref[r] = jnp.maximum(scores[0], scores[1])
        own.append((scores, new))
    for d in range(holders):
        stat = answer_ref[d, :, 2 * HEAD_SIZE :].astype(F32)
        stat = jnp.concatenate([stat, stat], axis=0)
        level = jnp.sum(jnp.where((lane < 6) & ((lane >= 3) == later), stat, 0.0), axis=1, keepdims=True)
        level_ref[d] = jnp.broadcast_to(level, (lists, HEAD_SIZE))
    for d in range(holders):
        r = row_ref[d]
        top_ref[r] = jnp.maximum(top_ref[r], level_ref[d])
    for r in range(rows):
        scores, new = own[r]
        first = jnp.exp2(scores[0] - top_ref[r])
        second = jnp.exp2(scores[1] - top_ref[r])
        sum_ref[r] = first + second
        acc_ref[r] = first * new[1:2, :] + second * new[3:4, :]
    for d in range(holders):
        r = row_ref[d]
        weight = jnp.exp2(level_ref[d] - top_ref[r])
        sum_ref[r] = sum_ref[r] + weight
        o = answer_ref[d, :, : 2 * HEAD_SIZE].astype(F32)
        o = jnp.concatenate([o[:, :HEAD_SIZE], o[:, HEAD_SIZE:]], axis=0)
        acc_ref[r] = acc_ref[r] + weight * o
    for r in range(rows):
        o = acc_ref[r] / sum_ref[r]
        for t in range(2):
            for h in range(heads):
                flat_ref[2 * r + t : 2 * r + t + 1, h * HEAD_SIZE : (h + 1) * HEAD_SIZE] = o[
                    t * heads + h : t * heads + h + 1, :
                ]
    out_ref[...] = flat_ref[...].astype(BF16)


def gather_answers(row_of, answer, q, new):
    rows, lists, width = q.shape
    holders = answer.shape[0]
    heads = lists // 2
    state = pltpu.VMEM((rows, lists, width), F32)
    return pl.pallas_call(
        gather_body,
        out_shape=jax.ShapeDtypeStruct((2 * rows, heads * width), BF16),
        in_specs=[SMEM, VMEM, VMEM, VMEM],
        out_specs=VMEM,
        scratch_shapes=[
            pltpu.VMEM((holders, lists, width), F32),
            state,
            state,
            state,
            pltpu.VMEM((2 * rows, heads * width), F32),
        ],
        compiler_params=params(16),
        name="gather_answers",
    )(row_of, answer, q, new)


def project_body(place_ref, own_ref, w_ref, *refs):
    ref_list, out_ref, total_ref, rows_ref = refs[:-3], refs[-3], refs[-2], refs[-1]
    rows = own_ref.shape[0]
    rows_ref[:rows, :] = own_ref[...]
    for n, ref in enumerate(ref_list):
        rows_ref[(n + 1) * rows : (n + 2) * rows, :] = ref[ref.shape[0] - rows :, :]
    total = dot_nn(rows_ref[...], w_ref[...])
    for n in range(rows_ref.shape[0] // 8):
        at = pl.multiple_of(place_ref[n], 8)
        total_ref[pl.ds(at, 8), :] = total[8 * n : 8 * n + 8]
    out_ref[...] = total_ref[...].astype(BF16)


def project(place, own, w, parts):
    rows = own.shape[0] * (len(parts) + 1)
    return pl.pallas_call(
        project_body,
        out_shape=jax.ShapeDtypeStruct((rows, w.shape[1]), BF16),
        in_specs=[SMEM] + [VMEM] * (len(parts) + 2),
        out_specs=VMEM,
        scratch_shapes=[pltpu.VMEM((rows, w.shape[1]), F32), pltpu.VMEM((rows, own.shape[1]), BF16)],
        compiler_params=params(16),
        name="project",
    )(place, own, w, *parts)


def shards(
    q_stretch,
    stretch_key_value,
    context_key_value,
    dec_q,
    dec_new,
    pool_key_value,
    block_table,
    cache_len,
    w_out,
):
    me = lax.axis_index(CTX)
    z = lax.axis_index("z")
    cycle = lax.axis_size(CTX)
    stretch = q_stretch.shape[0]
    rows_dev, nblk = dec_q.shape[0], block_table.shape[1]
    pool_dev, block_size = pool_key_value.shape[:2]

    def after(x, *others):
        return lax.optimization_barrier((x, *others))[0]

    def swap(x, name):
        return lax.ppermute(x, name, [(0, 1), (1, 0)])

    def turn(x, step):
        return lax.ppermute(x, "z", [(n, (n + step) % Z_CHIPS) for n in range(Z_CHIPS)])

    ask, row_of, q_rows = question(me.reshape(1).astype(jnp.int32), block_table.T, cache_len, dec_q, cycle)
    pool, q_stretch, ask = lax.optimization_barrier((pool_key_value, q_stretch, ask))
    ask = lax.all_to_all(ask, CTX, split_axis=0, concat_axis=0, tiled=True)
    table = block_table.reshape(cycle, rows_dev * nblk)
    place = jnp.sum(jnp.where(table // pool_dev == me, table % pool_dev, 0), axis=1)

    right, left = [q_stretch] + [None] * 4, [q_stretch] + [None] * 3
    right[1], right[4], left[3] = turn(q_stretch, 1), turn(q_stretch, 4), turn(q_stretch, -3)
    right[3], left[2] = turn(q_stretch, 3), turn(q_stretch, -2)
    context, fresh, right[1] = lax.optimization_barrier((context_key_value, stretch_key_value, right[1]))
    kv = split_keys_values(context.reshape(-1, HEAD_SIZE), fresh.reshape(-1, HEAD_SIZE))
    kv_core, kv_y = swap(kv, "core"), swap(kv, "y")
    blocks = fetch(pool.reshape(pool_dev, 2 * block_size, HEAD_SIZE))
    look_out = look(place, after(ask, kv), blocks)
    answer = lax.all_to_all(look_out, CTX, split_axis=0, concat_axis=0, tiled=True)
    near = after(q_stretch, look_out)
    right[2], left[1] = turn(near, 2), turn(near, -1)
    kv_yc = swap(after(kv_y, look_out), "core")
    kv_yc, answer = lax.optimization_barrier((kv_yc, answer))
    attn = gather_answers(row_of, answer, q_rows, dec_new.reshape(rows_dev, 4, HEAD_SIZE))
    attn_core = swap(attn, "core")
    sets, _ = lax.optimization_barrier(([kv, kv_core, kv_y, kv_yc], attn))
    keys, values = stack(sets)
    pair = jnp.concatenate([attn, attn_core], axis=0)
    pair_y = swap(pair, "y")

    shifts = jnp.arange(Z_CHIPS, dtype=jnp.int32)
    corners = jnp.arange(2 * CORES, dtype=jnp.int32)
    corners = me ^ (corners // CORES * CORES * Z_CHIPS + corners % CORES)
    askers = me + ((z - shifts + Z_CHIPS) % Z_CHIPS - z) * CORES
    deltas = (askers[:, None] - corners[None, :]) * stretch

    def go(shift, previous, part=None, rider=None, carry=True):
        queries = right[shift] if shift >= 0 else left[-shift]
        return attend(shift % Z_CHIPS, after(deltas, *previous), queries, keys, values, part, rider, carry)

    own = go(0, [pair])
    attn = jnp.concatenate([pair, pair_y], axis=0)
    out = go(4, [own], None, attn)
    from_right = [turn(out, -1)]
    out = go(-3, [out], None, attn)
    from_left = [turn(out, 1)]
    out = go(3, [out], from_right[-1])
    from_right.append(turn(out, -1))
    out = go(-2, [out], from_left[-1])
    from_left.append(turn(out, 1))
    out = go(2, [out], from_right[-1])
    from_right.append(turn(out, -1))
    out = go(-1, [out], from_left[-1])
    from_left.append(turn(out, 1))
    rest = from_right[2][stretch + 16 :]
    farthest = turn(rest, -1)
    out = go(1, [out, rest], from_right[2], None, False)
    last = turn(out, -1)

    relative = jnp.where(shifts > Z_CHIPS // 2, Z_CHIPS // 2 - shifts, shifts)
    there = ((z + relative + Z_CHIPS) % Z_CHIPS - z) * CORES
    holders = ((there[:, None] + corners[None, :]) * (2 * rows_dev)).reshape(-1)
    partial_out = project(holders, after(attn, out), w_out, [*from_right, farthest, *from_left])
    shares = lax.axis_size(("grp", "tp"))
    pieces = lax.all_to_all(
        partial_out.reshape(shares, -1, partial_out.shape[1]), ("grp", "tp"), split_axis=0, concat_axis=0, tiled=True
    )
    pre_out = merge([own, last, from_left[2]], stretch)
    dec_out = jnp.sum(pieces.astype(F32), axis=0).astype(BF16)
    return (pre_out, dec_out.reshape(-1, 2, dec_out.shape[1]))


def solution(mesh):
    shape = mesh.devices.shape
    fine = jax.sharding.Mesh(mesh.devices.reshape(-1, Z_CHIPS, CORES, *shape[1:]), (*CTX, *mesh.axis_names[1:]))
    placed = (
        P(CTX, ("grp", "tp")),
        P(CTX, None, ("grp", "tp")),
        P(CTX, None, ("grp", "tp")),
        P(CTX, None, ("grp", "tp")),
        P(CTX, None, None, ("grp", "tp")),
        P(CTX, None, None, ("grp", "tp")),
        P(),
        P(CTX),
        P(("grp", "tp"), CTX),
    )
    return jax.shard_map(
        shards,
        mesh=fine,
        in_specs=placed,
        out_specs=(P(CTX, ("grp", "tp")), P(("grp", "tp"), None, CTX)),
        check_vma=False,
    )
```

```python
import functools
import math

import jax
import jax.numpy as jnp
from jax import lax
from jax.experimental import pallas as pl
from jax.experimental.pallas import tpu as pltpu
from jax.sharding import PartitionSpec as P

HEAD_SIZE = 128
CORES = 2
Z_CHIPS = 8
CONTEXT_DEV = 1280
BLOCK = 128
CTX = ("y", "z", "core")
SCALE = math.log2(math.e) / math.sqrt(HEAD_SIZE)
LOWEST = -1e30
F32 = jnp.float32
BF16 = jnp.bfloat16
VMEM = pl.BlockSpec(memory_space=pltpu.VMEM)
SMEM = pl.BlockSpec(memory_space=pltpu.SMEM)
HBM = pl.BlockSpec(memory_space=pltpu.HBM)


def params(mib):
    return pltpu.CompilerParams(vmem_limit_bytes=mib * 1024 * 1024)


def in_hbm(x):
    return pltpu.with_memory_space_constraint(x, pltpu.HBM)


def in_vmem(x):
    return pltpu.with_memory_space_constraint(x, pltpu.VMEM)


def dot_nt(a, b):
    return lax.dot_general(a, b, (((1,), (1,)), ((), ())), preferred_element_type=F32)


def dot_nn(a, b):
    return lax.dot_general(a, b, (((1,), (0,)), ((), ())), preferred_element_type=F32)


def prepare_body(
    me_ref,
    table_hbm,
    length_hbm,
    q_hbm,
    context_hbm,
    stretch_hbm,
    ask_ref,
    row_ref,
    rows_ref,
    kv_ref,
    list_ref,
    table_ref,
    length_ref,
    q_ref,
    context_ref,
    stretch_ref,
    sem,
):
    pieces = 5
    total = context_ref.shape[0]
    step = total // pieces
    copies = [
        pltpu.make_async_copy(q_hbm, q_ref, sem.at[0]),
        pltpu.make_async_copy(table_hbm, table_ref, sem.at[1]),
        pltpu.make_async_copy(length_hbm, length_ref, sem.at[2]),
    ]
    for n in range(pieces):
        rows = pl.ds(n * step, step)
        copies.append(pltpu.make_async_copy(context_hbm.at[rows], context_ref.at[rows], sem.at[3 + n]))
    copies.append(pltpu.make_async_copy(stretch_hbm, stretch_ref, sem.at[3 + pieces]))
    for copy in copies:
        copy.start()

    rows_dev = length_ref.shape[0]
    nblk = table_ref.shape[0]
    lists = rows_ref.shape[1]
    heads = lists // 2
    pool_dev = ask_ref.shape[0]
    copies[0].wait()
    for r in range(rows_dev):
        q = q_ref[r].astype(F32)
        for t in range(2):
            for h in range(heads):
                at = t * heads + h
                list_ref[r, at : at + 1, :] = q[t : t + 1, h * HEAD_SIZE : (h + 1) * HEAD_SIZE]
    copies[1].wait()
    copies[2].wait()
    for r in range(rows_dev):
        listed = list_ref[r]
        rows_ref[r] = listed.astype(BF16)
        asked = jnp.concatenate([listed[:heads], listed[heads:]], axis=1).astype(BF16)
        for n in range(nblk):
            holder = table_ref[n, me_ref[0] * rows_dev + r] // pool_dev
            left = jnp.clip(length_ref[r] - n * BLOCK, 0, BLOCK).astype(F32)
            ask_ref[holder, :, : 2 * HEAD_SIZE] = asked
            ask_ref[holder, :, 2 * HEAD_SIZE :] = jnp.full((heads, HEAD_SIZE), left, F32).astype(BF16)
            row_ref[holder] = r

    def split(rows, at):
        count = rows.shape[0]
        half = count // 2
        i = lax.broadcasted_iota(jnp.int32, (count, count), 0)
        j = lax.broadcasted_iota(jnp.int32, (count, count), 1)
        source = jnp.where(i < half, 2 * i, 2 * (i - half) + 1)
        pick = jnp.where(j == source, 1.0, 0.0).astype(BF16)
        parted = dot_nn(pick, rows).astype(BF16)
        kv_ref[0, at : at + half, :] = parted[:half]
        kv_ref[1, at : at + half, :] = parted[half:]

    for copy in copies[3:]:
        copy.wait()
    for start in range(0, total, 256):
        split(context_ref[start : start + 256, :], start // 2)
    split(stretch_ref[...], total // 2)


def prepare(me, table, length, q, context, stretch, holders):
    rows_dev = length.shape[0]
    lists = 2 * q.shape[2] // HEAD_SIZE
    rows = (context.shape[0] + stretch.shape[0]) // 2
    return pl.pallas_call(
        prepare_body,
        out_shape=[
            jax.ShapeDtypeStruct((holders, lists // 2, 3 * HEAD_SIZE), BF16),
            jax.ShapeDtypeStruct((holders,), jnp.int32),
            jax.ShapeDtypeStruct((rows_dev, lists, HEAD_SIZE), BF16),
            jax.ShapeDtypeStruct((2, rows, HEAD_SIZE), BF16),
        ],
        in_specs=[SMEM] + [HBM] * 5,
        out_specs=[VMEM, SMEM, VMEM, VMEM],
        scratch_shapes=[
            pltpu.VMEM((rows_dev, lists, HEAD_SIZE), F32),
            pltpu.SMEM(table.shape, jnp.int32),
            pltpu.SMEM(length.shape, jnp.int32),
            pltpu.VMEM(q.shape, BF16),
            pltpu.VMEM(context.shape, BF16),
            pltpu.VMEM(stretch.shape, BF16),
            pltpu.SemaphoreType.DMA((9,)),
        ],
        compiler_params=params(16),
        name="prepare",
    )(me, *(in_hbm(x) for x in (table, length, q, context, stretch)))


def stack_body(*refs):
    kv_refs, k_ref, v_ref = refs[:-2], refs[-2], refs[-1]
    sets = len(kv_refs)
    stretch = v_ref.shape[0] // sets - CONTEXT_DEV
    one = jnp.where(diagonal(), 1.0, 0.0).astype(BF16)
    v_ref[:, HEAD_SIZE:] = jnp.ones((v_ref.shape[0], HEAD_SIZE), BF16)
    for n, ref in enumerate(kv_refs):
        first, last = n * CONTEXT_DEV, sets * CONTEXT_DEV + n * stretch
        for at in range(0, CONTEXT_DEV, 256):
            k_ref[:, first + at : first + at + 256] = dot_nt(one, ref[0, at : at + 256, :]).astype(BF16)
        v_ref[first : first + CONTEXT_DEV, :HEAD_SIZE] = ref[1, :CONTEXT_DEV, :]
        v_ref[last : last + stretch, :HEAD_SIZE] = ref[1, CONTEXT_DEV:, :]
    k = jnp.concatenate([ref[0, CONTEXT_DEV:, :] for ref in kv_refs], axis=0)
    k_ref[:, sets * CONTEXT_DEV :] = dot_nt(one, k).astype(BF16)


def stack(sets):
    keys = len(sets) * sets[0].shape[1]
    return pl.pallas_call(
        stack_body,
        out_shape=[
            jax.ShapeDtypeStruct((HEAD_SIZE, keys), BF16),
            jax.ShapeDtypeStruct((keys, 2 * HEAD_SIZE), BF16),
        ],
        in_specs=[VMEM] * len(sets),
        out_specs=[VMEM, VMEM],
        compiler_params=params(16),
        name="stack",
    )(*sets)


def diagonal():
    i = lax.broadcasted_iota(jnp.int32, (HEAD_SIZE, HEAD_SIZE), 0)
    j = lax.broadcasted_iota(jnp.int32, (HEAD_SIZE, HEAD_SIZE), 1)
    return i == j


def read_part(ref, stretch, first, heads):
    columns = range(first * HEAD_SIZE, (first + heads) * HEAD_SIZE, HEAD_SIZE)
    outputs = jnp.concatenate([ref[:stretch, c : c + HEAD_SIZE] for c in columns], axis=0)
    stat = ref[stretch : stretch + 16, first * stretch : (first + heads) * stretch].astype(F32)
    level = stat[0:1] + stat[1:2] + stat[2:3]
    columns = []
    for g in range(0, heads * stretch, HEAD_SIZE):
        column = jnp.sum(jnp.where(diagonal(), level[:, g : g + HEAD_SIZE], 0.0), axis=1, keepdims=True)
        columns.append(jnp.broadcast_to(column, (HEAD_SIZE, HEAD_SIZE)))
    return outputs.astype(F32), jnp.concatenate(columns, axis=0)


def join(outputs, levels):
    top = functools.reduce(jnp.maximum, levels)
    weights = [jnp.exp2(level - top) for level in levels]
    total = functools.reduce(jnp.add, weights)
    mixed = functools.reduce(jnp.add, [weight * output for weight, output in zip(weights, outputs)])
    return mixed / total, top + jnp.log2(total)


def write_outputs(ref, outputs, stretch, first):
    outputs = outputs.astype(BF16)
    for h in range(outputs.shape[0] // stretch):
        ref[:stretch, (first + h) * HEAD_SIZE : (first + h + 1) * HEAD_SIZE] = outputs[h * stretch : (h + 1) * stretch]


def write_level(ref, level, stretch, first):
    rows = level.shape[0]
    lines = []
    for g in range(0, rows, HEAD_SIZE):
        lines.append(jnp.sum(jnp.where(diagonal(), level[g : g + HEAD_SIZE], 0.0), axis=0, keepdims=True))
    level = jnp.concatenate(lines, axis=1)
    high = level.astype(BF16).astype(F32)
    rest = level - high
    middle = rest.astype(BF16).astype(F32)
    row = lax.broadcasted_iota(jnp.int32, (16, rows), 0)
    stat = jnp.where(row == 0, high, jnp.where(row == 1, middle, jnp.where(row == 2, rest - middle, 0.0)))
    ref[stretch : stretch + 16, first * stretch : first * stretch + rows] = stat.astype(BF16)


def attend_body(which, arrived, riders, delta_ref, k_ref, v_ref, q_ref, *refs):
    refs = list(refs)
    part_ref = refs.pop(0) if arrived else None
    rider_ref = refs.pop(0) if riders == "own" else part_ref
    out_ref, p_ref, total_ref, top_ref = refs
    stretch, width = q_ref.shape
    sets = delta_ref.shape[1]
    keys = v_ref.shape[0]
    halves, rows = p_ref.shape[:2]
    heads = rows // stretch
    chunk = 256

    if riders is not None:
        start = 0 if riders == "own" else stretch + 16
        out_ref[stretch + 16 :, :] = rider_ref[start:, :]
    out_ref[stretch : stretch + 16, halves * rows :] = jnp.zeros((16, width - halves * rows), BF16)

    def queries(n):
        columns = range(n * heads * HEAD_SIZE, (n + 1) * heads * HEAD_SIZE, HEAD_SIZE)
        return jnp.concatenate([q_ref[:, c : c + HEAD_SIZE] for c in columns], axis=0)

    def score(q, k, masked):
        s = dot_nn(q, k)
        if masked:
            row = lax.rem(lax.broadcasted_iota(jnp.int32, s.shape, 0), stretch)
            col = lax.broadcasted_iota(jnp.int32, s.shape, 1)
            bound = delta_ref[which, sets - 1] + (sets - 1) * stretch - col
            for m in reversed(range(sets - 1)):
                bound = jnp.where(col < (m + 1) * stretch, delta_ref[which, m] + m * stretch - col, bound)
            s = jnp.where(row + bound >= 0, s, LOWEST)
        return s

    def highest(s):
        parts = [s[:, c : c + HEAD_SIZE] for c in range(0, s.shape[1], HEAD_SIZE)]
        return functools.reduce(jnp.maximum, parts)

    def spread(top):
        return jnp.broadcast_to(jnp.max(top, axis=1, keepdims=True), (rows, HEAD_SIZE)) * SCALE

    def weigh(s, top):
        parts = [s[:, c : c + HEAD_SIZE] for c in range(0, s.shape[1], HEAD_SIZE)]
        return jnp.concatenate([jnp.exp2(part * SCALE - top) for part in parts], axis=1).astype(BF16)

    def finish(n, total, top):
        weight = total[:, HEAD_SIZE:]
        output, level = total[:, :HEAD_SIZE] / weight, top + jnp.log2(weight)
        if arrived:
            other, other_level = read_part(part_ref, stretch, n * heads, heads)
            output, level = join([output, other], [level, other_level])
        write_outputs(out_ref, output, stretch, n * heads)
        write_level(out_ref, level, stretch, n * heads)

    steps = keys // chunk
    ends = [steps * chunk * n // 21 for n in (5, 10, 15, 18, 20, 21)]
    tops = [spread(highest(score(queries(n), k_ref[:, :chunk], False))) for n in range(halves)]
    sums = []
    for n in range(halves):
        q = queries(n)
        total = None
        begun = 0
        for at in range(0, keys, chunk):
            masked = at >= sets * CONTEXT_DEV
            p_ref[n, :, at : at + chunk] = weigh(score(q, k_ref[:, at : at + chunk], masked), tops[n])
            done = at + chunk
            if done in ends:
                part = dot_nn(p_ref[n, :, begun:done], v_ref[begun:done, :])
                total = part if total is None else total + part
                begun = done
        sums.append(total[:, HEAD_SIZE:])
        finish(n, total, tops[n])

    @pl.when(jnp.logical_not(jnp.max(functools.reduce(jnp.maximum, sums)) < 1e37))
    def again():
        for n in range(halves):
            q = queries(n)
            last = score(q, k_ref[:, keys - chunk :], True)

            def climb(m, top):
                k = k_ref[:, pl.ds(pl.multiple_of(m * chunk, chunk), chunk)]
                return jnp.maximum(top, highest(score(q, k, False)))

            top_ref[...] = spread(lax.fori_loop(0, steps - 1, climb, highest(last)))
            total_ref[...] = dot_nn(weigh(last, top_ref[...]), v_ref[keys - chunk :, :])

            def add(m, carry):
                at = pl.ds(pl.multiple_of(m * chunk, chunk), chunk)
                total_ref[...] += dot_nn(weigh(score(q, k_ref[:, at], False), top_ref[...]), v_ref[at, :])
                return carry

            lax.fori_loop(0, steps - 1, add, 0)
            finish(n, total_ref[...], top_ref[...])


def attend(which, deltas, queries, keys, values, part=None, rider=None, carry=True):
    stretch, width = queries.shape
    rows = width // HEAD_SIZE * stretch // 2
    count = values.shape[0]
    operands = [deltas, keys, values, queries]
    out_rows = stretch + 16
    riders = None
    if part is not None:
        operands.append(part)
        if carry:
            riders = "arrived"
            out_rows = part.shape[0]
    if rider is not None:
        riders = "own"
        operands.append(rider)
        out_rows += rider.shape[0]
    return pl.pallas_call(
        functools.partial(attend_body, which, part is not None, riders),
        out_shape=jax.ShapeDtypeStruct((out_rows, width), BF16),
        in_specs=[SMEM] + [VMEM] * (len(operands) - 1),
        out_specs=VMEM,
        scratch_shapes=[
            pltpu.VMEM((2, rows, count), BF16),
            pltpu.VMEM((rows, 2 * HEAD_SIZE), F32),
            pltpu.VMEM((rows, HEAD_SIZE), F32),
        ],
        compiler_params=params(24),
        cost_estimate=pl.CostEstimate(
            flops=16 * rows * count * HEAD_SIZE,
            bytes_accessed=4 * count * HEAD_SIZE,
            transcendentals=2 * rows * count,
        ),
        name="attend",
    )(*operands)


def merge_body(*refs):
    part_refs, out_ref = refs[:-1], refs[-1]
    stretch = out_ref.shape[0]
    read = [read_part(ref, stretch, 0, out_ref.shape[1] // HEAD_SIZE) for ref in part_refs]
    output, _ = join([x for x, _ in read], [x for _, x in read])
    write_outputs(out_ref, output, stretch, 0)


def merge(parts, stretch):
    return pl.pallas_call(
        merge_body,
        out_shape=jax.ShapeDtypeStruct((stretch, parts[0].shape[1]), BF16),
        in_specs=[VMEM] * len(parts),
        out_specs=VMEM,
        compiler_params=params(16),
        name="merge",
    )(*parts)


def fetch_body(pool_hbm, pool_ref, sem):
    copies = []
    step = pool_ref.shape[0] // sem.shape[0]
    for n in range(sem.shape[0]):
        blocks = pl.ds(n * step, step)
        copies.append(pltpu.make_async_copy(pool_hbm.at[blocks], pool_ref.at[blocks], sem.at[n]))
        copies[n].start()
    for copy in copies:
        copy.wait()


def fetch(pool):
    return pl.pallas_call(
        fetch_body,
        out_shape=pltpu.VMEM(pool.shape, BF16),
        in_specs=[HBM],
        out_specs=VMEM,
        scratch_shapes=[pltpu.SemaphoreType.DMA((4,))],
        compiler_params=params(16),
        name="fetch_blocks",
    )(in_hbm(pool))


def look_body(place_ref, ask_ref, pool_ref, out_ref, s_ref, p_ref, scale_ref):
    owners, heads = ask_ref.shape[:2]
    lists = 2 * heads
    span = pool_ref.shape[1]
    for d in range(owners):
        q = ask_ref[d, :, : 2 * HEAD_SIZE].astype(F32)
        q = jnp.concatenate([q[:, :HEAD_SIZE], q[:, HEAD_SIZE:]], axis=0).astype(BF16)
        s_ref[d * lists : (d + 1) * lists, :] = dot_nt(q, pool_ref[place_ref[d]])
    col = lax.broadcasted_iota(jnp.int32, (lists, span), 1)
    lane = lax.broadcasted_iota(jnp.int32, (heads, HEAD_SIZE), 1)
    even = (col & 1) == 0
    for d in range(owners):
        limit = ask_ref[d, :, 2 * HEAD_SIZE :].astype(F32) * 2.0
        limit = jnp.concatenate([limit] * 2, axis=0)
        limit = jnp.concatenate([limit] * (span // HEAD_SIZE), axis=1)
        allowed = even & (col.astype(F32) < limit)
        s = jnp.where(allowed, s_ref[d * lists : (d + 1) * lists, :], LOWEST)
        top = jnp.max(s, axis=1, keepdims=True)
        p = jnp.where(allowed, jnp.exp2((s - top) * SCALE), 0.0)
        total = jnp.sum(p, axis=1, keepdims=True)
        p_ref[d * lists : (d + 1) * lists, :] = pltpu.roll(p, 1, 1).astype(BF16)
        seen = total > 0.0
        level = jnp.where(seen, top * SCALE + jnp.log2(jnp.where(seen, total, 1.0)), LOWEST)
        level = jnp.broadcast_to(level, (lists, HEAD_SIZE))
        high = level.astype(BF16).astype(F32)
        rest = level - high
        middle = rest.astype(BF16).astype(F32)
        stat = jnp.zeros((heads, HEAD_SIZE), F32)
        for t in range(2):
            for n, piece in enumerate((high, middle, rest - middle)):
                stat = jnp.where(lane == 3 * t + n, piece[t * heads : (t + 1) * heads], stat)
        out_ref[d, :, 2 * HEAD_SIZE :] = stat.astype(BF16)
        scale_ref[d * lists : (d + 1) * lists, :] = jnp.broadcast_to(
            jnp.where(seen, 1.0 / jnp.where(seen, total, 1.0), 0.0), (lists, HEAD_SIZE)
        )
    for d in range(owners):
        o = dot_nn(p_ref[d * lists : (d + 1) * lists, :], pool_ref[place_ref[d]])
        o = o * scale_ref[d * lists : (d + 1) * lists, :]
        out_ref[d, :, : 2 * HEAD_SIZE] = jnp.concatenate([o[:heads], o[heads:]], axis=1).astype(BF16)


def look(place, ask, pool):
    owners, heads, width = ask.shape
    span = pool.shape[1]
    rows = 2 * owners * heads
    return pl.pallas_call(
        look_body,
        out_shape=jax.ShapeDtypeStruct(ask.shape, BF16),
        in_specs=[SMEM, VMEM, VMEM],
        out_specs=VMEM,
        scratch_shapes=[
            pltpu.VMEM((rows, span), F32),
            pltpu.VMEM((rows, span), BF16),
            pltpu.VMEM((rows, HEAD_SIZE), F32),
        ],
        compiler_params=params(24),
        cost_estimate=pl.CostEstimate(
            flops=4 * rows * span * HEAD_SIZE, bytes_accessed=2 * owners * span * HEAD_SIZE, transcendentals=0
        ),
        name="look_in_blocks",
    )(place, ask, pool)


def gather_body(row_ref, answer_ref, q_ref, new_ref, out_ref, level_ref, top_ref, sum_ref, acc_ref, flat_ref):
    holders = answer_ref.shape[0]
    rows, lists = q_ref.shape[0], q_ref.shape[1]
    heads = lists // 2
    lane = lax.broadcasted_iota(jnp.int32, (lists, HEAD_SIZE), 1)
    later = lax.broadcasted_iota(jnp.int32, (lists, HEAD_SIZE), 0) >= heads
    own = []
    for r in range(rows):
        q = q_ref[r].astype(F32)
        new = new_ref[r].astype(F32)
        scores = []
        for t in range(2):
            s = jnp.sum(q * new[2 * t : 2 * t + 1, :], axis=1, keepdims=True) * SCALE
            scores.append(jnp.broadcast_to(s, (lists, HEAD_SIZE)))
        scores[1] = jnp.where(later, scores[1], LOWEST)
        top_ref[r] = jnp.maximum(scores[0], scores[1])
        own.append((scores, new))
    for d in range(holders):
        stat = answer_ref[d, :, 2 * HEAD_SIZE :].astype(F32)
        stat = jnp.concatenate([stat, stat], axis=0)
        level = jnp.sum(jnp.where((lane < 6) & ((lane >= 3) == later), stat, 0.0), axis=1, keepdims=True)
        level_ref[d] = jnp.broadcast_to(level, (lists, HEAD_SIZE))
    for d in range(holders):
        r = row_ref[d]
        top_ref[r] = jnp.maximum(top_ref[r], level_ref[d])
    for r in range(rows):
        scores, new = own[r]
        first = jnp.exp2(scores[0] - top_ref[r])
        second = jnp.exp2(scores[1] - top_ref[r])
        sum_ref[r] = first + second
        acc_ref[r] = first * new[1:2, :] + second * new[3:4, :]
    for d in range(holders):
        r = row_ref[d]
        weight = jnp.exp2(level_ref[d] - top_ref[r])
        sum_ref[r] = sum_ref[r] + weight
        o = answer_ref[d, :, : 2 * HEAD_SIZE].astype(F32)
        o = jnp.concatenate([o[:, :HEAD_SIZE], o[:, HEAD_SIZE:]], axis=0)
        acc_ref[r] = acc_ref[r] + weight * o
    for r in range(rows):
        o = acc_ref[r] / sum_ref[r]
        for t in range(2):
            for h in range(heads):
                flat_ref[2 * r + t : 2 * r + t + 1, h * HEAD_SIZE : (h + 1) * HEAD_SIZE] = o[
                    t * heads + h : t * heads + h + 1, :
                ]
    out_ref[...] = flat_ref[...].astype(BF16)


def gather_answers(row_of, answer, q, new):
    rows, lists, width = q.shape
    holders = answer.shape[0]
    heads = lists // 2
    state = pltpu.VMEM((rows, lists, width), F32)
    return pl.pallas_call(
        gather_body,
        out_shape=jax.ShapeDtypeStruct((2 * rows, heads * width), BF16),
        in_specs=[SMEM, VMEM, VMEM, VMEM],
        out_specs=VMEM,
        scratch_shapes=[
            pltpu.VMEM((holders, lists, width), F32),
            state,
            state,
            state,
            pltpu.VMEM((2 * rows, heads * width), F32),
        ],
        compiler_params=params(16),
        name="gather_answers",
    )(row_of, answer, q, new)


def project_body(place_ref, own_ref, w_ref, *refs):
    ref_list, out_ref, total_ref, rows_ref = refs[:-3], refs[-3], refs[-2], refs[-1]
    rows = own_ref.shape[0]
    rows_ref[:rows, :] = own_ref[...]
    for n, ref in enumerate(ref_list):
        rows_ref[(n + 1) * rows : (n + 2) * rows, :] = ref[ref.shape[0] - rows :, :]
    total = dot_nn(rows_ref[...], w_ref[...])
    for n in range(rows_ref.shape[0] // 8):
        at = pl.multiple_of(place_ref[n], 8)
        total_ref[pl.ds(at, 8), :] = total[8 * n : 8 * n + 8]
    out_ref[...] = total_ref[...].astype(BF16)


def project(place, own, w, parts):
    rows = own.shape[0] * (len(parts) + 1)
    return pl.pallas_call(
        project_body,
        out_shape=jax.ShapeDtypeStruct((rows, w.shape[1]), BF16),
        in_specs=[SMEM] + [VMEM] * (len(parts) + 2),
        out_specs=VMEM,
        scratch_shapes=[pltpu.VMEM((rows, w.shape[1]), F32), pltpu.VMEM((rows, own.shape[1]), BF16)],
        compiler_params=params(16),
        name="project",
    )(place, own, w, *parts)


def shards(
    q_stretch,
    stretch_key_value,
    context_key_value,
    dec_q,
    dec_new,
    pool_key_value,
    block_table,
    cache_len,
    w_out,
):
    me = lax.axis_index(CTX)
    z = lax.axis_index("z")
    cycle = lax.axis_size(CTX)
    stretch = q_stretch.shape[0]
    rows_dev, nblk = dec_q.shape[0], block_table.shape[1]
    pool_dev, block_size = pool_key_value.shape[:2]

    def after(x, *others):
        return lax.optimization_barrier((x, *others))[0]

    def swap(x, name):
        return lax.ppermute(x, name, [(0, 1), (1, 0)])

    def turn(x, step):
        return lax.ppermute(x, "z", [(n, (n + step) % Z_CHIPS) for n in range(Z_CHIPS)])

    ask, row_of, q_rows, kv = prepare(
        me.reshape(1).astype(jnp.int32),
        block_table.T,
        cache_len,
        dec_q,
        context_key_value.reshape(-1, HEAD_SIZE),
        stretch_key_value.reshape(-1, HEAD_SIZE),
        cycle,
    )
    pool, q_stretch, ask = lax.optimization_barrier((pool_key_value, q_stretch, ask))
    ask = lax.all_to_all(ask, CTX, split_axis=0, concat_axis=0, tiled=True)
    table = block_table.reshape(cycle, rows_dev * nblk)
    place = jnp.sum(jnp.where(table // pool_dev == me, table % pool_dev, 0), axis=1)

    kv_core, kv_y = swap(kv, "core"), swap(kv, "y")
    right = [q_stretch, turn(q_stretch, 1), turn(q_stretch, 2)]
    left = [q_stretch, turn(q_stretch, -1), turn(q_stretch, -2)]
    blocks = fetch(pool.reshape(pool_dev, 2 * block_size, HEAD_SIZE))
    look_out = look(place, ask, blocks)
    right[1], right[2], left[1], left[2], look_out = lax.optimization_barrier(
        (right[1], right[2], left[1], left[2], look_out)
    )
    answer = lax.all_to_all(look_out, CTX, split_axis=0, concat_axis=0, tiled=True)
    right += [turn(right[1], 2), turn(right[2], 2)]
    left.append(turn(left[1], -2))
    kv_yc = swap(after(kv_y, look_out), "core")
    kv_yc, answer = lax.optimization_barrier((kv_yc, answer))
    attn = gather_answers(row_of, answer, q_rows, dec_new.reshape(rows_dev, 4, HEAD_SIZE))
    attn_core = swap(attn, "core")
    sets, _ = lax.optimization_barrier(([kv, kv_core, kv_y, kv_yc], attn))
    keys, values = stack(sets)
    pair = jnp.concatenate([attn, attn_core], axis=0)
    pair_y = swap(pair, "y")

    shifts = jnp.arange(Z_CHIPS, dtype=jnp.int32)
    corners = jnp.arange(2 * CORES, dtype=jnp.int32)
    corners = me ^ (corners // CORES * CORES * Z_CHIPS + corners % CORES)
    askers = me + ((z - shifts + Z_CHIPS) % Z_CHIPS - z) * CORES
    deltas = (askers[:, None] - corners[None, :]) * stretch

    def go(shift, previous, part=None, rider=None, carry=True):
        queries = right[shift] if shift >= 0 else left[-shift]
        return attend(shift % Z_CHIPS, after(deltas, *previous), queries, keys, values, part, rider, carry)

    own = go(0, [pair])
    attn = jnp.concatenate([pair, pair_y], axis=0)
    out = go(4, [own], None, attn)
    from_right = [turn(out, -1)]
    out = go(-3, [out], None, attn)
    from_left = [turn(out, 1)]
    out = go(3, [out], from_right[-1])
    from_right.append(turn(out, -1))
    out = go(-2, [out], from_left[-1])
    from_left.append(turn(out, 1))
    out = go(2, [out], from_right[-1])
    from_right.append(turn(out, -1))
    out = go(-1, [out], from_left[-1])
    from_left.append(turn(out, 1))
    rest = from_right[2][stretch + 16 :]
    farthest = turn(rest, -1)
    out = go(1, [out, rest], from_right[2], None, False)
    last = turn(out, -1)

    relative = jnp.where(shifts > Z_CHIPS // 2, Z_CHIPS // 2 - shifts, shifts)
    there = ((z + relative + Z_CHIPS) % Z_CHIPS - z) * CORES
    holders = ((there[:, None] + corners[None, :]) * (2 * rows_dev)).reshape(-1)
    partial_out = project(holders, after(attn, out), w_out, [*from_right, farthest, *from_left])
    shares = lax.axis_size(("grp", "tp"))
    pieces = lax.all_to_all(
        partial_out.reshape(shares, -1, partial_out.shape[1]), ("grp", "tp"), split_axis=0, concat_axis=0, tiled=True
    )
    pre_out = merge([own, last, from_left[2]], stretch)
    dec_out = jnp.sum(pieces.astype(F32), axis=0).astype(BF16)
    return (pre_out, dec_out.reshape(-1, 2, dec_out.shape[1]))


def solution(mesh):
    shape = mesh.devices.shape
    fine = jax.sharding.Mesh(mesh.devices.reshape(-1, Z_CHIPS, CORES, *shape[1:]), (*CTX, *mesh.axis_names[1:]))
    placed = (
        P(CTX, ("grp", "tp")),
        P(CTX, None, ("grp", "tp")),
        P(CTX, None, ("grp", "tp")),
        P(CTX, None, ("grp", "tp")),
        P(CTX, None, None, ("grp", "tp")),
        P(CTX, None, None, ("grp", "tp")),
        P(),
        P(CTX),
        P(("grp", "tp"), CTX),
    )
    return jax.shard_map(
        shards,
        mesh=fine,
        in_specs=placed,
        out_specs=(P(CTX, ("grp", "tp")), P(("grp", "tp"), None, CTX)),
        check_vma=False,
    )
```

```python
import functools
import math

import jax
import jax.numpy as jnp
from jax import lax
from jax.experimental import pallas as pl
from jax.experimental.pallas import tpu as pltpu
from jax.sharding import PartitionSpec as P

HEAD_SIZE = 128
CORES = 2
Z_CHIPS = 8
CONTEXT_DEV = 1280
BLOCK = 128
CTX = ("y", "z", "core")
SCALE = math.log2(math.e) / math.sqrt(HEAD_SIZE)
LOWEST = -1e30
F32 = jnp.float32
BF16 = jnp.bfloat16
VMEM = pl.BlockSpec(memory_space=pltpu.VMEM)
SMEM = pl.BlockSpec(memory_space=pltpu.SMEM)
HBM = pl.BlockSpec(memory_space=pltpu.HBM)


def params(mib):
    return pltpu.CompilerParams(vmem_limit_bytes=mib * 1024 * 1024)


def in_hbm(x):
    return pltpu.with_memory_space_constraint(x, pltpu.HBM)


def in_vmem(x):
    return pltpu.with_memory_space_constraint(x, pltpu.VMEM)


def dot_nt(a, b):
    return lax.dot_general(a, b, (((1,), (1,)), ((), ())), preferred_element_type=F32)


def dot_nn(a, b):
    return lax.dot_general(a, b, (((1,), (0,)), ((), ())), preferred_element_type=F32)


def prepare_body(
    me_ref,
    table_hbm,
    length_hbm,
    q_hbm,
    context_hbm,
    stretch_hbm,
    ask_ref,
    row_ref,
    rows_ref,
    kv_ref,
    list_ref,
    table_ref,
    length_ref,
    q_ref,
    context_ref,
    stretch_ref,
    sem,
):
    pieces = 5
    total = context_ref.shape[0]
    step = total // pieces
    copies = [
        pltpu.make_async_copy(q_hbm, q_ref, sem.at[0]),
        pltpu.make_async_copy(table_hbm, table_ref, sem.at[1]),
        pltpu.make_async_copy(length_hbm, length_ref, sem.at[2]),
    ]
    for n in range(pieces):
        rows = pl.ds(n * step, step)
        copies.append(pltpu.make_async_copy(context_hbm.at[rows], context_ref.at[rows], sem.at[3 + n]))
    copies.append(pltpu.make_async_copy(stretch_hbm, stretch_ref, sem.at[3 + pieces]))
    for copy in copies:
        copy.start()

    rows_dev = length_ref.shape[0]
    nblk = table_ref.shape[0]
    lists = rows_ref.shape[1]
    heads = lists // 2
    pool_dev = ask_ref.shape[0]
    copies[0].wait()
    for r in range(rows_dev):
        q = q_ref[r].astype(F32)
        for t in range(2):
            for h in range(heads):
                at = t * heads + h
                list_ref[r, at : at + 1, :] = q[t : t + 1, h * HEAD_SIZE : (h + 1) * HEAD_SIZE]
    copies[1].wait()
    copies[2].wait()
    for r in range(rows_dev):
        listed = list_ref[r]
        rows_ref[r] = listed.astype(BF16)
        asked = jnp.concatenate([listed[:heads], listed[heads:]], axis=1).astype(BF16)
        for n in range(nblk):
            holder = table_ref[n, me_ref[0] * rows_dev + r] // pool_dev
            left = jnp.clip(length_ref[r] - n * BLOCK, 0, BLOCK).astype(F32)
            ask_ref[holder, :, : 2 * HEAD_SIZE] = asked
            ask_ref[holder, :, 2 * HEAD_SIZE :] = jnp.full((heads, HEAD_SIZE), left, F32).astype(BF16)
            row_ref[holder] = r

    def split(rows, at):
        count = rows.shape[0]
        half = count // 2
        i = lax.broadcasted_iota(jnp.int32, (count, count), 0)
        j = lax.broadcasted_iota(jnp.int32, (count, count), 1)
        source = jnp.where(i < half, 2 * i, 2 * (i - half) + 1)
        pick = jnp.where(j == source, 1.0, 0.0).astype(BF16)
        parted = dot_nn(pick, rows).astype(BF16)
        kv_ref[0, at : at + half, :] = parted[:half]
        kv_ref[1, at : at + half, :] = parted[half:]

    for copy in copies[3:]:
        copy.wait()
    for start in range(0, total, 256):
        split(context_ref[start : start + 256, :], start // 2)
    split(stretch_ref[...], total // 2)


def prepare(me, table, length, q, context, stretch, holders):
    rows_dev = length.shape[0]
    lists = 2 * q.shape[2] // HEAD_SIZE
    rows = (context.shape[0] + stretch.shape[0]) // 2
    return pl.pallas_call(
        prepare_body,
        out_shape=[
            jax.ShapeDtypeStruct((holders, lists // 2, 3 * HEAD_SIZE), BF16),
            jax.ShapeDtypeStruct((holders,), jnp.int32),
            jax.ShapeDtypeStruct((rows_dev, lists, HEAD_SIZE), BF16),
            jax.ShapeDtypeStruct((2, rows, HEAD_SIZE), BF16),
        ],
        in_specs=[SMEM] + [HBM] * 5,
        out_specs=[VMEM, SMEM, VMEM, VMEM],
        scratch_shapes=[
            pltpu.VMEM((rows_dev, lists, HEAD_SIZE), F32),
            pltpu.SMEM(table.shape, jnp.int32),
            pltpu.SMEM(length.shape, jnp.int32),
            pltpu.VMEM(q.shape, BF16),
            pltpu.VMEM(context.shape, BF16),
            pltpu.VMEM(stretch.shape, BF16),
            pltpu.SemaphoreType.DMA((9,)),
        ],
        compiler_params=params(16),
        name="prepare",
    )(me, *(in_hbm(x) for x in (table, length, q, context, stretch)))


def stack_body(*refs):
    sets = len(refs) - 4
    k_ref, v_ref, kv_ref, sem = refs[sets:]
    copies = [pltpu.make_async_copy(refs[n], kv_ref.at[n], sem.at[n]) for n in range(sets)]
    for copy in copies:
        copy.start()
    stretch = v_ref.shape[0] // sets - CONTEXT_DEV
    one = jnp.where(diagonal(), 1.0, 0.0).astype(BF16)
    v_ref[:, HEAD_SIZE:] = jnp.ones((v_ref.shape[0], HEAD_SIZE), BF16)
    for n in range(sets):
        copies[n].wait()
        ref = kv_ref.at[n]
        first, last = n * CONTEXT_DEV, sets * CONTEXT_DEV + n * stretch
        for at in range(0, CONTEXT_DEV, 256):
            k_ref[:, first + at : first + at + 256] = dot_nt(one, ref[0, at : at + 256, :]).astype(BF16)
        v_ref[first : first + CONTEXT_DEV, :HEAD_SIZE] = ref[1, :CONTEXT_DEV, :]
        v_ref[last : last + stretch, :HEAD_SIZE] = ref[1, CONTEXT_DEV:, :]
    k = jnp.concatenate([kv_ref[n, 0, CONTEXT_DEV:, :] for n in range(sets)], axis=0)
    k_ref[:, sets * CONTEXT_DEV :] = dot_nt(one, k).astype(BF16)


def stack(sets):
    keys = len(sets) * sets[0].shape[1]
    return pl.pallas_call(
        stack_body,
        out_shape=[
            jax.ShapeDtypeStruct((HEAD_SIZE, keys), BF16),
            jax.ShapeDtypeStruct((keys, 2 * HEAD_SIZE), BF16),
        ],
        in_specs=[HBM] * len(sets),
        out_specs=[VMEM, VMEM],
        scratch_shapes=[
            pltpu.VMEM((len(sets), *sets[0].shape), BF16),
            pltpu.SemaphoreType.DMA((len(sets),)),
        ],
        compiler_params=params(16),
        name="stack",
    )(*(in_hbm(x) for x in sets))


def diagonal():
    i = lax.broadcasted_iota(jnp.int32, (HEAD_SIZE, HEAD_SIZE), 0)
    j = lax.broadcasted_iota(jnp.int32, (HEAD_SIZE, HEAD_SIZE), 1)
    return i == j


def read_part(ref, stretch, first, heads):
    columns = range(first * HEAD_SIZE, (first + heads) * HEAD_SIZE, HEAD_SIZE)
    outputs = jnp.concatenate([ref[:stretch, c : c + HEAD_SIZE] for c in columns], axis=0)
    stat = ref[stretch : stretch + 16, first * stretch : (first + heads) * stretch].astype(F32)
    level = stat[0:1] + stat[1:2] + stat[2:3]
    columns = []
    for g in range(0, heads * stretch, HEAD_SIZE):
        column = jnp.sum(jnp.where(diagonal(), level[:, g : g + HEAD_SIZE], 0.0), axis=1, keepdims=True)
        columns.append(jnp.broadcast_to(column, (HEAD_SIZE, HEAD_SIZE)))
    return outputs.astype(F32), jnp.concatenate(columns, axis=0)


def join(outputs, levels):
    top = functools.reduce(jnp.maximum, levels)
    weights = [jnp.exp2(level - top) for level in levels]
    total = functools.reduce(jnp.add, weights)
    mixed = functools.reduce(jnp.add, [weight * output for weight, output in zip(weights, outputs)])
    return mixed / total, top + jnp.log2(total)


def write_outputs(ref, outputs, stretch, first):
    outputs = outputs.astype(BF16)
    for h in range(outputs.shape[0] // stretch):
        ref[:stretch, (first + h) * HEAD_SIZE : (first + h + 1) * HEAD_SIZE] = outputs[h * stretch : (h + 1) * stretch]


def write_level(ref, level, stretch, first):
    rows = level.shape[0]
    lines = []
    for g in range(0, rows, HEAD_SIZE):
        lines.append(jnp.sum(jnp.where(diagonal(), level[g : g + HEAD_SIZE], 0.0), axis=0, keepdims=True))
    level = jnp.concatenate(lines, axis=1)
    high = level.astype(BF16).astype(F32)
    rest = level - high
    middle = rest.astype(BF16).astype(F32)
    row = lax.broadcasted_iota(jnp.int32, (16, rows), 0)
    stat = jnp.where(row == 0, high, jnp.where(row == 1, middle, jnp.where(row == 2, rest - middle, 0.0)))
    ref[stretch : stretch + 16, first * stretch : first * stretch + rows] = stat.astype(BF16)


def attend_body(which, arrived, riders, delta_ref, k_ref, v_ref, q_ref, *refs):
    refs = list(refs)
    part_ref = refs.pop(0) if arrived else None
    rider_ref = refs.pop(0) if riders == "own" else part_ref
    out_ref, p_ref, total_ref, top_ref = refs
    stretch, width = q_ref.shape
    sets = delta_ref.shape[1]
    keys = v_ref.shape[0]
    halves, rows = p_ref.shape[:2]
    heads = rows // stretch
    chunk = 256

    if riders is not None:
        start = 0 if riders == "own" else stretch + 16
        out_ref[stretch + 16 :, :] = rider_ref[start:, :]
    out_ref[stretch : stretch + 16, halves * rows :] = jnp.zeros((16, width - halves * rows), BF16)

    def queries(n):
        columns = range(n * heads * HEAD_SIZE, (n + 1) * heads * HEAD_SIZE, HEAD_SIZE)
        return jnp.concatenate([q_ref[:, c : c + HEAD_SIZE] for c in columns], axis=0)

    def score(q, k, masked):
        s = dot_nn(q, k)
        if masked:
            row = lax.rem(lax.broadcasted_iota(jnp.int32, s.shape, 0), stretch)
            col = lax.broadcasted_iota(jnp.int32, s.shape, 1)
            bound = delta_ref[which, sets - 1] + (sets - 1) * stretch - col
            for m in reversed(range(sets - 1)):
                bound = jnp.where(col < (m + 1) * stretch, delta_ref[which, m] + m * stretch - col, bound)
            s = jnp.where(row + bound >= 0, s, LOWEST)
        return s

    def highest(s):
        parts = [s[:, c : c + HEAD_SIZE] for c in range(0, s.shape[1], HEAD_SIZE)]
        return functools.reduce(jnp.maximum, parts)

    def spread(top):
        return jnp.broadcast_to(jnp.max(top, axis=1, keepdims=True), (rows, HEAD_SIZE)) * SCALE

    def weigh(s, top):
        parts = [s[:, c : c + HEAD_SIZE] for c in range(0, s.shape[1], HEAD_SIZE)]
        return jnp.concatenate([jnp.exp2(part * SCALE - top) for part in parts], axis=1).astype(BF16)

    def finish(n, total, top):
        weight = total[:, HEAD_SIZE:]
        output, level = total[:, :HEAD_SIZE] / weight, top + jnp.log2(weight)
        if arrived:
            other, other_level = read_part(part_ref, stretch, n * heads, heads)
            output, level = join([output, other], [level, other_level])
        write_outputs(out_ref, output, stretch, n * heads)
        write_level(out_ref, level, stretch, n * heads)

    steps = keys // chunk
    ends = [steps * chunk * n // 21 for n in (5, 10, 15, 18, 20, 21)]
    tops = [spread(highest(score(queries(n), k_ref[:, :chunk], False))) for n in range(halves)]
    sums = []
    for n in range(halves):
        q = queries(n)
        total = None
        begun = 0
        for at in range(0, keys, chunk):
            masked = at >= sets * CONTEXT_DEV
            p_ref[n, :, at : at + chunk] = weigh(score(q, k_ref[:, at : at + chunk], masked), tops[n])
            done = at + chunk
            if done in ends:
                part = dot_nn(p_ref[n, :, begun:done], v_ref[begun:done, :])
                total = part if total is None else total + part
                begun = done
        sums.append(total[:, HEAD_SIZE:])
        finish(n, total, tops[n])

    @pl.when(jnp.logical_not(jnp.max(functools.reduce(jnp.maximum, sums)) < 1e37))
    def again():
        for n in range(halves):
            q = queries(n)
            last = score(q, k_ref[:, keys - chunk :], True)

            def climb(m, top):
                k = k_ref[:, pl.ds(pl.multiple_of(m * chunk, chunk), chunk)]
                return jnp.maximum(top, highest(score(q, k, False)))

            top_ref[...] = spread(lax.fori_loop(0, steps - 1, climb, highest(last)))
            total_ref[...] = dot_nn(weigh(last, top_ref[...]), v_ref[keys - chunk :, :])

            def add(m, carry):
                at = pl.ds(pl.multiple_of(m * chunk, chunk), chunk)
                total_ref[...] += dot_nn(weigh(score(q, k_ref[:, at], False), top_ref[...]), v_ref[at, :])
                return carry

            lax.fori_loop(0, steps - 1, add, 0)
            finish(n, total_ref[...], top_ref[...])


def attend(which, deltas, queries, keys, values, part=None, rider=None, carry=True):
    stretch, width = queries.shape
    rows = width // HEAD_SIZE * stretch // 2
    count = values.shape[0]
    operands = [deltas, keys, values, queries]
    out_rows = stretch + 16
    riders = None
    if part is not None:
        operands.append(part)
        if carry:
            riders = "arrived"
            out_rows = part.shape[0]
    if rider is not None:
        riders = "own"
        operands.append(rider)
        out_rows += rider.shape[0]
    return pl.pallas_call(
        functools.partial(attend_body, which, part is not None, riders),
        out_shape=jax.ShapeDtypeStruct((out_rows, width), BF16),
        in_specs=[SMEM] + [VMEM] * (len(operands) - 1),
        out_specs=VMEM,
        scratch_shapes=[
            pltpu.VMEM((2, rows, count), BF16),
            pltpu.VMEM((rows, 2 * HEAD_SIZE), F32),
            pltpu.VMEM((rows, HEAD_SIZE), F32),
        ],
        compiler_params=params(24),
        cost_estimate=pl.CostEstimate(
            flops=16 * rows * count * HEAD_SIZE,
            bytes_accessed=4 * count * HEAD_SIZE,
            transcendentals=2 * rows * count,
        ),
        name="attend",
    )(*operands)


def merge_body(*refs):
    part_refs, out_ref = refs[:-1], refs[-1]
    stretch = out_ref.shape[0]
    read = [read_part(ref, stretch, 0, out_ref.shape[1] // HEAD_SIZE) for ref in part_refs]
    output, _ = join([x for x, _ in read], [x for _, x in read])
    write_outputs(out_ref, output, stretch, 0)


def merge(parts, stretch):
    return pl.pallas_call(
        merge_body,
        out_shape=jax.ShapeDtypeStruct((stretch, parts[0].shape[1]), BF16),
        in_specs=[VMEM] * len(parts),
        out_specs=VMEM,
        compiler_params=params(16),
        name="merge",
    )(*parts)


def fetch_body(pool_hbm, pool_ref, sem):
    copies = []
    step = pool_ref.shape[0] // sem.shape[0]
    for n in range(sem.shape[0]):
        blocks = pl.ds(n * step, step)
        copies.append(pltpu.make_async_copy(pool_hbm.at[blocks], pool_ref.at[blocks], sem.at[n]))
        copies[n].start()
    for copy in copies:
        copy.wait()


def fetch(pool):
    return pl.pallas_call(
        fetch_body,
        out_shape=pltpu.VMEM(pool.shape, BF16),
        in_specs=[HBM],
        out_specs=VMEM,
        scratch_shapes=[pltpu.SemaphoreType.DMA((4,))],
        compiler_params=params(16),
        name="fetch_blocks",
    )(in_hbm(pool))


def look_body(place_ref, ask_ref, pool_ref, out_ref, s_ref, p_ref, scale_ref):
    owners, heads = ask_ref.shape[:2]
    lists = 2 * heads
    span = pool_ref.shape[1]
    for d in range(owners):
        q = ask_ref[d, :, : 2 * HEAD_SIZE].astype(F32)
        q = jnp.concatenate([q[:, :HEAD_SIZE], q[:, HEAD_SIZE:]], axis=0).astype(BF16)
        s_ref[d * lists : (d + 1) * lists, :] = dot_nt(q, pool_ref[place_ref[d]])
    col = lax.broadcasted_iota(jnp.int32, (lists, span), 1)
    lane = lax.broadcasted_iota(jnp.int32, (heads, HEAD_SIZE), 1)
    even = (col & 1) == 0
    for d in range(owners):
        limit = ask_ref[d, :, 2 * HEAD_SIZE :].astype(F32) * 2.0
        limit = jnp.concatenate([limit] * 2, axis=0)
        limit = jnp.concatenate([limit] * (span // HEAD_SIZE), axis=1)
        allowed = even & (col.astype(F32) < limit)
        s = jnp.where(allowed, s_ref[d * lists : (d + 1) * lists, :], LOWEST)
        top = jnp.max(s, axis=1, keepdims=True)
        p = jnp.where(allowed, jnp.exp2((s - top) * SCALE), 0.0)
        total = jnp.sum(p, axis=1, keepdims=True)
        p_ref[d * lists : (d + 1) * lists, :] = pltpu.roll(p, 1, 1).astype(BF16)
        seen = total > 0.0
        level = jnp.where(seen, top * SCALE + jnp.log2(jnp.where(seen, total, 1.0)), LOWEST)
        level = jnp.broadcast_to(level, (lists, HEAD_SIZE))
        high = level.astype(BF16).astype(F32)
        rest = level - high
        middle = rest.astype(BF16).astype(F32)
        stat = jnp.zeros((heads, HEAD_SIZE), F32)
        for t in range(2):
            for n, piece in enumerate((high, middle, rest - middle)):
                stat = jnp.where(lane == 3 * t + n, piece[t * heads : (t + 1) * heads], stat)
        out_ref[d, :, 2 * HEAD_SIZE :] = stat.astype(BF16)
        scale_ref[d * lists : (d + 1) * lists, :] = jnp.broadcast_to(
            jnp.where(seen, 1.0 / jnp.where(seen, total, 1.0), 0.0), (lists, HEAD_SIZE)
        )
    for d in range(owners):
        o = dot_nn(p_ref[d * lists : (d + 1) * lists, :], pool_ref[place_ref[d]])
        o = o * scale_ref[d * lists : (d + 1) * lists, :]
        out_ref[d, :, : 2 * HEAD_SIZE] = jnp.concatenate([o[:heads], o[heads:]], axis=1).astype(BF16)


def look(place, ask, pool):
    owners, heads, width = ask.shape
    span = pool.shape[1]
    rows = 2 * owners * heads
    return pl.pallas_call(
        look_body,
        out_shape=jax.ShapeDtypeStruct(ask.shape, BF16),
        in_specs=[SMEM, VMEM, VMEM],
        out_specs=VMEM,
        scratch_shapes=[
            pltpu.VMEM((rows, span), F32),
            pltpu.VMEM((rows, span), BF16),
            pltpu.VMEM((rows, HEAD_SIZE), F32),
        ],
        compiler_params=params(24),
        cost_estimate=pl.CostEstimate(
            flops=4 * rows * span * HEAD_SIZE, bytes_accessed=2 * owners * span * HEAD_SIZE, transcendentals=0
        ),
        name="look_in_blocks",
    )(place, ask, pool)


def gather_body(row_ref, answer_ref, q_ref, new_ref, out_ref, level_ref, top_ref, sum_ref, acc_ref, flat_ref):
    holders = answer_ref.shape[0]
    rows, lists = q_ref.shape[0], q_ref.shape[1]
    heads = lists // 2
    lane = lax.broadcasted_iota(jnp.int32, (lists, HEAD_SIZE), 1)
    later = lax.broadcasted_iota(jnp.int32, (lists, HEAD_SIZE), 0) >= heads
    own = []
    for r in range(rows):
        q = q_ref[r].astype(F32)
        new = new_ref[r].astype(F32)
        scores = []
        for t in range(2):
            s = jnp.sum(q * new[2 * t : 2 * t + 1, :], axis=1, keepdims=True) * SCALE
            scores.append(jnp.broadcast_to(s, (lists, HEAD_SIZE)))
        scores[1] = jnp.where(later, scores[1], LOWEST)
        top_ref[r] = jnp.maximum(scores[0], scores[1])
        own.append((scores, new))
    for d in range(holders):
        stat = answer_ref[d, :, 2 * HEAD_SIZE :].astype(F32)
        stat = jnp.concatenate([stat, stat], axis=0)
        level = jnp.sum(jnp.where((lane < 6) & ((lane >= 3) == later), stat, 0.0), axis=1, keepdims=True)
        level_ref[d] = jnp.broadcast_to(level, (lists, HEAD_SIZE))
    for d in range(holders):
        r = row_ref[d]
        top_ref[r] = jnp.maximum(top_ref[r], level_ref[d])
    for r in range(rows):
        scores, new = own[r]
        first = jnp.exp2(scores[0] - top_ref[r])
        second = jnp.exp2(scores[1] - top_ref[r])
        sum_ref[r] = first + second
        acc_ref[r] = first * new[1:2, :] + second * new[3:4, :]
    for d in range(holders):
        r = row_ref[d]
        weight = jnp.exp2(level_ref[d] - top_ref[r])
        sum_ref[r] = sum_ref[r] + weight
        o = answer_ref[d, :, : 2 * HEAD_SIZE].astype(F32)
        o = jnp.concatenate([o[:, :HEAD_SIZE], o[:, HEAD_SIZE:]], axis=0)
        acc_ref[r] = acc_ref[r] + weight * o
    for r in range(rows):
        o = acc_ref[r] / sum_ref[r]
        for t in range(2):
            for h in range(heads):
                flat_ref[2 * r + t : 2 * r + t + 1, h * HEAD_SIZE : (h + 1) * HEAD_SIZE] = o[
                    t * heads + h : t * heads + h + 1, :
                ]
    out_ref[...] = flat_ref[...].astype(BF16)


def gather_answers(row_of, answer, q, new):
    rows, lists, width = q.shape
    holders = answer.shape[0]
    heads = lists // 2
    state = pltpu.VMEM((rows, lists, width), F32)
    return pl.pallas_call(
        gather_body,
        out_shape=jax.ShapeDtypeStruct((2 * rows, heads * width), BF16),
        in_specs=[SMEM, VMEM, VMEM, VMEM],
        out_specs=VMEM,
        scratch_shapes=[
            pltpu.VMEM((holders, lists, width), F32),
            state,
            state,
            state,
            pltpu.VMEM((2 * rows, heads * width), F32),
        ],
        compiler_params=params(16),
        name="gather_answers",
    )(row_of, answer, q, new)


def project_body(place_ref, own_ref, w_ref, *refs):
    ref_list, out_ref, total_ref, rows_ref = refs[:-3], refs[-3], refs[-2], refs[-1]
    rows = own_ref.shape[0]
    rows_ref[:rows, :] = own_ref[...]
    for n, ref in enumerate(ref_list):
        rows_ref[(n + 1) * rows : (n + 2) * rows, :] = ref[ref.shape[0] - rows :, :]
    total = dot_nn(rows_ref[...], w_ref[...])
    for n in range(rows_ref.shape[0] // 8):
        at = pl.multiple_of(place_ref[n], 8)
        total_ref[pl.ds(at, 8), :] = total[8 * n : 8 * n + 8]
    out_ref[...] = total_ref[...].astype(BF16)


def project(place, own, w, parts):
    rows = own.shape[0] * (len(parts) + 1)
    return pl.pallas_call(
        project_body,
        out_shape=jax.ShapeDtypeStruct((rows, w.shape[1]), BF16),
        in_specs=[SMEM] + [VMEM] * (len(parts) + 2),
        out_specs=VMEM,
        scratch_shapes=[pltpu.VMEM((rows, w.shape[1]), F32), pltpu.VMEM((rows, own.shape[1]), BF16)],
        compiler_params=params(16),
        name="project",
    )(place, own, w, *parts)


def shards(
    q_stretch,
    stretch_key_value,
    context_key_value,
    dec_q,
    dec_new,
    pool_key_value,
    block_table,
    cache_len,
    w_out,
):
    me = lax.axis_index(CTX)
    z = lax.axis_index("z")
    cycle = lax.axis_size(CTX)
    stretch = q_stretch.shape[0]
    rows_dev, nblk = dec_q.shape[0], block_table.shape[1]
    pool_dev, block_size = pool_key_value.shape[:2]

    def after(x, *others):
        return lax.optimization_barrier((x, *others))[0]

    def swap(x, name):
        return lax.ppermute(x, name, [(0, 1), (1, 0)])

    def turn(x, step):
        return lax.ppermute(x, "z", [(n, (n + step) % Z_CHIPS) for n in range(Z_CHIPS)])

    ask, row_of, q_rows, kv = prepare(
        me.reshape(1).astype(jnp.int32),
        block_table.T,
        cache_len,
        dec_q,
        context_key_value.reshape(-1, HEAD_SIZE),
        stretch_key_value.reshape(-1, HEAD_SIZE),
        cycle,
    )
    pool, q_stretch, ask = lax.optimization_barrier((pool_key_value, q_stretch, ask))
    ask = lax.all_to_all(ask, CTX, split_axis=0, concat_axis=0, tiled=True)
    table = block_table.reshape(cycle, rows_dev * nblk)
    place = jnp.sum(jnp.where(table // pool_dev == me, table % pool_dev, 0), axis=1)

    kv_core, kv_y = swap(kv, "core"), swap(kv, "y")
    right = [q_stretch, turn(q_stretch, 1), turn(q_stretch, 2)]
    left = [q_stretch, turn(q_stretch, -1), turn(q_stretch, -2)]
    blocks = fetch(pool.reshape(pool_dev, 2 * block_size, HEAD_SIZE))
    look_out = look(place, ask, blocks)
    right[1], right[2], left[1], left[2], look_out = lax.optimization_barrier(
        (right[1], right[2], left[1], left[2], look_out)
    )
    answer = lax.all_to_all(look_out, CTX, split_axis=0, concat_axis=0, tiled=True)
    right += [turn(right[1], 2), turn(right[2], 2)]
    left.append(turn(left[1], -2))
    kv_yc = swap(after(kv_y, look_out), "core")
    sets = [kv, kv_core, kv_y, kv_yc]

    shifts = jnp.arange(Z_CHIPS, dtype=jnp.int32)
    corners = jnp.arange(2 * CORES, dtype=jnp.int32)
    corners = me ^ (corners // CORES * CORES * Z_CHIPS + corners % CORES)
    askers = me + ((z - shifts + Z_CHIPS) % Z_CHIPS - z) * CORES
    deltas = (askers[:, None] - corners[None, :]) * stretch

    keys, values = stack(sets)
    own = attend(0, deltas, q_stretch, keys, values)
    own, answer = lax.optimization_barrier((own, answer))
    attn = gather_answers(row_of, answer, q_rows, dec_new.reshape(rows_dev, 4, HEAD_SIZE))
    attn_core = swap(attn, "core")
    sets, _ = lax.optimization_barrier((sets, attn))
    keys, values = stack(sets)
    pair = jnp.concatenate([attn, attn_core], axis=0)
    pair_y = swap(pair, "y")

    def go(shift, previous, part=None, rider=None, carry=True):
        queries = right[shift] if shift >= 0 else left[-shift]
        return attend(shift % Z_CHIPS, after(deltas, *previous), queries, keys, values, part, rider, carry)

    attn = jnp.concatenate([pair, pair_y], axis=0)
    out = go(4, [attn], None, attn)
    from_right = [turn(out, -1)]
    out = go(-3, [out], None, attn)
    from_left = [turn(out, 1)]
    out = go(3, [out], from_right[-1])
    from_right.append(turn(out, -1))
    out = go(-2, [out], from_left[-1])
    from_left.append(turn(out, 1))
    out = go(2, [out], from_right[-1])
    from_right.append(turn(out, -1))
    out = go(-1, [out], from_left[-1])
    from_left.append(turn(out, 1))
    rest = from_right[2][stretch + 16 :]
    farthest = turn(rest, -1)
    out = go(1, [out, rest], from_right[2], None, False)
    last = turn(out, -1)

    relative = jnp.where(shifts > Z_CHIPS // 2, Z_CHIPS // 2 - shifts, shifts)
    there = ((z + relative + Z_CHIPS) % Z_CHIPS - z) * CORES
    holders = ((there[:, None] + corners[None, :]) * (2 * rows_dev)).reshape(-1)
    partial_out = project(holders, after(attn, out), w_out, [*from_right, farthest, *from_left])
    shares = lax.axis_size(("grp", "tp"))
    pieces = lax.all_to_all(
        partial_out.reshape(shares, -1, partial_out.shape[1]), ("grp", "tp"), split_axis=0, concat_axis=0, tiled=True
    )
    pre_out = merge([own, last, from_left[2]], stretch)
    dec_out = jnp.sum(pieces.astype(F32), axis=0).astype(BF16)
    return (pre_out, dec_out.reshape(-1, 2, dec_out.shape[1]))


def solution(mesh):
    shape = mesh.devices.shape
    fine = jax.sharding.Mesh(mesh.devices.reshape(-1, Z_CHIPS, CORES, *shape[1:]), (*CTX, *mesh.axis_names[1:]))
    placed = (
        P(CTX, ("grp", "tp")),
        P(CTX, None, ("grp", "tp")),
        P(CTX, None, ("grp", "tp")),
        P(CTX, None, ("grp", "tp")),
        P(CTX, None, None, ("grp", "tp")),
        P(CTX, None, None, ("grp", "tp")),
        P(),
        P(CTX),
        P(("grp", "tp"), CTX),
    )
    return jax.shard_map(
        shards,
        mesh=fine,
        in_specs=placed,
        out_specs=(P(CTX, ("grp", "tp")), P(("grp", "tp"), None, CTX)),
        check_vma=False,
    )
```

```python
import functools
import math

import jax
import jax.numpy as jnp
from jax import lax
from jax.experimental import pallas as pl
from jax.experimental.pallas import tpu as pltpu
from jax.sharding import PartitionSpec as P

HEAD_SIZE = 128
CORES = 2
Z_CHIPS = 8
CONTEXT_DEV = 1280
BLOCK = 128
CTX = ("y", "z", "core")
SCALE = math.log2(math.e) / math.sqrt(HEAD_SIZE)
LOWEST = -1e30
F32 = jnp.float32
BF16 = jnp.bfloat16
VMEM = pl.BlockSpec(memory_space=pltpu.VMEM)
SMEM = pl.BlockSpec(memory_space=pltpu.SMEM)
HBM = pl.BlockSpec(memory_space=pltpu.HBM)


def params(mib):
    return pltpu.CompilerParams(vmem_limit_bytes=mib * 1024 * 1024)


def in_hbm(x):
    return pltpu.with_memory_space_constraint(x, pltpu.HBM)


def in_vmem(x):
    return pltpu.with_memory_space_constraint(x, pltpu.VMEM)


def dot_nt(a, b):
    return lax.dot_general(a, b, (((1,), (1,)), ((), ())), preferred_element_type=F32)


def dot_nn(a, b):
    return lax.dot_general(a, b, (((1,), (0,)), ((), ())), preferred_element_type=F32)


def prepare_body(
    me_ref,
    table_hbm,
    length_hbm,
    q_hbm,
    context_hbm,
    stretch_hbm,
    ask_ref,
    row_ref,
    rows_ref,
    kv_ref,
    list_ref,
    table_ref,
    length_ref,
    q_ref,
    context_ref,
    stretch_ref,
    sem,
):
    pieces = 5
    total = context_ref.shape[0]
    step = total // pieces
    copies = [
        pltpu.make_async_copy(q_hbm, q_ref, sem.at[0]),
        pltpu.make_async_copy(table_hbm, table_ref, sem.at[1]),
        pltpu.make_async_copy(length_hbm, length_ref, sem.at[2]),
    ]
    for n in range(pieces):
        rows = pl.ds(n * step, step)
        copies.append(pltpu.make_async_copy(context_hbm.at[rows], context_ref.at[rows], sem.at[3 + n]))
    copies.append(pltpu.make_async_copy(stretch_hbm, stretch_ref, sem.at[3 + pieces]))
    for copy in copies:
        copy.start()

    rows_dev = length_ref.shape[0]
    nblk = table_ref.shape[0]
    lists = rows_ref.shape[1]
    heads = lists // 2
    pool_dev = ask_ref.shape[0]
    copies[0].wait()
    for r in range(rows_dev):
        q = q_ref[r].astype(F32)
        for t in range(2):
            for h in range(heads):
                at = t * heads + h
                list_ref[r, at : at + 1, :] = q[t : t + 1, h * HEAD_SIZE : (h + 1) * HEAD_SIZE]
    copies[1].wait()
    copies[2].wait()
    for r in range(rows_dev):
        listed = list_ref[r]
        rows_ref[r] = listed.astype(BF16)
        asked = jnp.concatenate([listed[:heads], listed[heads:]], axis=1).astype(BF16)
        for n in range(nblk):
            holder = table_ref[n, me_ref[0] * rows_dev + r] // pool_dev
            left = jnp.clip(length_ref[r] - n * BLOCK, 0, BLOCK).astype(F32)
            ask_ref[holder, :, : 2 * HEAD_SIZE] = asked
            ask_ref[holder, :, 2 * HEAD_SIZE :] = jnp.full((heads, HEAD_SIZE), left, F32).astype(BF16)
            row_ref[holder] = r

    def split(rows, at):
        count = rows.shape[0]
        half = count // 2
        i = lax.broadcasted_iota(jnp.int32, (count, count), 0)
        j = lax.broadcasted_iota(jnp.int32, (count, count), 1)
        source = jnp.where(i < half, 2 * i, 2 * (i - half) + 1)
        pick = jnp.where(j == source, 1.0, 0.0).astype(BF16)
        parted = dot_nn(pick, rows).astype(BF16)
        kv_ref[0, at : at + half, :] = parted[:half]
        kv_ref[1, at : at + half, :] = parted[half:]

    for copy in copies[3:]:
        copy.wait()
    for start in range(0, total, 256):
        split(context_ref[start : start + 256, :], start // 2)
    split(stretch_ref[...], total // 2)


def prepare(me, table, length, q, context, stretch, holders):
    rows_dev = length.shape[0]
    lists = 2 * q.shape[2] // HEAD_SIZE
    rows = (context.shape[0] + stretch.shape[0]) // 2
    return pl.pallas_call(
        prepare_body,
        out_shape=[
            jax.ShapeDtypeStruct((holders, lists // 2, 3 * HEAD_SIZE), BF16),
            jax.ShapeDtypeStruct((holders,), jnp.int32),
            jax.ShapeDtypeStruct((rows_dev, lists, HEAD_SIZE), BF16),
            jax.ShapeDtypeStruct((2, rows, HEAD_SIZE), BF16),
        ],
        in_specs=[SMEM] + [HBM] * 5,
        out_specs=[VMEM, SMEM, VMEM, VMEM],
        scratch_shapes=[
            pltpu.VMEM((rows_dev, lists, HEAD_SIZE), F32),
            pltpu.SMEM(table.shape, jnp.int32),
            pltpu.SMEM(length.shape, jnp.int32),
            pltpu.VMEM(q.shape, BF16),
            pltpu.VMEM(context.shape, BF16),
            pltpu.VMEM(stretch.shape, BF16),
            pltpu.SemaphoreType.DMA((9,)),
        ],
        compiler_params=params(16),
        name="prepare",
    )(me, *(in_hbm(x) for x in (table, length, q, context, stretch)))


def stack_body(*refs):
    kv_refs, k_ref, v_ref = refs[:-2], refs[-2], refs[-1]
    sets = len(kv_refs)
    stretch = v_ref.shape[0] // sets - CONTEXT_DEV
    one = jnp.where(diagonal(), 1.0, 0.0).astype(BF16)
    v_ref[:, HEAD_SIZE:] = jnp.ones((v_ref.shape[0], HEAD_SIZE), BF16)
    for n, ref in enumerate(kv_refs):
        first, last = n * CONTEXT_DEV, sets * CONTEXT_DEV + n * stretch
        for at in range(0, CONTEXT_DEV, 256):
            k_ref[:, first + at : first + at + 256] = dot_nt(one, ref[0, at : at + 256, :]).astype(BF16)
        v_ref[first : first + CONTEXT_DEV, :HEAD_SIZE] = ref[1, :CONTEXT_DEV, :]
        v_ref[last : last + stretch, :HEAD_SIZE] = ref[1, CONTEXT_DEV:, :]
    k = jnp.concatenate([ref[0, CONTEXT_DEV:, :] for ref in kv_refs], axis=0)
    k_ref[:, sets * CONTEXT_DEV :] = dot_nt(one, k).astype(BF16)


def stack(sets):
    keys = len(sets) * sets[0].shape[1]
    return pl.pallas_call(
        stack_body,
        out_shape=[
            jax.ShapeDtypeStruct((HEAD_SIZE, keys), BF16),
            jax.ShapeDtypeStruct((keys, 2 * HEAD_SIZE), BF16),
        ],
        in_specs=[VMEM] * len(sets),
        out_specs=[VMEM, VMEM],
        compiler_params=params(16),
        name="stack",
    )(*sets)


def diagonal():
    i = lax.broadcasted_iota(jnp.int32, (HEAD_SIZE, HEAD_SIZE), 0)
    j = lax.broadcasted_iota(jnp.int32, (HEAD_SIZE, HEAD_SIZE), 1)
    return i == j


def read_part(ref, stretch, first, heads):
    columns = range(first * HEAD_SIZE, (first + heads) * HEAD_SIZE, HEAD_SIZE)
    outputs = jnp.concatenate([ref[:stretch, c : c + HEAD_SIZE] for c in columns], axis=0)
    stat = ref[stretch : stretch + 16, first * stretch : (first + heads) * stretch].astype(F32)
    level = stat[0:1] + stat[1:2] + stat[2:3]
    columns = []
    for g in range(0, heads * stretch, HEAD_SIZE):
        column = jnp.sum(jnp.where(diagonal(), level[:, g : g + HEAD_SIZE], 0.0), axis=1, keepdims=True)
        columns.append(jnp.broadcast_to(column, (HEAD_SIZE, HEAD_SIZE)))
    return outputs.astype(F32), jnp.concatenate(columns, axis=0)


def join(outputs, levels):
    top = functools.reduce(jnp.maximum, levels)
    weights = [jnp.exp2(level - top) for level in levels]
    total = functools.reduce(jnp.add, weights)
    mixed = functools.reduce(jnp.add, [weight * output for weight, output in zip(weights, outputs)])
    return mixed / total, top + jnp.log2(total)


def write_outputs(ref, outputs, stretch, first):
    outputs = outputs.astype(BF16)
    for h in range(outputs.shape[0] // stretch):
        ref[:stretch, (first + h) * HEAD_SIZE : (first + h + 1) * HEAD_SIZE] = outputs[h * stretch : (h + 1) * stretch]


def write_level(ref, level, stretch, first):
    rows = level.shape[0]
    lines = []
    for g in range(0, rows, HEAD_SIZE):
        lines.append(jnp.sum(jnp.where(diagonal(), level[g : g + HEAD_SIZE], 0.0), axis=0, keepdims=True))
    level = jnp.concatenate(lines, axis=1)
    high = level.astype(BF16).astype(F32)
    rest = level - high
    middle = rest.astype(BF16).astype(F32)
    row = lax.broadcasted_iota(jnp.int32, (16, rows), 0)
    stat = jnp.where(row == 0, high, jnp.where(row == 1, middle, jnp.where(row == 2, rest - middle, 0.0)))
    ref[stretch : stretch + 16, first * stretch : first * stretch + rows] = stat.astype(BF16)


def attend_body(which, arrived, riders, half, delta_ref, k_ref, v_ref, q_ref, *refs):
    refs = list(refs)
    part_ref = refs.pop(0) if arrived else None
    rider_ref = refs.pop(0) if riders == "own" else part_ref
    out_ref, p_ref, total_ref, top_ref = refs
    stretch, width = q_ref.shape
    if half is not None:
        stretch //= 2
        q_ref = q_ref.at[half * stretch : (half + 1) * stretch]
    sets = delta_ref.shape[1]
    keys = v_ref.shape[0]
    halves, rows = p_ref.shape[:2]
    heads = rows // stretch
    chunk = 256

    if riders is not None:
        start = 0 if riders == "own" else stretch + 16
        out_ref[stretch + 16 :, :] = rider_ref[start:, :]
    out_ref[stretch : stretch + 16, halves * rows :] = jnp.zeros((16, width - halves * rows), BF16)

    def queries(n):
        columns = range(n * heads * HEAD_SIZE, (n + 1) * heads * HEAD_SIZE, HEAD_SIZE)
        return jnp.concatenate([q_ref[:, c : c + HEAD_SIZE] for c in columns], axis=0)

    def score(q, k, masked):
        s = dot_nn(q, k)
        if masked:
            row = lax.rem(lax.broadcasted_iota(jnp.int32, s.shape, 0), stretch)
            col = lax.broadcasted_iota(jnp.int32, s.shape, 1)
            bound = delta_ref[which, sets - 1] + (sets - 1) * stretch - col
            for m in reversed(range(sets - 1)):
                bound = jnp.where(col < (m + 1) * stretch, delta_ref[which, m] + m * stretch - col, bound)
            s = jnp.where(row + bound >= 0, s, LOWEST)
        return s

    def highest(s):
        parts = [s[:, c : c + HEAD_SIZE] for c in range(0, s.shape[1], HEAD_SIZE)]
        return functools.reduce(jnp.maximum, parts)

    def spread(top):
        return jnp.broadcast_to(jnp.max(top, axis=1, keepdims=True), (rows, HEAD_SIZE)) * SCALE

    def weigh(s, top):
        parts = [s[:, c : c + HEAD_SIZE] for c in range(0, s.shape[1], HEAD_SIZE)]
        return jnp.concatenate([jnp.exp2(part * SCALE - top) for part in parts], axis=1).astype(BF16)

    def finish(n, total, top):
        weight = total[:, HEAD_SIZE:]
        output, level = total[:, :HEAD_SIZE] / weight, top + jnp.log2(weight)
        if arrived:
            other, other_level = read_part(part_ref, stretch, n * heads, heads)
            output, level = join([output, other], [level, other_level])
        write_outputs(out_ref, output, stretch, n * heads)
        write_level(out_ref, level, stretch, n * heads)

    steps = keys // chunk
    ends = [steps * chunk * n // 21 for n in (5, 10, 15, 18, 20, 21)]
    tops = [spread(highest(score(queries(n), k_ref[:, :chunk], False))) for n in range(halves)]
    sums = []
    for n in range(halves):
        q = queries(n)
        total = None
        begun = 0
        for at in range(0, keys, chunk):
            masked = at >= sets * CONTEXT_DEV
            p_ref[n, :, at : at + chunk] = weigh(score(q, k_ref[:, at : at + chunk], masked), tops[n])
            done = at + chunk
            if done in ends:
                part = dot_nn(p_ref[n, :, begun:done], v_ref[begun:done, :])
                total = part if total is None else total + part
                begun = done
        sums.append(total[:, HEAD_SIZE:])
        finish(n, total, tops[n])

    @pl.when(jnp.logical_not(jnp.max(functools.reduce(jnp.maximum, sums)) < 1e37))
    def again():
        for n in range(halves):
            q = queries(n)
            last = score(q, k_ref[:, keys - chunk :], True)

            def climb(m, top):
                k = k_ref[:, pl.ds(pl.multiple_of(m * chunk, chunk), chunk)]
                return jnp.maximum(top, highest(score(q, k, False)))

            top_ref[...] = spread(lax.fori_loop(0, steps - 1, climb, highest(last)))
            total_ref[...] = dot_nn(weigh(last, top_ref[...]), v_ref[keys - chunk :, :])

            def add(m, carry):
                at = pl.ds(pl.multiple_of(m * chunk, chunk), chunk)
                total_ref[...] += dot_nn(weigh(score(q, k_ref[:, at], False), top_ref[...]), v_ref[at, :])
                return carry

            lax.fori_loop(0, steps - 1, add, 0)
            finish(n, total_ref[...], top_ref[...])


def attend(which, deltas, queries, keys, values, part=None, rider=None, carry=True, half=None):
    stretch, width = queries.shape
    if half is not None:
        stretch //= 2
    rows = width // HEAD_SIZE * stretch // 2
    count = values.shape[0]
    operands = [deltas, keys, values, queries]
    out_rows = stretch + 16
    riders = None
    if part is not None:
        operands.append(part)
        if carry:
            riders = "arrived"
            out_rows = part.shape[0]
    if rider is not None:
        riders = "own"
        operands.append(rider)
        out_rows += rider.shape[0]
    return pl.pallas_call(
        functools.partial(attend_body, which, part is not None, riders, half),
        out_shape=jax.ShapeDtypeStruct((out_rows, width), BF16),
        in_specs=[SMEM] + [VMEM] * (len(operands) - 1),
        out_specs=VMEM,
        scratch_shapes=[
            pltpu.VMEM((2, rows, count), BF16),
            pltpu.VMEM((rows, 2 * HEAD_SIZE), F32),
            pltpu.VMEM((rows, HEAD_SIZE), F32),
        ],
        compiler_params=params(24),
        cost_estimate=pl.CostEstimate(
            flops=16 * rows * count * HEAD_SIZE,
            bytes_accessed=4 * count * HEAD_SIZE,
            transcendentals=2 * rows * count,
        ),
        name="attend",
    )(*operands)


def merge_body(*refs):
    part_refs, out_ref = refs[:-1], refs[-1]
    stretch = out_ref.shape[0]
    read = [read_part(ref, stretch, 0, out_ref.shape[1] // HEAD_SIZE) for ref in part_refs]
    output, _ = join([x for x, _ in read], [x for _, x in read])
    write_outputs(out_ref, output, stretch, 0)


def merge(parts, stretch):
    return pl.pallas_call(
        merge_body,
        out_shape=jax.ShapeDtypeStruct((stretch, parts[0].shape[1]), BF16),
        in_specs=[VMEM] * len(parts),
        out_specs=VMEM,
        compiler_params=params(16),
        name="merge",
    )(*parts)


def fetch_body(pool_hbm, pool_ref, sem):
    copies = []
    step = pool_ref.shape[0] // sem.shape[0]
    for n in range(sem.shape[0]):
        blocks = pl.ds(n * step, step)
        copies.append(pltpu.make_async_copy(pool_hbm.at[blocks], pool_ref.at[blocks], sem.at[n]))
        copies[n].start()
    for copy in copies:
        copy.wait()


def fetch(pool):
    return pl.pallas_call(
        fetch_body,
        out_shape=pltpu.VMEM(pool.shape, BF16),
        in_specs=[HBM],
        out_specs=VMEM,
        scratch_shapes=[pltpu.SemaphoreType.DMA((4,))],
        compiler_params=params(16),
        name="fetch_blocks",
    )(in_hbm(pool))


def look_body(place_ref, ask_ref, pool_ref, out_ref, s_ref, p_ref, scale_ref):
    owners, heads = ask_ref.shape[:2]
    lists = 2 * heads
    span = pool_ref.shape[1]
    for d in range(owners):
        q = ask_ref[d, :, : 2 * HEAD_SIZE].astype(F32)
        q = jnp.concatenate([q[:, :HEAD_SIZE], q[:, HEAD_SIZE:]], axis=0).astype(BF16)
        s_ref[d * lists : (d + 1) * lists, :] = dot_nt(q, pool_ref[place_ref[d]])
    col = lax.broadcasted_iota(jnp.int32, (lists, span), 1)
    lane = lax.broadcasted_iota(jnp.int32, (heads, HEAD_SIZE), 1)
    even = (col & 1) == 0
    for d in range(owners):
        limit = ask_ref[d, :, 2 * HEAD_SIZE :].astype(F32) * 2.0
        limit = jnp.concatenate([limit] * 2, axis=0)
        limit = jnp.concatenate([limit] * (span // HEAD_SIZE), axis=1)
        allowed = even & (col.astype(F32) < limit)
        s = jnp.where(allowed, s_ref[d * lists : (d + 1) * lists, :], LOWEST)
        top = jnp.max(s, axis=1, keepdims=True)
        p = jnp.where(allowed, jnp.exp2((s - top) * SCALE), 0.0)
        total = jnp.sum(p, axis=1, keepdims=True)
        p_ref[d * lists : (d + 1) * lists, :] = pltpu.roll(p, 1, 1).astype(BF16)
        seen = total > 0.0
        level = jnp.where(seen, top * SCALE + jnp.log2(jnp.where(seen, total, 1.0)), LOWEST)
        level = jnp.broadcast_to(level, (lists, HEAD_SIZE))
        high = level.astype(BF16).astype(F32)
        rest = level - high
        middle = rest.astype(BF16).astype(F32)
        stat = jnp.zeros((heads, HEAD_SIZE), F32)
        for t in range(2):
            for n, piece in enumerate((high, middle, rest - middle)):
                stat = jnp.where(lane == 3 * t + n, piece[t * heads : (t + 1) * heads], stat)
        out_ref[d, :, 2 * HEAD_SIZE :] = stat.astype(BF16)
        scale_ref[d * lists : (d + 1) * lists, :] = jnp.broadcast_to(
            jnp.where(seen, 1.0 / jnp.where(seen, total, 1.0), 0.0), (lists, HEAD_SIZE)
        )
    for d in range(owners):
        o = dot_nn(p_ref[d * lists : (d + 1) * lists, :], pool_ref[place_ref[d]])
        o = o * scale_ref[d * lists : (d + 1) * lists, :]
        out_ref[d, :, : 2 * HEAD_SIZE] = jnp.concatenate([o[:heads], o[heads:]], axis=1).astype(BF16)


def look(place, ask, pool):
    owners, heads, width = ask.shape
    span = pool.shape[1]
    rows = 2 * owners * heads
    return pl.pallas_call(
        look_body,
        out_shape=jax.ShapeDtypeStruct(ask.shape, BF16),
        in_specs=[SMEM, VMEM, VMEM],
        out_specs=VMEM,
        scratch_shapes=[
            pltpu.VMEM((rows, span), F32),
            pltpu.VMEM((rows, span), BF16),
            pltpu.VMEM((rows, HEAD_SIZE), F32),
        ],
        compiler_params=params(24),
        cost_estimate=pl.CostEstimate(
            flops=4 * rows * span * HEAD_SIZE, bytes_accessed=2 * owners * span * HEAD_SIZE, transcendentals=0
        ),
        name="look_in_blocks",
    )(place, ask, pool)


def gather_body(row_ref, answer_ref, q_ref, new_ref, out_ref, level_ref, top_ref, sum_ref, acc_ref, flat_ref):
    holders = answer_ref.shape[0]
    rows, lists = q_ref.shape[0], q_ref.shape[1]
    heads = lists // 2
    lane = lax.broadcasted_iota(jnp.int32, (lists, HEAD_SIZE), 1)
    later = lax.broadcasted_iota(jnp.int32, (lists, HEAD_SIZE), 0) >= heads
    own = []
    for r in range(rows):
        q = q_ref[r].astype(F32)
        new = new_ref[r].astype(F32)
        scores = []
        for t in range(2):
            s = jnp.sum(q * new[2 * t : 2 * t + 1, :], axis=1, keepdims=True) * SCALE
            scores.append(jnp.broadcast_to(s, (lists, HEAD_SIZE)))
        scores[1] = jnp.where(later, scores[1], LOWEST)
        top_ref[r] = jnp.maximum(scores[0], scores[1])
        own.append((scores, new))
    for d in range(holders):
        stat = answer_ref[d, :, 2 * HEAD_SIZE :].astype(F32)
        stat = jnp.concatenate([stat, stat], axis=0)
        level = jnp.sum(jnp.where((lane < 6) & ((lane >= 3) == later), stat, 0.0), axis=1, keepdims=True)
        level_ref[d] = jnp.broadcast_to(level, (lists, HEAD_SIZE))
    for d in range(holders):
        r = row_ref[d]
        top_ref[r] = jnp.maximum(top_ref[r], level_ref[d])
    for r in range(rows):
        scores, new = own[r]
        first = jnp.exp2(scores[0] - top_ref[r])
        second = jnp.exp2(scores[1] - top_ref[r])
        sum_ref[r] = first + second
        acc_ref[r] = first * new[1:2, :] + second * new[3:4, :]
    for d in range(holders):
        r = row_ref[d]
        weight = jnp.exp2(level_ref[d] - top_ref[r])
        sum_ref[r] = sum_ref[r] + weight
        o = answer_ref[d, :, : 2 * HEAD_SIZE].astype(F32)
        o = jnp.concatenate([o[:, :HEAD_SIZE], o[:, HEAD_SIZE:]], axis=0)
        acc_ref[r] = acc_ref[r] + weight * o
    for r in range(rows):
        o = acc_ref[r] / sum_ref[r]
        for t in range(2):
            for h in range(heads):
                flat_ref[2 * r + t : 2 * r + t + 1, h * HEAD_SIZE : (h + 1) * HEAD_SIZE] = o[
                    t * heads + h : t * heads + h + 1, :
                ]
    out_ref[...] = flat_ref[...].astype(BF16)


def gather_answers(row_of, answer, q, new):
    rows, lists, width = q.shape
    holders = answer.shape[0]
    heads = lists // 2
    state = pltpu.VMEM((rows, lists, width), F32)
    return pl.pallas_call(
        gather_body,
        out_shape=jax.ShapeDtypeStruct((2 * rows, heads * width), BF16),
        in_specs=[SMEM, VMEM, VMEM, VMEM],
        out_specs=VMEM,
        scratch_shapes=[
            pltpu.VMEM((holders, lists, width), F32),
            state,
            state,
            state,
            pltpu.VMEM((2 * rows, heads * width), F32),
        ],
        compiler_params=params(16),
        name="gather_answers",
    )(row_of, answer, q, new)


def project_body(place_ref, own_ref, w_ref, *refs):
    ref_list, out_ref, total_ref, rows_ref = refs[:-3], refs[-3], refs[-2], refs[-1]
    rows = own_ref.shape[0]
    rows_ref[:rows, :] = own_ref[...]
    for n, ref in enumerate(ref_list):
        rows_ref[(n + 1) * rows : (n + 2) * rows, :] = ref[ref.shape[0] - rows :, :]
    total = dot_nn(rows_ref[...], w_ref[...])
    for n in range(rows_ref.shape[0] // 8):
        at = pl.multiple_of(place_ref[n], 8)
        total_ref[pl.ds(at, 8), :] = total[8 * n : 8 * n + 8]
    out_ref[...] = total_ref[...].astype(BF16)


def project(place, own, w, parts):
    rows = own.shape[0] * (len(parts) + 1)
    return pl.pallas_call(
        project_body,
        out_shape=jax.ShapeDtypeStruct((rows, w.shape[1]), BF16),
        in_specs=[SMEM] + [VMEM] * (len(parts) + 2),
        out_specs=VMEM,
        scratch_shapes=[pltpu.VMEM((rows, w.shape[1]), F32), pltpu.VMEM((rows, own.shape[1]), BF16)],
        compiler_params=params(16),
        name="project",
    )(place, own, w, *parts)


def shards(
    q_stretch,
    stretch_key_value,
    context_key_value,
    dec_q,
    dec_new,
    pool_key_value,
    block_table,
    cache_len,
    w_out,
):
    me = lax.axis_index(CTX)
    z = lax.axis_index("z")
    cycle = lax.axis_size(CTX)
    stretch = q_stretch.shape[0]
    rows_dev, nblk = dec_q.shape[0], block_table.shape[1]
    pool_dev, block_size = pool_key_value.shape[:2]

    def after(x, *others):
        return lax.optimization_barrier((x, *others))[0]

    def swap(x, name):
        return lax.ppermute(x, name, [(0, 1), (1, 0)])

    def turn(x, step):
        return lax.ppermute(x, "z", [(n, (n + step) % Z_CHIPS) for n in range(Z_CHIPS)])

    ask, row_of, q_rows, kv = prepare(
        me.reshape(1).astype(jnp.int32),
        block_table.T,
        cache_len,
        dec_q,
        context_key_value.reshape(-1, HEAD_SIZE),
        stretch_key_value.reshape(-1, HEAD_SIZE),
        cycle,
    )
    pool, q_stretch, ask = lax.optimization_barrier((pool_key_value, q_stretch, ask))
    ask = lax.all_to_all(ask, CTX, split_axis=0, concat_axis=0, tiled=True)
    table = block_table.reshape(cycle, rows_dev * nblk)
    place = jnp.sum(jnp.where(table // pool_dev == me, table % pool_dev, 0), axis=1)

    kv_core, kv_y = swap(kv, "core"), swap(kv, "y")
    right = [q_stretch, turn(q_stretch, 1), turn(q_stretch, 2)]
    left = [q_stretch, turn(q_stretch, -1), turn(q_stretch, -2)]
    blocks = fetch(pool.reshape(pool_dev, 2 * block_size, HEAD_SIZE))
    look_out = look(place, ask, blocks)
    right[1], right[2], left[1], left[2], look_out = lax.optimization_barrier(
        (right[1], right[2], left[1], left[2], look_out)
    )
    answer = lax.all_to_all(look_out, CTX, split_axis=0, concat_axis=0, tiled=True)
    farther = turn(jnp.concatenate([right[1], right[2]], axis=0), 2)
    left.append(turn(left[1], -2))
    kv_yc = swap(after(kv_y, look_out), "core")
    sets = [kv, kv_core, kv_y, kv_yc]

    shifts = jnp.arange(Z_CHIPS, dtype=jnp.int32)
    corners = jnp.arange(2 * CORES, dtype=jnp.int32)
    corners = me ^ (corners // CORES * CORES * Z_CHIPS + corners % CORES)
    askers = me + ((z - shifts + Z_CHIPS) % Z_CHIPS - z) * CORES
    deltas = (askers[:, None] - corners[None, :]) * stretch

    keys, values = stack(sets)
    own = attend(0, deltas, q_stretch, keys, values)
    own, answer = lax.optimization_barrier((own, answer))
    attn = gather_answers(row_of, answer, q_rows, dec_new.reshape(rows_dev, 4, HEAD_SIZE))
    attn_core = swap(attn, "core")
    sets, _ = lax.optimization_barrier((sets, attn))
    keys, values = stack(sets)
    pair = jnp.concatenate([attn, after(attn_core, keys)], axis=0)
    pair_y = swap(pair, "y")

    def go(shift, previous, part=None, rider=None, carry=True):
        half = None
        if shift > 2:
            queries, half = farther, shift - 3
        else:
            queries = right[shift] if shift >= 0 else left[-shift]
        return attend(shift % Z_CHIPS, after(deltas, *previous), queries, keys, values, part, rider, carry, half)

    attn = jnp.concatenate([pair, pair_y], axis=0)
    out = go(4, [attn], None, attn)
    from_right = [turn(out, -1)]
    out = go(-3, [out], None, attn)
    from_left = [turn(out, 1)]
    out = go(3, [out], from_right[-1])
    from_right.append(turn(out, -1))
    out = go(-2, [out], from_left[-1])
    from_left.append(turn(out, 1))
    out = go(2, [out], from_right[-1])
    from_right.append(turn(out, -1))
    out = go(-1, [out], from_left[-1])
    from_left.append(turn(out, 1))
    rest = from_right[2][stretch + 16 :]
    farthest = turn(rest, -1)
    out = go(1, [out, rest], from_right[2], None, False)
    last = turn(out, -1)

    relative = jnp.where(shifts > Z_CHIPS // 2, Z_CHIPS // 2 - shifts, shifts)
    there = ((z + relative + Z_CHIPS) % Z_CHIPS - z) * CORES
    holders = ((there[:, None] + corners[None, :]) * (2 * rows_dev)).reshape(-1)
    partial_out = project(holders, after(attn, out), w_out, [*from_right, farthest, *from_left])
    shares = lax.axis_size(("grp", "tp"))
    pieces = lax.all_to_all(
        partial_out.reshape(shares, -1, partial_out.shape[1]), ("grp", "tp"), split_axis=0, concat_axis=0, tiled=True
    )
    pre_out = merge([own, last, from_left[2]], stretch)
    dec_out = jnp.sum(pieces.astype(F32), axis=0).astype(BF16)
    return (pre_out, dec_out.reshape(-1, 2, dec_out.shape[1]))


def solution(mesh):
    shape = mesh.devices.shape
    fine = jax.sharding.Mesh(mesh.devices.reshape(-1, Z_CHIPS, CORES, *shape[1:]), (*CTX, *mesh.axis_names[1:]))
    placed = (
        P(CTX, ("grp", "tp")),
        P(CTX, None, ("grp", "tp")),
        P(CTX, None, ("grp", "tp")),
        P(CTX, None, ("grp", "tp")),
        P(CTX, None, None, ("grp", "tp")),
        P(CTX, None, None, ("grp", "tp")),
        P(),
        P(CTX),
        P(("grp", "tp"), CTX),
    )
    return jax.shard_map(
        shards,
        mesh=fine,
        in_specs=placed,
        out_specs=(P(CTX, ("grp", "tp")), P(("grp", "tp"), None, CTX)),
        check_vma=False,
    )
```

```python
import functools
import math

import jax
import jax.numpy as jnp
from jax import lax
from jax.experimental import pallas as pl
from jax.experimental.pallas import tpu as pltpu
from jax.sharding import PartitionSpec as P

HEAD_SIZE = 128
CORES = 2
Z_CHIPS = 8
CONTEXT_DEV = 1280
BLOCK = 128
CTX = ("y", "z", "core")
SCALE = math.log2(math.e) / math.sqrt(HEAD_SIZE)
LOWEST = -1e30
F32 = jnp.float32
BF16 = jnp.bfloat16
VMEM = pl.BlockSpec(memory_space=pltpu.VMEM)
SMEM = pl.BlockSpec(memory_space=pltpu.SMEM)
HBM = pl.BlockSpec(memory_space=pltpu.HBM)


def params(mib):
    return pltpu.CompilerParams(vmem_limit_bytes=mib * 1024 * 1024)


def in_hbm(x):
    return pltpu.with_memory_space_constraint(x, pltpu.HBM)


def in_vmem(x):
    return pltpu.with_memory_space_constraint(x, pltpu.VMEM)


def dot_nt(a, b):
    return lax.dot_general(a, b, (((1,), (1,)), ((), ())), preferred_element_type=F32)


def dot_nn(a, b):
    return lax.dot_general(a, b, (((1,), (0,)), ((), ())), preferred_element_type=F32)


def prepare_body(
    me_ref,
    table_hbm,
    length_hbm,
    q_hbm,
    context_hbm,
    stretch_hbm,
    ask_ref,
    row_ref,
    rows_ref,
    kv_ref,
    list_ref,
    table_ref,
    length_ref,
    q_ref,
    context_ref,
    stretch_ref,
    sem,
):
    pieces = 5
    total = context_ref.shape[0]
    step = total // pieces
    copies = [
        pltpu.make_async_copy(q_hbm, q_ref, sem.at[0]),
        pltpu.make_async_copy(table_hbm, table_ref, sem.at[1]),
        pltpu.make_async_copy(length_hbm, length_ref, sem.at[2]),
    ]
    for n in range(pieces):
        rows = pl.ds(n * step, step)
        copies.append(pltpu.make_async_copy(context_hbm.at[rows], context_ref.at[rows], sem.at[3 + n]))
    copies.append(pltpu.make_async_copy(stretch_hbm, stretch_ref, sem.at[3 + pieces]))
    for copy in copies:
        copy.start()

    rows_dev = length_ref.shape[0]
    nblk = table_ref.shape[0]
    lists = rows_ref.shape[1]
    heads = lists // 2
    pool_dev = ask_ref.shape[0]
    copies[0].wait()
    for r in range(rows_dev):
        q = q_ref[r].astype(F32)
        for t in range(2):
            for h in range(heads):
                at = t * heads + h
                list_ref[r, at : at + 1, :] = q[t : t + 1, h * HEAD_SIZE : (h + 1) * HEAD_SIZE]
    copies[1].wait()
    copies[2].wait()
    for r in range(rows_dev):
        listed = list_ref[r]
        rows_ref[r] = listed.astype(BF16)
        asked = jnp.concatenate([listed[:heads], listed[heads:]], axis=1).astype(BF16)
        for n in range(nblk):
            holder = table_ref[n, me_ref[0] * rows_dev + r] // pool_dev
            left = jnp.clip(length_ref[r] - n * BLOCK, 0, BLOCK).astype(F32)
            ask_ref[holder, :, : 2 * HEAD_SIZE] = asked
            ask_ref[holder, :, 2 * HEAD_SIZE :] = jnp.full((heads, HEAD_SIZE), left, F32).astype(BF16)
            row_ref[holder] = r

    def split(rows, at):
        count = rows.shape[0]
        half = count // 2
        i = lax.broadcasted_iota(jnp.int32, (count, count), 0)
        j = lax.broadcasted_iota(jnp.int32, (count, count), 1)
        source = jnp.where(i < half, 2 * i, 2 * (i - half) + 1)
        pick = jnp.where(j == source, 1.0, 0.0).astype(BF16)
        parted = dot_nn(pick, rows).astype(BF16)
        kv_ref[0, at : at + half, :] = parted[:half]
        kv_ref[1, at : at + half, :] = parted[half:]

    for copy in copies[3:]:
        copy.wait()
    for start in range(0, total, 256):
        split(context_ref[start : start + 256, :], start // 2)
    split(stretch_ref[...], total // 2)


def prepare(me, table, length, q, context, stretch, holders):
    rows_dev = length.shape[0]
    lists = 2 * q.shape[2] // HEAD_SIZE
    rows = (context.shape[0] + stretch.shape[0]) // 2
    return pl.pallas_call(
        prepare_body,
        out_shape=[
            jax.ShapeDtypeStruct((holders, lists // 2, 3 * HEAD_SIZE), BF16),
            jax.ShapeDtypeStruct((holders,), jnp.int32),
            jax.ShapeDtypeStruct((rows_dev, lists, HEAD_SIZE), BF16),
            jax.ShapeDtypeStruct((2, rows, HEAD_SIZE), BF16),
        ],
        in_specs=[SMEM] + [HBM] * 5,
        out_specs=[VMEM, SMEM, VMEM, VMEM],
        scratch_shapes=[
            pltpu.VMEM((rows_dev, lists, HEAD_SIZE), F32),
            pltpu.SMEM(table.shape, jnp.int32),
            pltpu.SMEM(length.shape, jnp.int32),
            pltpu.VMEM(q.shape, BF16),
            pltpu.VMEM(context.shape, BF16),
            pltpu.VMEM(stretch.shape, BF16),
            pltpu.SemaphoreType.DMA((9,)),
        ],
        compiler_params=params(16),
        name="prepare",
    )(me, *(in_hbm(x) for x in (table, length, q, context, stretch)))


def stack_body(*refs):
    kv_refs, k_ref, v_ref = refs[:-2], refs[-2], refs[-1]
    sets = len(kv_refs)
    stretch = v_ref.shape[0] // sets - CONTEXT_DEV
    one = jnp.where(diagonal(), 1.0, 0.0).astype(BF16)
    v_ref[:, HEAD_SIZE:] = jnp.ones((v_ref.shape[0], HEAD_SIZE), BF16)
    for n, ref in enumerate(kv_refs):
        first, last = n * CONTEXT_DEV, sets * CONTEXT_DEV + n * stretch
        for at in range(0, CONTEXT_DEV, 256):
            k_ref[:, first + at : first + at + 256] = dot_nt(one, ref[0, at : at + 256, :]).astype(BF16)
        v_ref[first : first + CONTEXT_DEV, :HEAD_SIZE] = ref[1, :CONTEXT_DEV, :]
        v_ref[last : last + stretch, :HEAD_SIZE] = ref[1, CONTEXT_DEV:, :]
    k = jnp.concatenate([ref[0, CONTEXT_DEV:, :] for ref in kv_refs], axis=0)
    k_ref[:, sets * CONTEXT_DEV :] = dot_nt(one, k).astype(BF16)


def stack(sets):
    keys = len(sets) * sets[0].shape[1]
    return pl.pallas_call(
        stack_body,
        out_shape=[
            jax.ShapeDtypeStruct((HEAD_SIZE, keys), BF16),
            jax.ShapeDtypeStruct((keys, 2 * HEAD_SIZE), BF16),
        ],
        in_specs=[VMEM] * len(sets),
        out_specs=[VMEM, VMEM],
        compiler_params=params(16),
        name="stack",
    )(*sets)


def diagonal():
    i = lax.broadcasted_iota(jnp.int32, (HEAD_SIZE, HEAD_SIZE), 0)
    j = lax.broadcasted_iota(jnp.int32, (HEAD_SIZE, HEAD_SIZE), 1)
    return i == j


def read_part(ref, stretch, first, heads):
    columns = range(first * HEAD_SIZE, (first + heads) * HEAD_SIZE, HEAD_SIZE)
    outputs = jnp.concatenate([ref[:stretch, c : c + HEAD_SIZE] for c in columns], axis=0)
    stat = ref[stretch : stretch + 16, first * stretch : (first + heads) * stretch].astype(F32)
    level = stat[0:1] + stat[1:2] + stat[2:3]
    columns = []
    for g in range(0, heads * stretch, HEAD_SIZE):
        column = jnp.sum(jnp.where(diagonal(), level[:, g : g + HEAD_SIZE], 0.0), axis=1, keepdims=True)
        columns.append(jnp.broadcast_to(column, (HEAD_SIZE, HEAD_SIZE)))
    return outputs.astype(F32), jnp.concatenate(columns, axis=0)


def join(outputs, levels):
    top = functools.reduce(jnp.maximum, levels)
    weights = [jnp.exp2(level - top) for level in levels]
    total = functools.reduce(jnp.add, weights)
    mixed = functools.reduce(jnp.add, [weight * output for weight, output in zip(weights, outputs)])
    return mixed / total, top + jnp.log2(total)


def write_outputs(ref, outputs, stretch, first):
    outputs = outputs.astype(BF16)
    for h in range(outputs.shape[0] // stretch):
        ref[:stretch, (first + h) * HEAD_SIZE : (first + h + 1) * HEAD_SIZE] = outputs[h * stretch : (h + 1) * stretch]


def write_level(ref, level, stretch, first):
    rows = level.shape[0]
    lines = []
    for g in range(0, rows, HEAD_SIZE):
        lines.append(jnp.sum(jnp.where(diagonal(), level[g : g + HEAD_SIZE], 0.0), axis=0, keepdims=True))
    level = jnp.concatenate(lines, axis=1)
    high = level.astype(BF16).astype(F32)
    rest = level - high
    middle = rest.astype(BF16).astype(F32)
    row = lax.broadcasted_iota(jnp.int32, (16, rows), 0)
    stat = jnp.where(row == 0, high, jnp.where(row == 1, middle, jnp.where(row == 2, rest - middle, 0.0)))
    ref[stretch : stretch + 16, first * stretch : first * stretch + rows] = stat.astype(BF16)


def attend_body(which, arrived, riders, delta_ref, k_ref, v_ref, q_ref, *refs):
    refs = list(refs)
    part_ref = refs.pop(0) if arrived else None
    rider_ref = refs.pop(0) if riders == "own" else part_ref
    out_ref, p_ref, total_ref, top_ref = refs
    stretch, width = q_ref.shape
    sets = delta_ref.shape[1]
    keys = v_ref.shape[0]
    halves, rows = p_ref.shape[:2]
    heads = rows // stretch
    chunk = 256

    if riders is not None:
        start = 0 if riders == "own" else stretch + 16
        out_ref[stretch + 16 :, :] = rider_ref[start:, :]
    out_ref[stretch : stretch + 16, halves * rows :] = jnp.zeros((16, width - halves * rows), BF16)

    def queries(n):
        columns = range(n * heads * HEAD_SIZE, (n + 1) * heads * HEAD_SIZE, HEAD_SIZE)
        return jnp.concatenate([q_ref[:, c : c + HEAD_SIZE] for c in columns], axis=0)

    def score(q, k, masked):
        s = dot_nn(q, k)
        if masked:
            row = lax.rem(lax.broadcasted_iota(jnp.int32, s.shape, 0), stretch)
            col = lax.broadcasted_iota(jnp.int32, s.shape, 1)
            bound = delta_ref[which, sets - 1] + (sets - 1) * stretch - col
            for m in reversed(range(sets - 1)):
                bound = jnp.where(col < (m + 1) * stretch, delta_ref[which, m] + m * stretch - col, bound)
            s = jnp.where(row + bound >= 0, s, LOWEST)
        return s

    def highest(s):
        parts = [s[:, c : c + HEAD_SIZE] for c in range(0, s.shape[1], HEAD_SIZE)]
        return functools.reduce(jnp.maximum, parts)

    def spread(top):
        return jnp.broadcast_to(jnp.max(top, axis=1, keepdims=True), (rows, HEAD_SIZE)) * SCALE

    def weigh(s, top):
        parts = [s[:, c : c + HEAD_SIZE] for c in range(0, s.shape[1], HEAD_SIZE)]
        return jnp.concatenate([jnp.exp2(part * SCALE - top) for part in parts], axis=1).astype(BF16)

    def finish(n, total, top):
        weight = total[:, HEAD_SIZE:]
        output, level = total[:, :HEAD_SIZE] / weight, top + jnp.log2(weight)
        if arrived:
            other, other_level = read_part(part_ref, stretch, n * heads, heads)
            output, level = join([output, other], [level, other_level])
        write_outputs(out_ref, output, stretch, n * heads)
        write_level(out_ref, level, stretch, n * heads)

    steps = keys // chunk
    ends = [steps * chunk * n // 21 for n in (5, 10, 15, 18, 20, 21)]
    tops = [spread(highest(score(queries(n), k_ref[:, :chunk], False))) for n in range(halves)]
    sums = []
    for n in range(halves):
        q = queries(n)
        total = None
        begun = 0
        for at in range(0, keys, chunk):
            masked = at >= sets * CONTEXT_DEV
            p_ref[n, :, at : at + chunk] = weigh(score(q, k_ref[:, at : at + chunk], masked), tops[n])
            done = at + chunk
            if done in ends:
                part = dot_nn(p_ref[n, :, begun:done], v_ref[begun:done, :])
                total = part if total is None else total + part
                begun = done
        sums.append(total[:, HEAD_SIZE:])
        finish(n, total, tops[n])

    @pl.when(jnp.logical_not(jnp.max(functools.reduce(jnp.maximum, sums)) < 1e37))
    def again():
        for n in range(halves):
            q = queries(n)
            last = score(q, k_ref[:, keys - chunk :], True)

            def climb(m, top):
                k = k_ref[:, pl.ds(pl.multiple_of(m * chunk, chunk), chunk)]
                return jnp.maximum(top, highest(score(q, k, False)))

            top_ref[...] = spread(lax.fori_loop(0, steps - 1, climb, highest(last)))
            total_ref[...] = dot_nn(weigh(last, top_ref[...]), v_ref[keys - chunk :, :])

            def add(m, carry):
                at = pl.ds(pl.multiple_of(m * chunk, chunk), chunk)
                total_ref[...] += dot_nn(weigh(score(q, k_ref[:, at], False), top_ref[...]), v_ref[at, :])
                return carry

            lax.fori_loop(0, steps - 1, add, 0)
            finish(n, total_ref[...], top_ref[...])


def attend(which, deltas, queries, keys, values, part=None, rider=None, carry=True):
    stretch, width = queries.shape
    rows = width // HEAD_SIZE * stretch // 2
    count = values.shape[0]
    operands = [deltas, keys, values, queries]
    out_rows = stretch + 16
    riders = None
    if part is not None:
        operands.append(part)
        if carry:
            riders = "arrived"
            out_rows = part.shape[0]
    if rider is not None:
        riders = "own"
        operands.append(rider)
        out_rows += rider.shape[0]
    return pl.pallas_call(
        functools.partial(attend_body, which, part is not None, riders),
        out_shape=jax.ShapeDtypeStruct((out_rows, width), BF16),
        in_specs=[SMEM] + [VMEM] * (len(operands) - 1),
        out_specs=VMEM,
        scratch_shapes=[
            pltpu.VMEM((2, rows, count), BF16),
            pltpu.VMEM((rows, 2 * HEAD_SIZE), F32),
            pltpu.VMEM((rows, HEAD_SIZE), F32),
        ],
        compiler_params=params(24),
        cost_estimate=pl.CostEstimate(
            flops=16 * rows * count * HEAD_SIZE,
            bytes_accessed=4 * count * HEAD_SIZE,
            transcendentals=2 * rows * count,
        ),
        name="attend",
    )(*operands)


def merge_body(*refs):
    part_refs, out_ref = refs[:-1], refs[-1]
    stretch = out_ref.shape[0]
    read = [read_part(ref, stretch, 0, out_ref.shape[1] // HEAD_SIZE) for ref in part_refs]
    output, _ = join([x for x, _ in read], [x for _, x in read])
    write_outputs(out_ref, output, stretch, 0)


def merge(parts, stretch):
    return pl.pallas_call(
        merge_body,
        out_shape=jax.ShapeDtypeStruct((stretch, parts[0].shape[1]), BF16),
        in_specs=[VMEM] * len(parts),
        out_specs=VMEM,
        compiler_params=params(16),
        name="merge",
    )(*parts)


def fetch_body(pool_hbm, pool_ref, sem):
    copies = []
    step = pool_ref.shape[0] // sem.shape[0]
    for n in range(sem.shape[0]):
        blocks = pl.ds(n * step, step)
        copies.append(pltpu.make_async_copy(pool_hbm.at[blocks], pool_ref.at[blocks], sem.at[n]))
        copies[n].start()
    for copy in copies:
        copy.wait()


def fetch(pool):
    return pl.pallas_call(
        fetch_body,
        out_shape=pltpu.VMEM(pool.shape, BF16),
        in_specs=[HBM],
        out_specs=VMEM,
        scratch_shapes=[pltpu.SemaphoreType.DMA((4,))],
        compiler_params=params(16),
        name="fetch_blocks",
    )(in_hbm(pool))


def look_body(place_ref, ask_ref, pool_ref, out_ref, s_ref, p_ref, scale_ref):
    owners, heads = ask_ref.shape[:2]
    lists = 2 * heads
    span = pool_ref.shape[1]
    for d in range(owners):
        q = ask_ref[d, :, : 2 * HEAD_SIZE].astype(F32)
        q = jnp.concatenate([q[:, :HEAD_SIZE], q[:, HEAD_SIZE:]], axis=0).astype(BF16)
        s_ref[d * lists : (d + 1) * lists, :] = dot_nt(q, pool_ref[place_ref[d]])
    col = lax.broadcasted_iota(jnp.int32, (lists, span), 1)
    lane = lax.broadcasted_iota(jnp.int32, (heads, HEAD_SIZE), 1)
    even = (col & 1) == 0
    for d in range(owners):
        limit = ask_ref[d, :, 2 * HEAD_SIZE :].astype(F32) * 2.0
        limit = jnp.concatenate([limit] * 2, axis=0)
        limit = jnp.concatenate([limit] * (span // HEAD_SIZE), axis=1)
        allowed = even & (col.astype(F32) < limit)
        s = jnp.where(allowed, s_ref[d * lists : (d + 1) * lists, :], LOWEST)
        top = jnp.max(s, axis=1, keepdims=True)
        p = jnp.where(allowed, jnp.exp2((s - top) * SCALE), 0.0)
        total = jnp.sum(p, axis=1, keepdims=True)
        p_ref[d * lists : (d + 1) * lists, :] = pltpu.roll(p, 1, 1).astype(BF16)
        seen = total > 0.0
        level = jnp.where(seen, top * SCALE + jnp.log2(jnp.where(seen, total, 1.0)), LOWEST)
        level = jnp.broadcast_to(level, (lists, HEAD_SIZE))
        high = level.astype(BF16).astype(F32)
        rest = level - high
        middle = rest.astype(BF16).astype(F32)
        stat = jnp.zeros((heads, HEAD_SIZE), F32)
        for t in range(2):
            for n, piece in enumerate((high, middle, rest - middle)):
                stat = jnp.where(lane == 3 * t + n, piece[t * heads : (t + 1) * heads], stat)
        out_ref[d, :, 2 * HEAD_SIZE :] = stat.astype(BF16)
        scale_ref[d * lists : (d + 1) * lists, :] = jnp.broadcast_to(
            jnp.where(seen, 1.0 / jnp.where(seen, total, 1.0), 0.0), (lists, HEAD_SIZE)
        )
    for d in range(owners):
        o = dot_nn(p_ref[d * lists : (d + 1) * lists, :], pool_ref[place_ref[d]])
        o = o * scale_ref[d * lists : (d + 1) * lists, :]
        out_ref[d, :, : 2 * HEAD_SIZE] = jnp.concatenate([o[:heads], o[heads:]], axis=1).astype(BF16)


def look(place, ask, pool):
    owners, heads, width = ask.shape
    span = pool.shape[1]
    rows = 2 * owners * heads
    return pl.pallas_call(
        look_body,
        out_shape=jax.ShapeDtypeStruct(ask.shape, BF16),
        in_specs=[SMEM, VMEM, VMEM],
        out_specs=VMEM,
        scratch_shapes=[
            pltpu.VMEM((rows, span), F32),
            pltpu.VMEM((rows, span), BF16),
            pltpu.VMEM((rows, HEAD_SIZE), F32),
        ],
        compiler_params=params(24),
        cost_estimate=pl.CostEstimate(
            flops=4 * rows * span * HEAD_SIZE, bytes_accessed=2 * owners * span * HEAD_SIZE, transcendentals=0
        ),
        name="look_in_blocks",
    )(place, ask, pool)


def gather_body(row_ref, answer_ref, q_ref, new_ref, out_ref, level_ref, top_ref, sum_ref, acc_ref, flat_ref):
    holders = answer_ref.shape[0]
    rows, lists = q_ref.shape[0], q_ref.shape[1]
    heads = lists // 2
    lane = lax.broadcasted_iota(jnp.int32, (lists, HEAD_SIZE), 1)
    later = lax.broadcasted_iota(jnp.int32, (lists, HEAD_SIZE), 0) >= heads
    own = []
    for r in range(rows):
        q = q_ref[r].astype(F32)
        new = new_ref[r].astype(F32)
        scores = []
        for t in range(2):
            s = jnp.sum(q * new[2 * t : 2 * t + 1, :], axis=1, keepdims=True) * SCALE
            scores.append(jnp.broadcast_to(s, (lists, HEAD_SIZE)))
        scores[1] = jnp.where(later, scores[1], LOWEST)
        top_ref[r] = jnp.maximum(scores[0], scores[1])
        own.append((scores, new))
    for d in range(holders):
        stat = answer_ref[d, :, 2 * HEAD_SIZE :].astype(F32)
        stat = jnp.concatenate([stat, stat], axis=0)
        level = jnp.sum(jnp.where((lane < 6) & ((lane >= 3) == later), stat, 0.0), axis=1, keepdims=True)
        level_ref[d] = jnp.broadcast_to(level, (lists, HEAD_SIZE))
    for d in range(holders):
        r = row_ref[d]
        top_ref[r] = jnp.maximum(top_ref[r], level_ref[d])
    for r in range(rows):
        scores, new = own[r]
        first = jnp.exp2(scores[0] - top_ref[r])
        second = jnp.exp2(scores[1] - top_ref[r])
        sum_ref[r] = first + second
        acc_ref[r] = first * new[1:2, :] + second * new[3:4, :]
    for d in range(holders):
        r = row_ref[d]
        weight = jnp.exp2(level_ref[d] - top_ref[r])
        sum_ref[r] = sum_ref[r] + weight
        o = answer_ref[d, :, : 2 * HEAD_SIZE].astype(F32)
        o = jnp.concatenate([o[:, :HEAD_SIZE], o[:, HEAD_SIZE:]], axis=0)
        acc_ref[r] = acc_ref[r] + weight * o
    for r in range(rows):
        o = acc_ref[r] / sum_ref[r]
        for t in range(2):
            for h in range(heads):
                flat_ref[2 * r + t : 2 * r + t + 1, h * HEAD_SIZE : (h + 1) * HEAD_SIZE] = o[
                    t * heads + h : t * heads + h + 1, :
                ]
    out_ref[...] = flat_ref[...].astype(BF16)


def gather_answers(row_of, answer, q, new):
    rows, lists, width = q.shape
    holders = answer.shape[0]
    heads = lists // 2
    state = pltpu.VMEM((rows, lists, width), F32)
    return pl.pallas_call(
        gather_body,
        out_shape=jax.ShapeDtypeStruct((2 * rows, heads * width), BF16),
        in_specs=[SMEM, VMEM, VMEM, VMEM],
        out_specs=VMEM,
        scratch_shapes=[
            pltpu.VMEM((holders, lists, width), F32),
            state,
            state,
            state,
            pltpu.VMEM((2 * rows, heads * width), F32),
        ],
        compiler_params=params(16),
        name="gather_answers",
    )(row_of, answer, q, new)


def project_body(place_ref, own_ref, w_ref, *refs):
    ref_list, out_ref, total_ref, rows_ref = refs[:-3], refs[-3], refs[-2], refs[-1]
    rows = own_ref.shape[0]
    rows_ref[:rows, :] = own_ref[...]
    for n, ref in enumerate(ref_list):
        rows_ref[(n + 1) * rows : (n + 2) * rows, :] = ref[ref.shape[0] - rows :, :]
    total = dot_nn(rows_ref[...], w_ref[...])
    for n in range(rows_ref.shape[0] // 8):
        at = pl.multiple_of(place_ref[n], 8)
        total_ref[pl.ds(at, 8), :] = total[8 * n : 8 * n + 8]
    out_ref[...] = total_ref[...].astype(BF16)


def project(place, own, w, parts):
    rows = own.shape[0] * (len(parts) + 1)
    return pl.pallas_call(
        project_body,
        out_shape=jax.ShapeDtypeStruct((rows, w.shape[1]), BF16),
        in_specs=[SMEM] + [VMEM] * (len(parts) + 2),
        out_specs=VMEM,
        scratch_shapes=[pltpu.VMEM((rows, w.shape[1]), F32), pltpu.VMEM((rows, own.shape[1]), BF16)],
        compiler_params=params(16),
        name="project",
    )(place, own, w, *parts)


def shards(
    q_stretch,
    stretch_key_value,
    context_key_value,
    dec_q,
    dec_new,
    pool_key_value,
    block_table,
    cache_len,
    w_out,
):
    me = lax.axis_index(CTX)
    z = lax.axis_index("z")
    cycle = lax.axis_size(CTX)
    stretch = q_stretch.shape[0]
    rows_dev, nblk = dec_q.shape[0], block_table.shape[1]
    pool_dev, block_size = pool_key_value.shape[:2]

    def after(x, *others):
        return lax.optimization_barrier((x, *others))[0]

    def swap(x, name):
        return lax.ppermute(x, name, [(0, 1), (1, 0)])

    def turn(x, step):
        return lax.ppermute(x, "z", [(n, (n + step) % Z_CHIPS) for n in range(Z_CHIPS)])

    ask, row_of, q_rows, kv = prepare(
        me.reshape(1).astype(jnp.int32),
        block_table.T,
        cache_len,
        dec_q,
        context_key_value.reshape(-1, HEAD_SIZE),
        stretch_key_value.reshape(-1, HEAD_SIZE),
        cycle,
    )
    pool, q_stretch, ask = lax.optimization_barrier((pool_key_value, q_stretch, ask))
    ask = lax.all_to_all(ask, CTX, split_axis=0, concat_axis=0, tiled=True)
    table = block_table.reshape(cycle, rows_dev * nblk)
    place = jnp.sum(jnp.where(table // pool_dev == me, table % pool_dev, 0), axis=1)

    kv_core, kv_y = swap(kv, "core"), swap(kv, "y")
    right = [q_stretch, turn(q_stretch, 1), turn(q_stretch, 2)]
    left = [q_stretch, turn(q_stretch, -1), turn(q_stretch, -2)]
    blocks = fetch(pool.reshape(pool_dev, 2 * block_size, HEAD_SIZE))
    look_out = look(place, ask, blocks)
    right[1], right[2], left[1], left[2], look_out = lax.optimization_barrier(
        (right[1], right[2], left[1], left[2], look_out)
    )
    answer = lax.all_to_all(look_out, CTX, split_axis=0, concat_axis=0, tiled=True)
    right += [None, turn(right[2], 2)]
    left.append(turn(left[1], -2))
    kv_yc = swap(after(kv_y, look_out), "core")
    sets = [kv, kv_core, kv_y, kv_yc]

    shifts = jnp.arange(Z_CHIPS, dtype=jnp.int32)
    corners = jnp.arange(2 * CORES, dtype=jnp.int32)
    corners = me ^ (corners // CORES * CORES * Z_CHIPS + corners % CORES)
    askers = me + ((z - shifts + Z_CHIPS) % Z_CHIPS - z) * CORES
    deltas = (askers[:, None] - corners[None, :]) * stretch

    keys, values = stack(sets)
    own = attend(0, deltas, q_stretch, keys, values)
    own, answer = lax.optimization_barrier((own, answer))
    attn = gather_answers(row_of, answer, q_rows, dec_new.reshape(rows_dev, 4, HEAD_SIZE))
    attn_core = swap(attn, "core")
    sets, _ = lax.optimization_barrier((sets, attn))
    keys, values = stack(sets)
    pair = jnp.concatenate([attn, after(attn_core, keys)], axis=0)
    pair_y = swap(pair, "y")

    def go(shift, previous, part=None, rider=None, carry=True):
        queries = right[shift] if shift >= 0 else left[-shift]
        return attend(shift % Z_CHIPS, after(deltas, *previous), queries, keys, values, part, rider, carry)

    attn = jnp.concatenate([pair, pair_y], axis=0)
    out = go(4, [attn], None, attn)
    from_right = [turn(out, -1)]
    right[3] = turn(after(right[1], out), 2)
    out = go(-3, [out], None, attn)
    from_left = [turn(out, 1)]
    out = go(3, [out], from_right[-1])
    from_right.append(turn(out, -1))
    out = go(-2, [out], from_left[-1])
    from_left.append(turn(out, 1))
    out = go(2, [out], from_right[-1])
    from_right.append(turn(out, -1))
    out = go(-1, [out], from_left[-1])
    from_left.append(turn(out, 1))
    rest = from_right[2][stretch + 16 :]
    farthest = turn(rest, -1)
    out = go(1, [out, rest], from_right[2], None, False)
    last = turn(out, -1)

    relative = jnp.where(shifts > Z_CHIPS // 2, Z_CHIPS // 2 - shifts, shifts)
    there = ((z + relative + Z_CHIPS) % Z_CHIPS - z) * CORES
    holders = ((there[:, None] + corners[None, :]) * (2 * rows_dev)).reshape(-1)
    partial_out = project(holders, after(attn, out), w_out, [*from_right, farthest, *from_left])
    shares = lax.axis_size(("grp", "tp"))
    pieces = lax.all_to_all(
        partial_out.reshape(shares, -1, partial_out.shape[1]), ("grp", "tp"), split_axis=0, concat_axis=0, tiled=True
    )
    pre_out = merge([own, last, from_left[2]], stretch)
    dec_out = jnp.sum(pieces.astype(F32), axis=0).astype(BF16)
    return (pre_out, dec_out.reshape(-1, 2, dec_out.shape[1]))


def solution(mesh):
    shape = mesh.devices.shape
    fine = jax.sharding.Mesh(mesh.devices.reshape(-1, Z_CHIPS, CORES, *shape[1:]), (*CTX, *mesh.axis_names[1:]))
    placed = (
        P(CTX, ("grp", "tp")),
        P(CTX, None, ("grp", "tp")),
        P(CTX, None, ("grp", "tp")),
        P(CTX, None, ("grp", "tp")),
        P(CTX, None, None, ("grp", "tp")),
        P(CTX, None, None, ("grp", "tp")),
        P(),
        P(CTX),
        P(("grp", "tp"), CTX),
    )
    return jax.shard_map(
        shards,
        mesh=fine,
        in_specs=placed,
        out_specs=(P(CTX, ("grp", "tp")), P(("grp", "tp"), None, CTX)),
        check_vma=False,
    )
```

```python
import functools
import math

import jax
import jax.numpy as jnp
from jax import lax
from jax.experimental import pallas as pl
from jax.experimental.pallas import tpu as pltpu
from jax.sharding import PartitionSpec as P

HEAD_SIZE = 128
CORES = 2
Z_CHIPS = 8
CONTEXT_DEV = 1280
BLOCK = 128
CTX = ("y", "z", "core")
SCALE = math.log2(math.e) / math.sqrt(HEAD_SIZE)
LOWEST = -1e30
F32 = jnp.float32
BF16 = jnp.bfloat16
VMEM = pl.BlockSpec(memory_space=pltpu.VMEM)
SMEM = pl.BlockSpec(memory_space=pltpu.SMEM)
HBM = pl.BlockSpec(memory_space=pltpu.HBM)


def params(mib):
    return pltpu.CompilerParams(vmem_limit_bytes=mib * 1024 * 1024)


def in_hbm(x):
    return pltpu.with_memory_space_constraint(x, pltpu.HBM)


def in_vmem(x):
    return pltpu.with_memory_space_constraint(x, pltpu.VMEM)


def dot_nt(a, b):
    return lax.dot_general(a, b, (((1,), (1,)), ((), ())), preferred_element_type=F32)


def dot_nn(a, b):
    return lax.dot_general(a, b, (((1,), (0,)), ((), ())), preferred_element_type=F32)


def prepare_body(
    me_ref,
    table_hbm,
    length_hbm,
    q_hbm,
    context_hbm,
    stretch_hbm,
    ask_ref,
    row_ref,
    rows_ref,
    kv_ref,
    list_ref,
    table_ref,
    length_ref,
    q_ref,
    context_ref,
    stretch_ref,
    sem,
):
    pieces = 5
    total = context_ref.shape[0]
    step = total // pieces
    copies = [
        pltpu.make_async_copy(q_hbm, q_ref, sem.at[0]),
        pltpu.make_async_copy(table_hbm, table_ref, sem.at[1]),
        pltpu.make_async_copy(length_hbm, length_ref, sem.at[2]),
    ]
    for n in range(pieces):
        rows = pl.ds(n * step, step)
        copies.append(pltpu.make_async_copy(context_hbm.at[rows], context_ref.at[rows], sem.at[3 + n]))
    copies.append(pltpu.make_async_copy(stretch_hbm, stretch_ref, sem.at[3 + pieces]))
    for copy in copies:
        copy.start()

    rows_dev = length_ref.shape[0]
    nblk = table_ref.shape[0]
    lists = rows_ref.shape[1]
    heads = lists // 2
    pool_dev = ask_ref.shape[0]
    copies[0].wait()
    for r in range(rows_dev):
        q = q_ref[r].astype(F32)
        for t in range(2):
            for h in range(heads):
                at = t * heads + h
                list_ref[r, at : at + 1, :] = q[t : t + 1, h * HEAD_SIZE : (h + 1) * HEAD_SIZE]
    copies[1].wait()
    copies[2].wait()
    for r in range(rows_dev):
        listed = list_ref[r]
        rows_ref[r] = listed.astype(BF16)
        asked = jnp.concatenate([listed[:heads], listed[heads:]], axis=1).astype(BF16)
        for n in range(nblk):
            holder = table_ref[n, me_ref[0] * rows_dev + r] // pool_dev
            left = jnp.clip(length_ref[r] - n * BLOCK, 0, BLOCK).astype(F32)
            ask_ref[holder, :, : 2 * HEAD_SIZE] = asked
            ask_ref[holder, :, 2 * HEAD_SIZE :] = jnp.full((heads, HEAD_SIZE), left, F32).astype(BF16)
            row_ref[holder] = r

    def split(rows, at):
        count = rows.shape[0]
        half = count // 2
        i = lax.broadcasted_iota(jnp.int32, (count, count), 0)
        j = lax.broadcasted_iota(jnp.int32, (count, count), 1)
        source = jnp.where(i < half, 2 * i, 2 * (i - half) + 1)
        pick = jnp.where(j == source, 1.0, 0.0).astype(BF16)
        parted = dot_nn(pick, rows).astype(BF16)
        kv_ref[0, at : at + half, :] = parted[:half]
        kv_ref[1, at : at + half, :] = parted[half:]

    for copy in copies[3:]:
        copy.wait()
    for start in range(0, total, 256):
        split(context_ref[start : start + 256, :], start // 2)
    split(stretch_ref[...], total // 2)


def prepare(me, table, length, q, context, stretch, holders):
    rows_dev = length.shape[0]
    lists = 2 * q.shape[2] // HEAD_SIZE
    rows = (context.shape[0] + stretch.shape[0]) // 2
    return pl.pallas_call(
        prepare_body,
        out_shape=[
            jax.ShapeDtypeStruct((holders, lists // 2, 3 * HEAD_SIZE), BF16),
            jax.ShapeDtypeStruct((holders,), jnp.int32),
            jax.ShapeDtypeStruct((rows_dev, lists, HEAD_SIZE), BF16),
            jax.ShapeDtypeStruct((2, rows, HEAD_SIZE), BF16),
        ],
        in_specs=[SMEM] + [HBM] * 5,
        out_specs=[VMEM, SMEM, VMEM, VMEM],
        scratch_shapes=[
            pltpu.VMEM((rows_dev, lists, HEAD_SIZE), F32),
            pltpu.SMEM(table.shape, jnp.int32),
            pltpu.SMEM(length.shape, jnp.int32),
            pltpu.VMEM(q.shape, BF16),
            pltpu.VMEM(context.shape, BF16),
            pltpu.VMEM(stretch.shape, BF16),
            pltpu.SemaphoreType.DMA((9,)),
        ],
        compiler_params=params(16),
        name="prepare",
    )(me, *(in_hbm(x) for x in (table, length, q, context, stretch)))


def stack_body(*refs):
    kv_refs, k_ref, v_ref = refs[:-2], refs[-2], refs[-1]
    sets = len(kv_refs)
    stretch = v_ref.shape[0] // sets - CONTEXT_DEV
    one = jnp.where(diagonal(), 1.0, 0.0).astype(BF16)
    v_ref[:, HEAD_SIZE:] = jnp.ones((v_ref.shape[0], HEAD_SIZE), BF16)
    for n, ref in enumerate(kv_refs):
        first, last = n * CONTEXT_DEV, sets * CONTEXT_DEV + n * stretch
        for at in range(0, CONTEXT_DEV, 256):
            k_ref[:, first + at : first + at + 256] = dot_nt(one, ref[0, at : at + 256, :]).astype(BF16)
        v_ref[first : first + CONTEXT_DEV, :HEAD_SIZE] = ref[1, :CONTEXT_DEV, :]
        v_ref[last : last + stretch, :HEAD_SIZE] = ref[1, CONTEXT_DEV:, :]
    k = jnp.concatenate([ref[0, CONTEXT_DEV:, :] for ref in kv_refs], axis=0)
    k_ref[:, sets * CONTEXT_DEV :] = dot_nt(one, k).astype(BF16)


def stack(sets):
    keys = len(sets) * sets[0].shape[1]
    return pl.pallas_call(
        stack_body,
        out_shape=[
            jax.ShapeDtypeStruct((HEAD_SIZE, keys), BF16),
            jax.ShapeDtypeStruct((keys, 2 * HEAD_SIZE), BF16),
        ],
        in_specs=[VMEM] * len(sets),
        out_specs=[VMEM, VMEM],
        compiler_params=params(16),
        name="stack",
    )(*sets)


def diagonal():
    i = lax.broadcasted_iota(jnp.int32, (HEAD_SIZE, HEAD_SIZE), 0)
    j = lax.broadcasted_iota(jnp.int32, (HEAD_SIZE, HEAD_SIZE), 1)
    return i == j


def read_part(ref, stretch, first, heads):
    columns = range(first * HEAD_SIZE, (first + heads) * HEAD_SIZE, HEAD_SIZE)
    outputs = jnp.concatenate([ref[:stretch, c : c + HEAD_SIZE] for c in columns], axis=0)
    stat = ref[stretch : stretch + 16, first * stretch : (first + heads) * stretch].astype(F32)
    level = stat[0:1] + stat[1:2] + stat[2:3]
    columns = []
    for g in range(0, heads * stretch, HEAD_SIZE):
        column = jnp.sum(jnp.where(diagonal(), level[:, g : g + HEAD_SIZE], 0.0), axis=1, keepdims=True)
        columns.append(jnp.broadcast_to(column, (HEAD_SIZE, HEAD_SIZE)))
    return outputs.astype(F32), jnp.concatenate(columns, axis=0)


def join(outputs, levels):
    top = functools.reduce(jnp.maximum, levels)
    weights = [jnp.exp2(level - top) for level in levels]
    total = functools.reduce(jnp.add, weights)
    mixed = functools.reduce(jnp.add, [weight * output for weight, output in zip(weights, outputs)])
    return mixed / total, top + jnp.log2(total)


def write_outputs(ref, outputs, stretch, first):
    outputs = outputs.astype(BF16)
    for h in range(outputs.shape[0] // stretch):
        ref[:stretch, (first + h) * HEAD_SIZE : (first + h + 1) * HEAD_SIZE] = outputs[h * stretch : (h + 1) * stretch]


def write_level(ref, level, stretch, first):
    rows = level.shape[0]
    lines = []
    for g in range(0, rows, HEAD_SIZE):
        lines.append(jnp.sum(jnp.where(diagonal(), level[g : g + HEAD_SIZE], 0.0), axis=0, keepdims=True))
    level = jnp.concatenate(lines, axis=1)
    high = level.astype(BF16).astype(F32)
    rest = level - high
    middle = rest.astype(BF16).astype(F32)
    row = lax.broadcasted_iota(jnp.int32, (16, rows), 0)
    stat = jnp.where(row == 0, high, jnp.where(row == 1, middle, jnp.where(row == 2, rest - middle, 0.0)))
    ref[stretch : stretch + 16, first * stretch : first * stretch + rows] = stat.astype(BF16)


def attend_body(which, arrived, riders, delta_ref, k_ref, v_ref, q_ref, *refs):
    refs = list(refs)
    part_ref = refs.pop(0) if arrived else None
    rider_ref = refs.pop(0) if riders == "own" else part_ref
    out_ref, p_ref, total_ref, top_ref = refs
    stretch, width = q_ref.shape
    sets = delta_ref.shape[1]
    keys = v_ref.shape[0]
    halves, rows = p_ref.shape[:2]
    heads = rows // stretch
    chunk = 256

    if riders is not None:
        start = 0 if riders == "own" else stretch + 16
        out_ref[stretch + 16 :, :] = rider_ref[start:, :]
    out_ref[stretch : stretch + 16, halves * rows :] = jnp.zeros((16, width - halves * rows), BF16)

    def queries(n):
        columns = range(n * heads * HEAD_SIZE, (n + 1) * heads * HEAD_SIZE, HEAD_SIZE)
        return jnp.concatenate([q_ref[:, c : c + HEAD_SIZE] for c in columns], axis=0)

    def score(q, k, masked):
        s = dot_nn(q, k)
        if masked:
            row = lax.rem(lax.broadcasted_iota(jnp.int32, s.shape, 0), stretch)
            col = lax.broadcasted_iota(jnp.int32, s.shape, 1)
            bound = delta_ref[which, sets - 1] + (sets - 1) * stretch - col
            for m in reversed(range(sets - 1)):
                bound = jnp.where(col < (m + 1) * stretch, delta_ref[which, m] + m * stretch - col, bound)
            s = jnp.where(row + bound >= 0, s, LOWEST)
        return s

    def highest(s):
        parts = [s[:, c : c + HEAD_SIZE] for c in range(0, s.shape[1], HEAD_SIZE)]
        return functools.reduce(jnp.maximum, parts)

    def spread(top):
        return jnp.broadcast_to(jnp.max(top, axis=1, keepdims=True), (rows, HEAD_SIZE)) * SCALE

    def weigh(s, top):
        parts = [s[:, c : c + HEAD_SIZE] for c in range(0, s.shape[1], HEAD_SIZE)]
        return jnp.concatenate([jnp.exp2(part * SCALE - top) for part in parts], axis=1).astype(BF16)

    def finish(n, total, top):
        weight = total[:, HEAD_SIZE:]
        output, level = total[:, :HEAD_SIZE] / weight, top + jnp.log2(weight)
        if arrived:
            other, other_level = read_part(part_ref, stretch, n * heads, heads)
            output, level = join([output, other], [level, other_level])
        write_outputs(out_ref, output, stretch, n * heads)
        write_level(out_ref, level, stretch, n * heads)

    steps = keys // chunk
    ends = [steps * chunk * n // 21 for n in (5, 10, 15, 18, 20, 21)]
    tops = [spread(highest(score(queries(n), k_ref[:, :chunk], False))) for n in range(halves)]
    sums = []
    for n in range(halves):
        q = queries(n)
        total = None
        begun = 0
        for at in range(0, keys, chunk):
            masked = at >= sets * CONTEXT_DEV
            p_ref[n, :, at : at + chunk] = weigh(score(q, k_ref[:, at : at + chunk], masked), tops[n])
            done = at + chunk
            if done in ends:
                part = dot_nn(p_ref[n, :, begun:done], v_ref[begun:done, :])
                total = part if total is None else total + part
                begun = done
        sums.append(total[:, HEAD_SIZE:])
        finish(n, total, tops[n])

    @pl.when(jnp.logical_not(jnp.max(functools.reduce(jnp.maximum, sums)) < 1e37))
    def again():
        for n in range(halves):
            q = queries(n)
            last = score(q, k_ref[:, keys - chunk :], True)

            def climb(m, top):
                k = k_ref[:, pl.ds(pl.multiple_of(m * chunk, chunk), chunk)]
                return jnp.maximum(top, highest(score(q, k, False)))

            top_ref[...] = spread(lax.fori_loop(0, steps - 1, climb, highest(last)))
            total_ref[...] = dot_nn(weigh(last, top_ref[...]), v_ref[keys - chunk :, :])

            def add(m, carry):
                at = pl.ds(pl.multiple_of(m * chunk, chunk), chunk)
                total_ref[...] += dot_nn(weigh(score(q, k_ref[:, at], False), top_ref[...]), v_ref[at, :])
                return carry

            lax.fori_loop(0, steps - 1, add, 0)
            finish(n, total_ref[...], top_ref[...])


def attend(which, deltas, queries, keys, values, part=None, rider=None, carry=True):
    stretch, width = queries.shape
    rows = width // HEAD_SIZE * stretch // 2
    count = values.shape[0]
    operands = [deltas, keys, values, queries]
    out_rows = stretch + 16
    riders = None
    if part is not None:
        operands.append(part)
        if carry:
            riders = "arrived"
            out_rows = part.shape[0]
    if rider is not None:
        riders = "own"
        operands.append(rider)
        out_rows += rider.shape[0]
    return pl.pallas_call(
        functools.partial(attend_body, which, part is not None, riders),
        out_shape=jax.ShapeDtypeStruct((out_rows, width), BF16),
        in_specs=[SMEM] + [VMEM] * (len(operands) - 1),
        out_specs=VMEM,
        scratch_shapes=[
            pltpu.VMEM((2, rows, count), BF16),
            pltpu.VMEM((rows, 2 * HEAD_SIZE), F32),
            pltpu.VMEM((rows, HEAD_SIZE), F32),
        ],
        compiler_params=params(24),
        cost_estimate=pl.CostEstimate(
            flops=16 * rows * count * HEAD_SIZE,
            bytes_accessed=4 * count * HEAD_SIZE,
            transcendentals=2 * rows * count,
        ),
        name="attend",
    )(*operands)


def merge_body(*refs):
    part_refs, out_ref = refs[:-1], refs[-1]
    stretch = out_ref.shape[0]
    read = [read_part(ref, stretch, 0, out_ref.shape[1] // HEAD_SIZE) for ref in part_refs]
    output, _ = join([x for x, _ in read], [x for _, x in read])
    write_outputs(out_ref, output, stretch, 0)


def merge(parts, stretch):
    return pl.pallas_call(
        merge_body,
        out_shape=jax.ShapeDtypeStruct((stretch, parts[0].shape[1]), BF16),
        in_specs=[VMEM] * len(parts),
        out_specs=VMEM,
        compiler_params=params(16),
        name="merge",
    )(*parts)


def fetch_body(pool_hbm, pool_ref, sem):
    copies = []
    step = pool_ref.shape[0] // sem.shape[0]
    for n in range(sem.shape[0]):
        blocks = pl.ds(n * step, step)
        copies.append(pltpu.make_async_copy(pool_hbm.at[blocks], pool_ref.at[blocks], sem.at[n]))
        copies[n].start()
    for copy in copies:
        copy.wait()


def fetch(pool):
    return pl.pallas_call(
        fetch_body,
        out_shape=pltpu.VMEM(pool.shape, BF16),
        in_specs=[HBM],
        out_specs=VMEM,
        scratch_shapes=[pltpu.SemaphoreType.DMA((4,))],
        compiler_params=params(16),
        name="fetch_blocks",
    )(in_hbm(pool))


def look_body(place_ref, ask_ref, pool_ref, out_ref, s_ref, p_ref, scale_ref):
    owners, heads = ask_ref.shape[:2]
    lists = 2 * heads
    span = pool_ref.shape[1]
    for d in range(owners):
        q = ask_ref[d, :, : 2 * HEAD_SIZE].astype(F32)
        q = jnp.concatenate([q[:, :HEAD_SIZE], q[:, HEAD_SIZE:]], axis=0).astype(BF16)
        s_ref[d * lists : (d + 1) * lists, :] = dot_nt(q, pool_ref[place_ref[d]])
    col = lax.broadcasted_iota(jnp.int32, (lists, span), 1)
    lane = lax.broadcasted_iota(jnp.int32, (heads, HEAD_SIZE), 1)
    even = (col & 1) == 0
    for d in range(owners):
        limit = ask_ref[d, :, 2 * HEAD_SIZE :].astype(F32) * 2.0
        limit = jnp.concatenate([limit] * 2, axis=0)
        limit = jnp.concatenate([limit] * (span // HEAD_SIZE), axis=1)
        allowed = even & (col.astype(F32) < limit)
        s = jnp.where(allowed, s_ref[d * lists : (d + 1) * lists, :], LOWEST)
        top = jnp.max(s, axis=1, keepdims=True)
        p = jnp.where(allowed, jnp.exp2((s - top) * SCALE), 0.0)
        total = jnp.sum(p, axis=1, keepdims=True)
        p_ref[d * lists : (d + 1) * lists, :] = pltpu.roll(p, 1, 1).astype(BF16)
        seen = total > 0.0
        level = jnp.where(seen, top * SCALE + jnp.log2(jnp.where(seen, total, 1.0)), LOWEST)
        level = jnp.broadcast_to(level, (lists, HEAD_SIZE))
        high = level.astype(BF16).astype(F32)
        rest = level - high
        middle = rest.astype(BF16).astype(F32)
        stat = jnp.zeros((heads, HEAD_SIZE), F32)
        for t in range(2):
            for n, piece in enumerate((high, middle, rest - middle)):
                stat = jnp.where(lane == 3 * t + n, piece[t * heads : (t + 1) * heads], stat)
        out_ref[d, :, 2 * HEAD_SIZE :] = stat.astype(BF16)
        scale_ref[d * lists : (d + 1) * lists, :] = jnp.broadcast_to(
            jnp.where(seen, 1.0 / jnp.where(seen, total, 1.0), 0.0), (lists, HEAD_SIZE)
        )
    for d in range(owners):
        o = dot_nn(p_ref[d * lists : (d + 1) * lists, :], pool_ref[place_ref[d]])
        o = o * scale_ref[d * lists : (d + 1) * lists, :]
        out_ref[d, :, : 2 * HEAD_SIZE] = jnp.concatenate([o[:heads], o[heads:]], axis=1).astype(BF16)


def look(place, ask, pool):
    owners, heads, width = ask.shape
    span = pool.shape[1]
    rows = 2 * owners * heads
    return pl.pallas_call(
        look_body,
        out_shape=jax.ShapeDtypeStruct(ask.shape, BF16),
        in_specs=[SMEM, VMEM, VMEM],
        out_specs=VMEM,
        scratch_shapes=[
            pltpu.VMEM((rows, span), F32),
            pltpu.VMEM((rows, span), BF16),
            pltpu.VMEM((rows, HEAD_SIZE), F32),
        ],
        compiler_params=params(24),
        cost_estimate=pl.CostEstimate(
            flops=4 * rows * span * HEAD_SIZE, bytes_accessed=2 * owners * span * HEAD_SIZE, transcendentals=0
        ),
        name="look_in_blocks",
    )(place, ask, pool)


def gather_body(row_ref, answer_ref, q_ref, new_ref, out_ref, level_ref, top_ref, sum_ref, acc_ref, flat_ref):
    holders = answer_ref.shape[0]
    rows, lists = q_ref.shape[0], q_ref.shape[1]
    heads = lists // 2
    lane = lax.broadcasted_iota(jnp.int32, (lists, HEAD_SIZE), 1)
    later = lax.broadcasted_iota(jnp.int32, (lists, HEAD_SIZE), 0) >= heads
    own = []
    for r in range(rows):
        q = q_ref[r].astype(F32)
        new = new_ref[r].astype(F32)
        scores = []
        for t in range(2):
            s = jnp.sum(q * new[2 * t : 2 * t + 1, :], axis=1, keepdims=True) * SCALE
            scores.append(jnp.broadcast_to(s, (lists, HEAD_SIZE)))
        scores[1] = jnp.where(later, scores[1], LOWEST)
        top_ref[r] = jnp.maximum(scores[0], scores[1])
        own.append((scores, new))
    for d in range(holders):
        stat = answer_ref[d, :, 2 * HEAD_SIZE :].astype(F32)
        stat = jnp.concatenate([stat, stat], axis=0)
        level = jnp.sum(jnp.where((lane < 6) & ((lane >= 3) == later), stat, 0.0), axis=1, keepdims=True)
        level_ref[d] = jnp.broadcast_to(level, (lists, HEAD_SIZE))
    for d in range(holders):
        r = row_ref[d]
        top_ref[r] = jnp.maximum(top_ref[r], level_ref[d])
    for r in range(rows):
        scores, new = own[r]
        first = jnp.exp2(scores[0] - top_ref[r])
        second = jnp.exp2(scores[1] - top_ref[r])
        sum_ref[r] = first + second
        acc_ref[r] = first * new[1:2, :] + second * new[3:4, :]
    for d in range(holders):
        r = row_ref[d]
        weight = jnp.exp2(level_ref[d] - top_ref[r])
        sum_ref[r] = sum_ref[r] + weight
        o = answer_ref[d, :, : 2 * HEAD_SIZE].astype(F32)
        o = jnp.concatenate([o[:, :HEAD_SIZE], o[:, HEAD_SIZE:]], axis=0)
        acc_ref[r] = acc_ref[r] + weight * o
    for r in range(rows):
        o = acc_ref[r] / sum_ref[r]
        for t in range(2):
            for h in range(heads):
                flat_ref[2 * r + t : 2 * r + t + 1, h * HEAD_SIZE : (h + 1) * HEAD_SIZE] = o[
                    t * heads + h : t * heads + h + 1, :
                ]
    out_ref[...] = flat_ref[...].astype(BF16)


def gather_answers(row_of, answer, q, new):
    rows, lists, width = q.shape
    holders = answer.shape[0]
    heads = lists // 2
    state = pltpu.VMEM((rows, lists, width), F32)
    return pl.pallas_call(
        gather_body,
        out_shape=jax.ShapeDtypeStruct((2 * rows, heads * width), BF16),
        in_specs=[SMEM, VMEM, VMEM, VMEM],
        out_specs=VMEM,
        scratch_shapes=[
            pltpu.VMEM((holders, lists, width), F32),
            state,
            state,
            state,
            pltpu.VMEM((2 * rows, heads * width), F32),
        ],
        compiler_params=params(16),
        name="gather_answers",
    )(row_of, answer, q, new)


def project_body(place_ref, own_ref, w_ref, *refs):
    ref_list, out_ref, total_ref, rows_ref = refs[:-3], refs[-3], refs[-2], refs[-1]
    rows = own_ref.shape[0]
    rows_ref[:rows, :] = own_ref[...]
    for n, ref in enumerate(ref_list):
        rows_ref[(n + 1) * rows : (n + 2) * rows, :] = ref[ref.shape[0] - rows :, :]
    total = dot_nn(rows_ref[...], w_ref[...])
    for n in range(rows_ref.shape[0] // 8):
        at = pl.multiple_of(place_ref[n], 8)
        total_ref[pl.ds(at, 8), :] = total[8 * n : 8 * n + 8]
    out_ref[...] = total_ref[...].astype(BF16)


def project(place, own, w, parts):
    rows = own.shape[0] * (len(parts) + 1)
    return pl.pallas_call(
        project_body,
        out_shape=jax.ShapeDtypeStruct((rows, w.shape[1]), BF16),
        in_specs=[SMEM] + [VMEM] * (len(parts) + 2),
        out_specs=VMEM,
        scratch_shapes=[pltpu.VMEM((rows, w.shape[1]), F32), pltpu.VMEM((rows, own.shape[1]), BF16)],
        compiler_params=params(16),
        name="project",
    )(place, own, w, *parts)


def shards(
    q_stretch,
    stretch_key_value,
    context_key_value,
    dec_q,
    dec_new,
    pool_key_value,
    block_table,
    cache_len,
    w_out,
):
    me = lax.axis_index(CTX)
    z = lax.axis_index("z")
    cycle = lax.axis_size(CTX)
    stretch = q_stretch.shape[0]
    rows_dev, nblk = dec_q.shape[0], block_table.shape[1]
    pool_dev, block_size = pool_key_value.shape[:2]

    def after(x, *others):
        return lax.optimization_barrier((x, *others))[0]

    def swap(x, name):
        return lax.ppermute(x, name, [(0, 1), (1, 0)])

    def turn(x, step):
        return lax.ppermute(x, "z", [(n, (n + step) % Z_CHIPS) for n in range(Z_CHIPS)])

    ask, row_of, q_rows, kv = prepare(
        me.reshape(1).astype(jnp.int32),
        block_table.T,
        cache_len,
        dec_q,
        context_key_value.reshape(-1, HEAD_SIZE),
        stretch_key_value.reshape(-1, HEAD_SIZE),
        cycle,
    )
    pool, q_stretch, ask = lax.optimization_barrier((pool_key_value, q_stretch, ask))
    ask = lax.all_to_all(ask, CTX, split_axis=0, concat_axis=0, tiled=True)
    table = block_table.reshape(cycle, rows_dev * nblk)
    place = jnp.sum(jnp.where(table // pool_dev == me, table % pool_dev, 0), axis=1)

    kv_core, kv_y = swap(kv, "core"), swap(kv, "y")
    right = [q_stretch, turn(q_stretch, 1), turn(q_stretch, 2)]
    left = [q_stretch, turn(q_stretch, -1), turn(q_stretch, -2)]
    blocks = fetch(pool.reshape(pool_dev, 2 * block_size, HEAD_SIZE))
    look_out = look(place, ask, blocks)
    right[1], right[2], left[1], left[2], look_out = lax.optimization_barrier(
        (right[1], right[2], left[1], left[2], look_out)
    )
    answer = lax.all_to_all(look_out, CTX, split_axis=0, concat_axis=0, tiled=True)
    right += [turn(right[1], 2), turn(right[2], 2)]
    left.append(turn(left[1], -2))
    kv_yc = swap(after(kv_y, look_out), "core")
    sets = [kv, kv_core, kv_y, kv_yc]

    shifts = jnp.arange(Z_CHIPS, dtype=jnp.int32)
    corners = jnp.arange(2 * CORES, dtype=jnp.int32)
    corners = me ^ (corners // CORES * CORES * Z_CHIPS + corners % CORES)
    askers = me + ((z - shifts + Z_CHIPS) % Z_CHIPS - z) * CORES
    deltas = (askers[:, None] - corners[None, :]) * stretch

    keys, values = stack(sets)
    own = attend(0, deltas, q_stretch, keys, values)
    own, right[4], answer = lax.optimization_barrier((own, right[4], answer))
    attn = gather_answers(row_of, answer, q_rows, dec_new.reshape(rows_dev, 4, HEAD_SIZE))
    attn_core = swap(attn, "core")
    sets, _ = lax.optimization_barrier((sets, attn))
    keys, values = stack(sets)
    pair = jnp.concatenate([attn, after(attn_core, keys)], axis=0)
    pair_y = swap(pair, "y")

    def go(shift, previous, part=None, rider=None, carry=True):
        queries = right[shift] if shift >= 0 else left[-shift]
        return attend(shift % Z_CHIPS, after(deltas, *previous), queries, keys, values, part, rider, carry)

    attn = jnp.concatenate([pair, pair_y], axis=0)
    out = go(4, [attn], None, attn)
    from_right = [turn(out, -1)]
    out = go(-3, [out], None, attn)
    from_left = [turn(out, 1)]
    out = go(3, [out], from_right[-1])
    from_right.append(turn(out, -1))
    out = go(-2, [out], from_left[-1])
    from_left.append(turn(out, 1))
    out = go(2, [out], from_right[-1])
    from_right.append(turn(out, -1))
    out = go(-1, [out], from_left[-1])
    from_left.append(turn(out, 1))
    rest = from_right[2][stretch + 16 :]
    farthest = turn(rest, -1)
    out = go(1, [out, rest], from_right[2], None, False)
    last = turn(out, -1)

    relative = jnp.where(shifts > Z_CHIPS // 2, Z_CHIPS // 2 - shifts, shifts)
    there = ((z + relative + Z_CHIPS) % Z_CHIPS - z) * CORES
    holders = ((there[:, None] + corners[None, :]) * (2 * rows_dev)).reshape(-1)
    partial_out = project(holders, after(attn, out), w_out, [*from_right, farthest, *from_left])
    shares = lax.axis_size(("grp", "tp"))
    pieces = lax.all_to_all(
        partial_out.reshape(shares, -1, partial_out.shape[1]), ("grp", "tp"), split_axis=0, concat_axis=0, tiled=True
    )
    pre_out = merge([own, last, from_left[2]], stretch)
    dec_out = jnp.sum(pieces.astype(F32), axis=0).astype(BF16)
    return (pre_out, dec_out.reshape(-1, 2, dec_out.shape[1]))


def solution(mesh):
    shape = mesh.devices.shape
    fine = jax.sharding.Mesh(mesh.devices.reshape(-1, Z_CHIPS, CORES, *shape[1:]), (*CTX, *mesh.axis_names[1:]))
    placed = (
        P(CTX, ("grp", "tp")),
        P(CTX, None, ("grp", "tp")),
        P(CTX, None, ("grp", "tp")),
        P(CTX, None, ("grp", "tp")),
        P(CTX, None, None, ("grp", "tp")),
        P(CTX, None, None, ("grp", "tp")),
        P(),
        P(CTX),
        P(("grp", "tp"), CTX),
    )
    return jax.shard_map(
        shards,
        mesh=fine,
        in_specs=placed,
        out_specs=(P(CTX, ("grp", "tp")), P(("grp", "tp"), None, CTX)),
        check_vma=False,
    )
```
